256 devices in a mesh: keys: 64 (over y, z, core), seq: 4 (over x).
Axes of the slice: x: 4, y: 4, z: 8, core: 2. Of those that a mesh axis runs over, the one named last changes fastest.
Arguments:
- span_queries: bfloat16 [1536, 768], P(('keys', 'seq')), may hold values from -6 to 6
- key_slab: bfloat16 [4096, 768], P('keys'), may hold values from -0.21875 to 0.21875
- neighbour_store: bfloat16 [4096, 64, 896], P('keys'), may hold values from -6 to 6
- neighbour_ids: int32 [1536, 2], P(('keys', 'seq')), may hold values from 0 to 4094, as said below
- attn_queries: bfloat16 [98304, 2048], P(('keys', 'seq')), may hold values from -200 to 200
- kv_weight: bfloat16 [2, 2048, 896], P(None, 'keys'), may hold values from -0.1875 to 0.1875
Outputs:
- best_scores: float32 [1536, 2], P(('keys', 'seq'))
- attended: bfloat16 [98304, 2048], P(('keys', 'seq'))
The draws below stay inside these ranges and needn't reach their ends.
Inputs may be any that keep to these rules, and one draw needn't show every extreme that they name: `neighbour_ids`: each id c has c mod 64 at most 62, so c + 1 lies on the same shard c // 64. Among the 12 ids of one device's spans (aligned blocks of 6 rows), no shard holds more than 1, and some shard holds exactly 1.
All inputs are finite; a program needn't handle non-finite values.
Results may differ from the reference program's by a relative error of at most 0.012.
The reference program's roundings to bfloat16 on the way count: a program that leaves them out, or rounds other values in their place, can miss the bound.
Values may be sent and summed in bfloat16 or wider, within the bound.
A program may use at most 128 MiB of HBM per device.

```python
import jax
import jax.numpy as jnp
from jax import lax

ENC_Q = 768
ENC = 896
HEADS = 16
HEAD_DIM = 128
SPAN = 64
CH_DEV = 6
BLK = 64
HQ = 2048
QCHUNKS = 1536
TOKENS = 98304
DB = 4096
N_KEYS = 64


def draw_neighbour_ids(key, part):
    per_shard = (2 * CH_DEV + N_KEYS - 1) // N_KEYS
    pick_count = 2 * CH_DEV
    group_count = QCHUNKS // CH_DEV
    candidate_count = N_KEYS * per_shard
    key_rank, key_noise, key_order, key_offset = jax.random.split(key, 4)
    popularity = jax.random.permutation(key_rank, jnp.arange(N_KEYS, dtype=jnp.int32))
    popular = popularity * popularity * 2 // N_KEYS
    candidate_shard = jnp.arange(candidate_count, dtype=jnp.int32) % N_KEYS
    noise_draw = jax.random.randint(key_noise, (group_count, candidate_count), 0, 256, dtype=jnp.int32)
    ranking = (noise_draw + popular[candidate_shard][None, :]) * candidate_count + jnp.arange(candidate_count, dtype=jnp.int32)[None, :]
    chosen = lax.top_k(ranking, pick_count)[1].astype(jnp.int32)
    shuffle_keys = jax.random.randint(key_order, (group_count, pick_count), 0, 1 << 16, dtype=jnp.int32) * pick_count + jnp.arange(pick_count, dtype=jnp.int32)[None, :]
    ordering = jnp.argsort(shuffle_keys, axis=1, stable=True)
    chosen = jnp.take_along_axis(chosen, ordering, axis=1)
    shards = chosen % N_KEYS
    offset = jax.random.randint(key_offset, (group_count, pick_count), 0, BLK - 1, dtype=jnp.int32)
    return (shards * BLK + offset).reshape(QCHUNKS, 2).astype(jnp.int32)


def draw_attn_queries(key, part):
    key_base = jax.random.fold_in(key, 0)
    values = jnp.clip(jax.random.normal(key_base, (TOKENS, HQ), jnp.float32), -6.0, 6.0)
    return values.astype(jnp.bfloat16)


def level_of(own_key, dims, cuts, least, high):
    loudness = 1.0
    for dim, shards_of in cuts:
        steps = jax.random.uniform(jax.random.fold_in(jax.random.fold_in(own_key, 6), dim), (shards_of,), jnp.float32, least / len(cuts), high / len(cuts))
        loudness = loudness * jnp.repeat(jnp.exp(steps), dims[dim] // shards_of).reshape((-1,) + (1,) * (len(dims) - 1 - dim))
    return loudness


def centred(own_key, shape, deviation, bound, cuts=(), held_as=jnp.bfloat16):
    entries = deviation * jax.random.normal(own_key, shape, jnp.float32)
    if cuts:
        entries = entries * level_of(own_key, shape, cuts, -0.22, 0.18)
    return jnp.clip(entries, -bound, bound).astype(held_as)


def setup_inputs(seed: int = 0) -> dict:
    arg_keys = jax.random.split(jax.random.key(seed), 7)
    span_queries = centred(arg_keys[0], (QCHUNKS, ENC_Q), 1.0, 6.0, ((0, 256),))
    key_slab = centred(arg_keys[1], (DB, ENC_Q), ENC_Q ** -0.5, 0.21875, ((0, 64),))
    neighbour_store = centred(arg_keys[2], (DB, SPAN, ENC), 1.0, 6.0, ((0, 64),))
    neighbour_ids = draw_neighbour_ids(jax.random.fold_in(arg_keys[6], 71), 0)
    attn_queries = draw_attn_queries(jax.random.fold_in(arg_keys[6], 71), 0)
    kv_weight = centred(arg_keys[5], (2, HQ, ENC), ENC ** -0.5, 0.1875, ((1, 64),))
    return dict(span_queries=span_queries, key_slab=key_slab, neighbour_store=neighbour_store, neighbour_ids=neighbour_ids, attn_queries=attn_queries, kv_weight=kv_weight)


def reference(span_queries, key_slab, neighbour_store, neighbour_ids, attn_queries, kv_weight):
    scores = jnp.dot(span_queries, key_slab.T, preferred_element_type=jnp.float32)
    best_scores = lax.top_k(scores, 2)[0]
    group_count = QCHUNKS // CH_DEV
    grouped_ids = neighbour_ids.reshape(group_count, CH_DEV, 2)
    grouped_queries = attn_queries.reshape(group_count, CH_DEV, SPAN, HEADS, HEAD_DIM)
    scale = HEAD_DIM ** -0.5

    def one_group(operands):
        group_ids, group_queries = operands
        first_span = neighbour_store[group_ids]
        next_span = neighbour_store[group_ids + 1]
        neighbours = jnp.stack([first_span, next_span], axis=2).reshape(CH_DEV * 4 * SPAN, ENC)
        key_rows = jnp.dot(neighbours, kv_weight[0].T, preferred_element_type=jnp.float32).astype(jnp.bfloat16)
        value_rows = jnp.dot(neighbours, kv_weight[1].T, preferred_element_type=jnp.float32).astype(jnp.bfloat16)
        key_rows = lax.optimization_barrier(key_rows)
        value_rows = lax.optimization_barrier(value_rows)
        key_rows = key_rows.astype(jnp.float32).reshape(CH_DEV, 4 * SPAN, HEADS, HEAD_DIM)
        value_rows = value_rows.astype(jnp.float32).reshape(CH_DEV, 4 * SPAN, HEADS, HEAD_DIM)
        logits = jnp.einsum("cqhd,ckhd->chqk", group_queries.astype(jnp.float32), key_rows) * scale
        largest = jnp.max(logits, axis=-1, keepdims=True)
        expo_terms = jnp.exp(logits - largest)
        weights = (expo_terms / jnp.sum(expo_terms, axis=-1, keepdims=True)).astype(jnp.bfloat16)
        weights = lax.optimization_barrier(weights).astype(jnp.float32)
        output = jnp.einsum("chqk,ckhd->cqhd", weights, value_rows)
        return output.astype(jnp.bfloat16)

    attended = lax.map(one_group, (grouped_ids, grouped_queries))
    return best_scores, attended.reshape(TOKENS, HQ)
```

```python
import functools

import jax
import jax.numpy as jnp
import numpy as np
from jax import lax
from jax.experimental import pallas as pl
from jax.experimental.pallas import tpu as pltpu
from jax.sharding import PartitionSpec as P

HEADS = 16
HEAD_DIM = 128
RING_Y, RING_Z, CORES = 4, 8, 2
Y_CAPS = (24, 17)
Z_CAPS = (12, 12, 11, 10)


def key_of(y, z, c):
    return (y * RING_Z + z) * CORES + c


def place():
    k = lax.axis_index("keys")
    return k // (RING_Z * CORES), (k // CORES) % RING_Z, k % CORES


def shifted(dy, dz, dc):
    pairs = []
    for y in range(RING_Y):
        for z in range(RING_Z):
            for c in range(CORES):
                to = key_of((y + dy) % RING_Y, (z + dz) % RING_Z, (c + dc) % CORES)
                pairs.append((key_of(y, z, c), to))
    return pairs


def greet(peers):
    barrier = pltpu.get_barrier_semaphore()
    for peer in peers:
        pl.semaphore_signal(
            barrier, inc=1, device_id={"keys": peer}, device_id_type=pl.DeviceIdType.MESH
        )
    pl.semaphore_wait(barrier, len(peers))


def peer_groups():
    y, z, c = place()
    core = [key_of(y, z, 1 - c)]
    depth = [key_of(y, (z + d) % RING_Z, c) for d in range(1, RING_Z)]
    row = [key_of((y + d) % RING_Y, z, c) for d in range(1, RING_Y)]
    return core, depth, row


def send(src, dst, send_sem, recv_sem, peer):
    copy = pltpu.make_async_remote_copy(
        src_ref=src,
        dst_ref=dst,
        send_sem=send_sem,
        recv_sem=recv_sem,
        device_id={"keys": peer},
        device_id_type=pl.DeviceIdType.MESH,
    )
    copy.start()
    return copy


def gather_ids_kernel(ids_ref, out_ref, held, send_sem, recv_sem):
    y, z, c = place()
    core, depth, row = peer_groups()
    greet(core + depth + row)
    held[y, z, c] = ids_ref[...]
    copies = [send(held.at[y, z, c], held.at[y, z, c], send_sem.at[0], recv_sem.at[0], core[0])]
    for copy in copies:
        copy.wait()
    copies = []
    for i, peer in enumerate(depth):
        copies.append(
            send(held.at[y, z], held.at[y, z], send_sem.at[1 + i], recv_sem.at[1 + i], peer)
        )
    for copy in copies:
        copy.wait()
    copies = []
    for i, peer in enumerate(row):
        copies.append(send(held.at[y], held.at[y], send_sem.at[8 + i], recv_sem.at[8 + i], peer))
    for copy in copies:
        copy.wait()
    out_ref[...] = held[...]


def gather_ids(ids):
    tile = jnp.zeros((8, 128), jnp.int32).at[0, : ids.size].set(ids.reshape(-1))
    shape = (RING_Y, RING_Z, CORES, 8, 128)
    held = pl.pallas_call(
        gather_ids_kernel,
        out_shape=jax.ShapeDtypeStruct(shape, jnp.int32),
        in_specs=[pl.BlockSpec(memory_space=pltpu.VMEM)],
        out_specs=pl.BlockSpec(memory_space=pltpu.VMEM),
        scratch_shapes=[
            pltpu.VMEM(shape, jnp.int32),
            pltpu.SemaphoreType.DMA((11,)),
            pltpu.SemaphoreType.DMA((11,)),
        ],
        compiler_params=pltpu.CompilerParams(collective_id=0, has_side_effects=True),
        name="gather_ids",
    )(tile)
    return held[..., 0, : ids.size].reshape(-1)


def merge(a, b):
    high = jnp.maximum(a[0:1], b[0:1])
    low = jnp.maximum(jnp.minimum(a[0:1], b[0:1]), jnp.maximum(a[1:2], b[1:2]))
    return jnp.concatenate([high, low, jnp.zeros((6, high.shape[1]), high.dtype)], axis=0)


def best_kernel(slab_ref, queries_ref, out_ref, own, after_core, after_depth, landed, send_sem, recv_sem):
    core, depth, row = peer_groups()
    greet(core + depth + row)
    scores = lax.dot_general(
        slab_ref[...],
        queries_ref[...],
        (((1,), (1,)), ((), ())),
        preferred_element_type=jnp.float32,
    )
    top = jnp.max(scores, axis=0, keepdims=True)
    at_top = scores == top
    ties = jnp.sum(jnp.where(at_top, 1.0, 0.0), axis=0, keepdims=True)
    rest = jnp.max(jnp.where(at_top, -jnp.inf, scores), axis=0, keepdims=True)
    second = jnp.where(ties > 1.5, top, rest)
    own[...] = jnp.concatenate([top, second, jnp.zeros((6, top.shape[1]), top.dtype)], axis=0)
    slot = 0
    holders = [own, after_core, after_depth, out_ref]
    for stage, peers in enumerate((core, depth, row)):
        source = holders[stage]
        copies = []
        for i, peer in enumerate(peers):
            copies.append(
                send(source, landed.at[slot + i], send_sem.at[slot + i], recv_sem.at[slot + i], peer)
            )
        for copy in copies:
            copy.wait()
        total = source[...]
        for i in range(len(peers)):
            total = merge(total, landed[slot + i])
        holders[stage + 1][...] = total
        slot += len(peers)


def best_two(key_slab, queries):
    rows = queries.shape[0]
    return pl.pallas_call(
        best_kernel,
        out_shape=jax.ShapeDtypeStruct((8, rows), jnp.float32),
        in_specs=[pl.BlockSpec(memory_space=pltpu.VMEM)] * 2,
        out_specs=pl.BlockSpec(memory_space=pltpu.VMEM),
        scratch_shapes=[pltpu.VMEM((8, rows), jnp.float32)] * 3
        + [
            pltpu.VMEM((11, 8, rows), jnp.float32),
            pltpu.SemaphoreType.DMA((11,)),
            pltpu.SemaphoreType.DMA((11,)),
        ],
        compiler_params=pltpu.CompilerParams(collective_id=1, has_side_effects=True),
        name="best_two",
    )(key_slab, queries)


def take_kernel(counts, reach, locs_ref, *refs):
    sources = refs[: len(counts)]
    outs = refs[len(counts) : -1]
    sems = refs[-1]
    starts = np.concatenate([[0], np.cumsum(counts)]).tolist()
    width = outs[0].shape[0]

    def begin(s, carry):
        for d, out in enumerate(outs):
            at = locs_ref[d, s]
            for k, source in enumerate(sources):
                if k not in reach[d]:
                    continue

                @pl.when((at >= starts[k]) & (at < starts[k + 1]))
                def _():
                    pltpu.make_async_copy(
                        source.at[at - starts[k]], out.at[s], sems.at[d, s]
                    ).start()

        return carry

    lax.fori_loop(0, width, begin, 0)

    def finish(s, carry):
        for d, out in enumerate(outs):
            pltpu.make_async_copy(sources[0].at[0], out.at[s], sems.at[d, s]).wait()
        return carry

    lax.fori_loop(0, width, finish, 0)


def take(sources, reach, locs):
    counts = tuple(s.shape[0] for s in sources)
    width = locs.shape[1]
    item = sources[0].shape[1:]
    nbytes = 4 * width * item[0] * item[1] * 2
    return pl.pallas_call(
        functools.partial(take_kernel, counts, reach),
        out_shape=[jax.ShapeDtypeStruct((width, *item), sources[0].dtype)] * 2,
        in_specs=[pl.BlockSpec(memory_space=pltpu.SMEM)]
        + [pl.BlockSpec(memory_space=pl.ANY)] * len(sources),
        out_specs=[pl.BlockSpec(memory_space=pl.ANY)] * 2,
        scratch_shapes=[pltpu.SemaphoreType.DMA((2, width))],
        cost_estimate=pl.CostEstimate(flops=0, bytes_accessed=nbytes, transcendentals=0),
        name="take_spans",
    )(locs, *sources)


def routes(all_ids):
    requests = all_ids.shape[0]
    per_device = requests // (RING_Y * RING_Z * CORES)
    index = np.arange(requests)
    k, n = index // per_device, index % per_device
    to_y, to_z = k // (RING_Z * CORES), (k // CORES) % RING_Z
    tie_y = jnp.asarray((n // 2 + k) % 2 == 1)
    tie_z = jnp.asarray((n + k) % 2 == 1)
    order = jnp.asarray(index, jnp.int32)
    to_y, to_z = jnp.asarray(to_y, jnp.int32), jnp.asarray(to_z, jnp.int32)
    y, z, c = place()
    shard, offset = all_ids // 64, all_ids % 64
    from_y, from_z, from_c = shard // (RING_Z * CORES), (shard // CORES) % RING_Z, shard % CORES
    loc = jnp.where(from_c == c, 0, 64) + offset
    base = 128
    sends = []

    def travel(position, target, ring, tie, node_of, mine, caps, loc, base):
        ahead = (target - position) % ring
        back = (ahead > ring // 2) | ((ahead == ring // 2) & tie)
        left = jnp.where(back, (ring - ahead) % ring, ahead)
        step = jnp.where(back, ring - 1, 1)
        way = back.astype(jnp.int32)
        for width in caps:
            node = node_of(position) * 2 + way
            moving = left > 0
            seat = jnp.where(moving, node, -1)
            priority = (16 - left) * 1024 + order
            before = (seat[:, None] == seat[None, :]) & (priority[:, None] < priority[None, :])
            rank = jnp.sum(before.astype(jnp.int32), axis=0)
            goes = moving & (rank < width)
            seat_rank = jnp.where(goes, node * 64 + rank, -1)
            wanted = (mine * 2 + np.arange(2, dtype=np.int32))[:, None] * 64 + np.arange(
                width, dtype=np.int32
            )
            hit = seat_rank[None, None, :] == wanted[:, :, None]
            sends.append(jnp.sum(jnp.where(hit, loc[None, None, :], 0), axis=-1))
            loc = jnp.where(goes, base + way * width + rank, loc)
            base += 2 * width
            position = jnp.where(goes, (position + step) % ring, position)
            left = left - goes.astype(jnp.int32)
        return jnp.max(left), loc, base

    stuck_y, loc, base = travel(
        from_y, to_y, RING_Y, tie_y, lambda p: p * RING_Z + from_z, y * RING_Z + z, Y_CAPS, loc, base
    )
    stuck_z, loc, base = travel(
        from_z, to_z, RING_Z, tie_z, lambda p: to_y * RING_Z + p, y * RING_Z + z, Z_CAPS, loc, base
    )
    table = loc.reshape(RING_Y * RING_Z, CORES, per_device)
    here = lax.dynamic_index_in_dim(table, y * RING_Z + z, 0, False)
    own = lax.dynamic_index_in_dim(here, c, 0, False)
    other = lax.dynamic_index_in_dim(here, 1 - c, 0, False)
    return sends, jnp.stack([own, other]), jnp.maximum(stuck_y, stuck_z)


def carried(held, sends, final, step):
    held_locs = lambda locs: jnp.where(locs < 128, locs + step, locs)
    sources = [held]
    y_count = 2 * len(Y_CAPS)
    moves = [(1, 0)] * len(Y_CAPS) + [(0, 1)] * len(Z_CAPS)
    for r, (dy, dz) in enumerate(moves):
        if dy:
            reach = [[0] + list(range(1 + d, len(sources), 2)) for d in range(2)]
        else:
            reach = [
                list(range(1 + y_count)) + list(range(1 + y_count + d, len(sources), 2))
                for d in range(2)
            ]
        up, down = take(sources, reach, held_locs(sends[r]))
        sources += [
            lax.ppermute(up, "keys", shifted(dy, dz, 0)),
            lax.ppermute(down, "keys", shifted(-dy, -dz, 0)),
        ]
    everything = list(range(len(sources)))
    own, other = take(sources, [everything] * 2, held_locs(final))
    return own, lax.ppermute(other, "keys", shifted(0, 0, 1))


def direct(neighbour_store, neighbour_ids):
    key_count = lax.axis_size("keys")
    shard_spans = neighbour_store.shape[0]
    flat_ids = neighbour_ids.reshape(-1)
    target, offset = flat_ids // shard_spans, flat_ids % shard_spans
    hit = target[:, None] == jnp.arange(key_count, dtype=jnp.int32)[None, :]
    table = jnp.sum(jnp.where(hit, offset[:, None], 0), axis=0)
    incoming = lax.all_to_all(table, "keys", split_axis=0, concat_axis=0, tiled=True)
    firsts, seconds = take([neighbour_store], [[0]] * 2, jnp.stack([incoming, incoming + 1]))
    arrived = [
        lax.all_to_all(spans, "keys", split_axis=0, concat_axis=0, tiled=True)
        for spans in (firsts, seconds)
    ]
    return take(arrived, [[0], [1]], jnp.stack([target, key_count + target]))


def body(span_queries, key_slab, neighbour_store, neighbour_ids, attn_queries, kv_weight):
    position = lax.axis_index("keys")
    y, z, c = place()
    own_spans = neighbour_ids.shape[0]
    span_rows = neighbour_store.shape[1]
    enc_width = neighbour_store.shape[2]
    half = span_rows // 2
    all_ids = gather_ids(neighbour_ids)
    kept = lax.dynamic_slice_in_dim(neighbour_store, c * half, half, axis=1)
    given = lax.dynamic_slice_in_dim(neighbour_store, (1 - c) * half, half, axis=1)
    held = jnp.concatenate([kept, lax.ppermute(given, "keys", shifted(0, 0, 1))], axis=0)
    groups = [[key_of(a, b, d) for a in range(RING_Y) for b in range(RING_Z)] for d in range(CORES)]
    weight_own = lax.all_gather(kv_weight, "keys", axis=1, axis_index_groups=groups)
    weight_other = lax.ppermute(weight_own, "keys", shifted(0, 0, 1))
    first = jnp.where(c == 0, weight_own, weight_other)
    second = jnp.where(c == 0, weight_other, weight_own)
    weights_all = jnp.stack([first, second], axis=2).reshape(2, HEADS * HEAD_DIM, enc_width)
    all_queries = lax.all_gather(span_queries, "keys", axis=0, tiled=True)
    sends, final, stuck = routes(all_ids)
    flag = jnp.full((8, 128), stuck, jnp.int32)
    seq = lax.axis_size("seq")
    worst = flag
    for d in range(1, seq):
        worst = jnp.maximum(
            worst, lax.ppermute(flag, "seq", [(s, (s + d) % seq) for s in range(seq)])
        )
    pieces = carried(held, sends, final, 0) + carried(held, sends, final, 1)

    def resend(store, ids, *fast):
        return tuple(
            spans[:, h * half : (h + 1) * half] for spans in direct(store, ids) for h in range(2)
        )

    pieces = lax.cond(
        worst[0, 0] > 0, resend, lambda store, ids, *fast: fast, neighbour_store, neighbour_ids, *pieces
    )
    neighbours = jnp.stack(
        [p.reshape(own_spans, 2, half, enc_width) for p in pieces], axis=1
    ).reshape(own_spans * 4 * span_rows, enc_width)
    best = best_two(key_slab, all_queries)
    best_scores = lax.dynamic_slice_in_dim(best, position * own_spans, own_spans, axis=1)[:2].T
    keys_values = jnp.einsum(
        "re,tce->rtc", neighbours, weights_all, preferred_element_type=jnp.float32
    ).astype(jnp.bfloat16)
    key_rows = keys_values[:, 0].reshape(own_spans, 4 * span_rows, HEADS, HEAD_DIM)
    value_rows = keys_values[:, 1].reshape(own_spans, 4 * span_rows, HEADS, HEAD_DIM)
    queries = attn_queries.reshape(own_spans, span_rows, HEADS, HEAD_DIM)
    logits = jnp.einsum(
        "cqhd,ckhd->chqk", queries, key_rows, preferred_element_type=jnp.float32
    ) * HEAD_DIM ** (-0.5)
    largest = jnp.max(logits, axis=-1, keepdims=True)
    expo_terms = jnp.exp(logits - largest)
    weights = (expo_terms / jnp.sum(expo_terms, axis=-1, keepdims=True)).astype(jnp.bfloat16)
    output = jnp.einsum("chqk,ckhd->cqhd", weights, value_rows, preferred_element_type=jnp.float32)
    attended = output.astype(jnp.bfloat16).reshape(own_spans * span_rows, HEADS * HEAD_DIM)
    return (best_scores, attended)


def solution(mesh):
    return jax.shard_map(
        body,
        mesh=mesh,
        in_specs=(
            P(("keys", "seq"), None),
            P("keys", None),
            P("keys", None, None),
            P(("keys", "seq"), None),
            P(("keys", "seq"), None),
            P(None, "keys", None),
        ),
        out_specs=(P(("keys", "seq"), None), P(("keys", "seq"), None)),
        check_vma=False,
    )
```

```python
import functools

import jax
import jax.numpy as jnp
import numpy as np
from jax import lax
from jax.experimental import pallas as pl
from jax.experimental.pallas import tpu as pltpu
from jax.sharding import PartitionSpec as P

HEADS = 16
HEAD_DIM = 128
RING_Y, RING_Z, CORES = 4, 8, 2
Y_CAPS = (24, 17)
Z_CAPS = (12, 12, 11, 10)


def key_of(y, z, c):
    return (y * RING_Z + z) * CORES + c


def place():
    k = lax.axis_index("keys")
    return k // (RING_Z * CORES), (k // CORES) % RING_Z, k % CORES


def shifted(dy, dz, dc):
    pairs = []
    for y in range(RING_Y):
        for z in range(RING_Z):
            for c in range(CORES):
                to = key_of((y + dy) % RING_Y, (z + dz) % RING_Z, (c + dc) % CORES)
                pairs.append((key_of(y, z, c), to))
    return pairs


def greet(peers):
    barrier = pltpu.get_barrier_semaphore()
    for peer in peers:
        pl.semaphore_signal(
            barrier, inc=1, device_id={"keys": peer}, device_id_type=pl.DeviceIdType.MESH
        )
    pl.semaphore_wait(barrier, len(peers))


def peer_groups():
    y, z, c = place()
    core = [key_of(y, z, 1 - c)]
    depth = [key_of(y, (z + d) % RING_Z, c) for d in range(1, RING_Z)]
    row = [key_of((y + d) % RING_Y, z, c) for d in range(1, RING_Y)]
    return core, depth, row


def send(src, dst, send_sem, recv_sem, peer):
    copy = pltpu.make_async_remote_copy(
        src_ref=src,
        dst_ref=dst,
        send_sem=send_sem,
        recv_sem=recv_sem,
        device_id={"keys": peer},
        device_id_type=pl.DeviceIdType.MESH,
    )
    copy.start()
    return copy


def gather_ids_kernel(ids_ref, out_ref, held, send_sem, recv_sem):
    y, z, c = place()
    core, depth, row = peer_groups()
    greet(core + depth + row)
    held[y, z, c] = ids_ref[...]
    copies = [send(held.at[y, z, c], held.at[y, z, c], send_sem.at[0], recv_sem.at[0], core[0])]
    for copy in copies:
        copy.wait()
    copies = []
    for i, peer in enumerate(depth):
        copies.append(
            send(held.at[y, z], held.at[y, z], send_sem.at[1 + i], recv_sem.at[1 + i], peer)
        )
    for copy in copies:
        copy.wait()
    copies = []
    for i, peer in enumerate(row):
        copies.append(send(held.at[y], held.at[y], send_sem.at[8 + i], recv_sem.at[8 + i], peer))
    for copy in copies:
        copy.wait()
    out_ref[...] = held[...]


def gather_ids(ids):
    tile = jnp.zeros((8, 128), jnp.int32).at[0, : ids.size].set(ids.reshape(-1))
    shape = (RING_Y, RING_Z, CORES, 8, 128)
    held = pl.pallas_call(
        gather_ids_kernel,
        out_shape=jax.ShapeDtypeStruct(shape, jnp.int32),
        in_specs=[pl.BlockSpec(memory_space=pltpu.VMEM)],
        out_specs=pl.BlockSpec(memory_space=pltpu.VMEM),
        scratch_shapes=[
            pltpu.VMEM(shape, jnp.int32),
            pltpu.SemaphoreType.DMA((11,)),
            pltpu.SemaphoreType.DMA((11,)),
        ],
        compiler_params=pltpu.CompilerParams(collective_id=0, has_side_effects=True),
        name="gather_ids",
    )(tile)
    return held[..., 0, : ids.size].reshape(-1)


def merge(a, b):
    high = jnp.maximum(a[0:1], b[0:1])
    low = jnp.maximum(jnp.minimum(a[0:1], b[0:1]), jnp.maximum(a[1:2], b[1:2]))
    return jnp.concatenate([high, low, jnp.zeros((6, high.shape[1]), high.dtype)], axis=0)


def best_kernel(
    slab_ref, mine_ref, other_ref, out_ref, own, after_core, after_depth, landed, send_sem, recv_sem
):
    core, depth, row = peer_groups()
    greet(core + depth + row)
    c = place()[2]
    for at, queries_ref in ((c, mine_ref), (1 - c, other_ref)):
        count = queries_ref.shape[0]
        scores = lax.dot_general(
            slab_ref[...],
            queries_ref[...],
            (((1,), (1,)), ((), ())),
            preferred_element_type=jnp.float32,
        )
        top = jnp.max(scores, axis=0, keepdims=True)
        at_top = scores == top
        ties = jnp.sum(jnp.where(at_top, 1.0, 0.0), axis=0, keepdims=True)
        rest = jnp.max(jnp.where(at_top, -jnp.inf, scores), axis=0, keepdims=True)
        second = jnp.where(ties > 1.5, top, rest)
        own[:, pl.ds(pl.multiple_of(at * count, count), count)] = jnp.concatenate(
            [top, second, jnp.zeros((6, count), top.dtype)], axis=0
        )
    slot = 0
    holders = [own, after_core, after_depth, out_ref]
    for stage, peers in enumerate((core, depth, row)):
        source = holders[stage]
        copies = []
        for i, peer in enumerate(peers):
            copies.append(
                send(source, landed.at[slot + i], send_sem.at[slot + i], recv_sem.at[slot + i], peer)
            )
        for copy in copies:
            copy.wait()
        total = source[...]
        for i in range(len(peers)):
            total = merge(total, landed[slot + i])
        holders[stage + 1][...] = total
        slot += len(peers)


def best_two(key_slab, mine, other):
    rows = 2 * mine.shape[0]
    return pl.pallas_call(
        best_kernel,
        out_shape=jax.ShapeDtypeStruct((8, rows), jnp.float32),
        in_specs=[pl.BlockSpec(memory_space=pltpu.VMEM)] * 3,
        out_specs=pl.BlockSpec(memory_space=pltpu.VMEM),
        scratch_shapes=[pltpu.VMEM((8, rows), jnp.float32)] * 3
        + [
            pltpu.VMEM((11, 8, rows), jnp.float32),
            pltpu.SemaphoreType.DMA((11,)),
            pltpu.SemaphoreType.DMA((11,)),
        ],
        compiler_params=pltpu.CompilerParams(collective_id=1, has_side_effects=True),
        name="best_two",
    )(key_slab, mine, other)


def take_kernel(counts, reach, row, locs_ref, *refs):
    sources = refs[: len(counts)]
    outs = refs[len(counts) : -1]
    sems = refs[-1]
    starts = np.concatenate([[0], np.cumsum(counts)]).tolist()
    width, rows = outs[0].shape[0], outs[0].shape[1]

    def piece(k, at):
        if sources[k].shape[1] == rows:
            return sources[k].at[at]
        return sources[k].at[at, pl.ds(pl.multiple_of(row(), rows), rows)]

    def begin(s, carry):
        for d, out in enumerate(outs):
            at = locs_ref[d, s]
            for k in reach[d]:

                @pl.when((at >= starts[k]) & (at < starts[k + 1]))
                def _():
                    pltpu.make_async_copy(
                        piece(k, at - starts[k]), out.at[s], sems.at[d, s]
                    ).start()

        return carry

    lax.fori_loop(0, width, begin, 0)

    def finish(s, carry):
        for d, out in enumerate(outs):
            pltpu.make_async_copy(piece(reach[d][0], 0), out.at[s], sems.at[d, s]).wait()
        return carry

    lax.fori_loop(0, width, finish, 0)


def take(sources, reach, locs, rows, row=None):
    counts = tuple(s.shape[0] for s in sources)
    width = locs.shape[1]
    item = (rows, sources[0].shape[2])
    nbytes = 4 * width * item[0] * item[1] * 2
    return pl.pallas_call(
        functools.partial(take_kernel, counts, reach, row),
        out_shape=[jax.ShapeDtypeStruct((width, *item), sources[0].dtype)] * 2,
        in_specs=[pl.BlockSpec(memory_space=pltpu.SMEM)]
        + [pl.BlockSpec(memory_space=pl.ANY)] * len(sources),
        out_specs=[pl.BlockSpec(memory_space=pltpu.VMEM)] * 2,
        scratch_shapes=[pltpu.SemaphoreType.DMA((2, width))],
        cost_estimate=pl.CostEstimate(flops=0, bytes_accessed=nbytes, transcendentals=0),
        compiler_params=pltpu.CompilerParams(vmem_limit_bytes=32 << 20),
        name="take_spans",
    )(locs, *sources)


def attend_kernel(own0, other0, own1, other1, w_own, w_other, q_ref, o_ref, x, wk, wv):
    c = place()[2]
    pieces = (own0, other0, own1, other1)
    spans = own0.shape[0] // 2
    rows = own0.shape[1] * 2
    width = own0.shape[2]

    @pl.when(pl.program_id(0) == 0)
    def _():
        for u in range(spans):
            for i, piece in enumerate(pieces):
                at = (u * 4 + i) * rows
                x[at : at + rows, :] = piece[2 * u : 2 * u + 2].reshape(rows, width)

    for kind, w in enumerate((wk, wv)):
        for j in range(w_own.shape[0]):
            mine = pl.multiple_of(j * 64 + c * 32, 32)
            theirs = pl.multiple_of(j * 64 + (1 - c) * 32, 32)
            w[pl.ds(mine, 32), :] = w_own[j, kind * 32 : kind * 32 + 32, :]
            w[pl.ds(theirs, 32), :] = w_other[j, kind * 32 : kind * 32 + 32, :]
    contract = (((1,), (1,)), ((), ()))
    dot = functools.partial(lax.dot_general, preferred_element_type=jnp.float32)
    for u in range(spans):
        near = x[u * 4 * rows : (u + 1) * 4 * rows, :]
        keys = dot(near, wk[...], contract).astype(jnp.bfloat16)
        values = dot(near, wv[...], contract).astype(jnp.bfloat16)
        for h in range(keys.shape[1] // HEAD_DIM):
            cols = slice(h * HEAD_DIM, (h + 1) * HEAD_DIM)
            q = q_ref[u * rows : (u + 1) * rows, cols]
            logits = dot(q, keys[:, cols], contract) * HEAD_DIM ** (-0.5)
            largest = jnp.max(logits, axis=-1, keepdims=True)
            terms = jnp.exp(logits - largest)
            total = jnp.sum(terms, axis=-1, keepdims=True)
            weights = (terms * (1.0 / total)).astype(jnp.bfloat16)
            out = dot(weights, values[:, cols], (((1,), (0,)), ((), ())))
            o_ref[u * rows : (u + 1) * rows, cols] = out.astype(jnp.bfloat16)


def attend(pieces, w_own, w_other, queries):
    requests, half, width = pieces[0].shape
    spans = requests // 2
    tokens, columns = queries.shape
    steps = 8
    pairs = w_own.shape[0] // steps
    cols = columns // steps
    whole = pl.BlockSpec((requests, half, width), lambda g: (0, 0, 0))
    weight = pl.BlockSpec((pairs, w_own.shape[1], width), lambda g: (g, 0, 0))
    block = pl.BlockSpec((tokens, cols), lambda g: (0, g))
    flops = 2 * spans * 8 * half * width * 2 * columns
    return pl.pallas_call(
        attend_kernel,
        grid=(steps,),
        out_shape=jax.ShapeDtypeStruct((tokens, columns), jnp.bfloat16),
        in_specs=[whole] * 4 + [weight] * 2 + [block],
        out_specs=block,
        scratch_shapes=[
            pltpu.VMEM((spans * 8 * half, width), jnp.bfloat16),
            pltpu.VMEM((cols, width), jnp.bfloat16),
            pltpu.VMEM((cols, width), jnp.bfloat16),
        ],
        compiler_params=pltpu.CompilerParams(vmem_limit_bytes=48 << 20),
        cost_estimate=pl.CostEstimate(
            flops=flops, bytes_accessed=20 << 20, transcendentals=tokens * HEADS * 256
        ),
        name="attend",
    )(*pieces, w_own, w_other, queries)


def routes(all_ids):
    requests = all_ids.shape[0]
    per_device = requests // (RING_Y * RING_Z * CORES)
    index = np.arange(requests)
    k, n = index // per_device, index % per_device
    to_y, to_z = k // (RING_Z * CORES), (k // CORES) % RING_Z
    tie_y = jnp.asarray((n // 2 + k) % 2 == 1)
    tie_z = jnp.asarray((n + k) % 2 == 1)
    order = jnp.asarray(index, jnp.int32)
    to_y, to_z = jnp.asarray(to_y, jnp.int32), jnp.asarray(to_z, jnp.int32)
    y, z, c = place()
    shard, offset = all_ids // 64, all_ids % 64
    from_y, from_z, from_c = shard // (RING_Z * CORES), (shard // CORES) % RING_Z, shard % CORES
    loc = jnp.where(from_c == c, 0, 64) + offset
    base = 128
    sends = []

    def travel(position, target, ring, tie, node_of, mine, caps, loc, base):
        ahead = (target - position) % ring
        back = (ahead > ring // 2) | ((ahead == ring // 2) & tie)
        left = jnp.where(back, (ring - ahead) % ring, ahead)
        step = jnp.where(back, ring - 1, 1)
        way = back.astype(jnp.int32)
        for width in caps:
            node = node_of(position) * 2 + way
            moving = left > 0
            seat = jnp.where(moving, node, -1)
            priority = (16 - left) * 1024 + order
            before = (seat[:, None] == seat[None, :]) & (priority[:, None] < priority[None, :])
            rank = jnp.sum(before.astype(jnp.int32), axis=0)
            goes = moving & (rank < width)
            seat_rank = jnp.where(goes, node * 64 + rank, -1)
            wanted = (mine * 2 + np.arange(2, dtype=np.int32))[:, None] * 64 + np.arange(
                width, dtype=np.int32
            )
            hit = seat_rank[None, None, :] == wanted[:, :, None]
            sends.append(jnp.sum(jnp.where(hit, loc[None, None, :], 0), axis=-1))
            loc = jnp.where(goes, base + way * width + rank, loc)
            base += 2 * width
            position = jnp.where(goes, (position + step) % ring, position)
            left = left - goes.astype(jnp.int32)
        return jnp.max(left), loc, base

    stuck_y, loc, base = travel(
        from_y, to_y, RING_Y, tie_y, lambda p: p * RING_Z + from_z, y * RING_Z + z, Y_CAPS, loc, base
    )
    stuck_z, loc, base = travel(
        from_z, to_z, RING_Z, tie_z, lambda p: to_y * RING_Z + p, y * RING_Z + z, Z_CAPS, loc, base
    )
    table = loc.reshape(RING_Y * RING_Z, CORES, per_device)
    here = lax.dynamic_index_in_dim(table, y * RING_Z + z, 0, False)
    own = lax.dynamic_index_in_dim(here, c, 0, False)
    other = lax.dynamic_index_in_dim(here, 1 - c, 0, False)
    return sends, jnp.stack([own, other]), jnp.maximum(stuck_y, stuck_z)


def carried(store, swapped, sends, final, step):
    rows = swapped.shape[1]
    row = lambda: place()[2] * rows
    held_locs = lambda locs: jnp.where(locs < 128, locs + step, locs)
    sources = [store, swapped]
    y_count = 2 * len(Y_CAPS)
    moves = [(1, 0)] * len(Y_CAPS) + [(0, 1)] * len(Z_CAPS)
    for r, (dy, dz) in enumerate(moves):
        if dy:
            reach = [[0, 1] + list(range(2 + d, len(sources), 2)) for d in range(2)]
        else:
            reach = [
                list(range(2 + y_count)) + list(range(2 + y_count + d, len(sources), 2))
                for d in range(2)
            ]
        up, down = take(sources, reach, held_locs(sends[r]), rows, row)
        sources += [
            lax.ppermute(up, "keys", shifted(dy, dz, 0)),
            lax.ppermute(down, "keys", shifted(-dy, -dz, 0)),
        ]
    everything = list(range(len(sources)))
    own, other = take(sources, [everything] * 2, held_locs(final), rows, row)
    return own, lax.ppermute(other, "keys", shifted(0, 0, 1))


def direct(neighbour_store, neighbour_ids):
    key_count = lax.axis_size("keys")
    shard_spans = neighbour_store.shape[0]
    flat_ids = neighbour_ids.reshape(-1)
    target, offset = flat_ids // shard_spans, flat_ids % shard_spans
    hit = target[:, None] == jnp.arange(key_count, dtype=jnp.int32)[None, :]
    table = jnp.sum(jnp.where(hit, offset[:, None], 0), axis=0)
    incoming = lax.all_to_all(table, "keys", split_axis=0, concat_axis=0, tiled=True)
    firsts, seconds = take(
        [neighbour_store], [[0]] * 2, jnp.stack([incoming, incoming + 1]), neighbour_store.shape[1]
    )
    arrived = [
        lax.all_to_all(spans, "keys", split_axis=0, concat_axis=0, tiled=True)
        for spans in (firsts, seconds)
    ]
    locs = jnp.stack([target, key_count + target])
    return take(arrived, [[0], [1]], locs, neighbour_store.shape[1])


def body(span_queries, key_slab, neighbour_store, neighbour_ids, attn_queries, kv_weight):
    position = lax.axis_index("keys")
    y, z, c = place()
    own_spans = neighbour_ids.shape[0]
    span_rows = neighbour_store.shape[1]
    enc_width = neighbour_store.shape[2]
    half = span_rows // 2
    all_ids = gather_ids(neighbour_ids)
    given = lax.dynamic_slice_in_dim(neighbour_store, (1 - c) * half, half, axis=1)
    swapped = lax.ppermute(given, "keys", shifted(0, 0, 1))
    asked = jnp.zeros((16, enc_width), span_queries.dtype)
    asked = lax.dynamic_update_slice(asked, span_queries, (0, 0))
    shard = jnp.concatenate([kv_weight[0], kv_weight[1], asked], axis=0)
    groups = [[key_of(a, b, d) for a in range(RING_Y) for b in range(RING_Z)] for d in range(CORES)]
    weight_own = lax.all_gather(shard, "keys", axis=0, axis_index_groups=groups)
    weight_other = lax.ppermute(weight_own, "keys", shifted(0, 0, 1))
    sends, final, stuck = routes(all_ids)
    flag = jnp.full((8, 128), stuck, jnp.int32)
    seq = lax.axis_size("seq")
    worst = flag
    for d in range(1, seq):
        worst = jnp.maximum(
            worst, lax.ppermute(flag, "seq", [(s, (s + d) % seq) for s in range(seq)])
        )
    pieces = carried(neighbour_store, swapped, sends, final, 0)
    pieces += carried(neighbour_store, swapped, sends, final, 1)

    def resend(store, ids, *fast):
        return tuple(
            spans[:, h * half : (h + 1) * half] for spans in direct(store, ids) for h in range(2)
        )

    pieces = lax.cond(
        worst[0, 0] > 0, resend, lambda store, ids, *fast: fast, neighbour_store, neighbour_ids, *pieces
    )
    asked_rows = [
        w[:, -16:, : span_queries.shape[1]].reshape(-1, span_queries.shape[1])
        for w in (weight_own, weight_other)
    ]
    best = best_two(key_slab, *asked_rows)
    column = c * asked_rows[0].shape[0] + (position // CORES) * 16
    best_scores = lax.dynamic_slice_in_dim(best, column, own_spans, axis=1)[:2].T
    attended = attend(pieces, weight_own, weight_other, attn_queries)
    return (best_scores, attended)


def solution(mesh):
    return jax.shard_map(
        body,
        mesh=mesh,
        in_specs=(
            P(("keys", "seq"), None),
            P("keys", None),
            P("keys", None, None),
            P(("keys", "seq"), None),
            P(("keys", "seq"), None),
            P(None, "keys", None),
        ),
        out_specs=(P(("keys", "seq"), None), P(("keys", "seq"), None)),
        check_vma=False,
    )
```

```python
import functools

import jax
import jax.numpy as jnp
import numpy as np
from jax import lax
from jax.experimental import pallas as pl
from jax.experimental.pallas import tpu as pltpu
from jax.sharding import PartitionSpec as P

HEADS = 16
HEAD_DIM = 128
RING_Y, RING_Z, CORES = 4, 8, 2
Y_CAPS = (24, 17)
Z_CAPS = (12, 12, 11, 10)


def key_of(y, z, c):
    return (y * RING_Z + z) * CORES + c


def place():
    k = lax.axis_index("keys")
    return k // (RING_Z * CORES), (k // CORES) % RING_Z, k % CORES


def shifted(dy, dz, dc):
    pairs = []
    for y in range(RING_Y):
        for z in range(RING_Z):
            for c in range(CORES):
                to = key_of((y + dy) % RING_Y, (z + dz) % RING_Z, (c + dc) % CORES)
                pairs.append((key_of(y, z, c), to))
    return pairs


def greet(peers):
    barrier = pltpu.get_barrier_semaphore()
    for peer in peers:
        pl.semaphore_signal(
            barrier, inc=1, device_id={"keys": peer}, device_id_type=pl.DeviceIdType.MESH
        )
    pl.semaphore_wait(barrier, len(peers))


def peer_groups():
    y, z, c = place()
    core = [key_of(y, z, 1 - c)]
    depth = [key_of(y, (z + d) % RING_Z, c) for d in range(1, RING_Z)]
    row = [key_of((y + d) % RING_Y, z, c) for d in range(1, RING_Y)]
    return core, depth, row


def send(src, dst, send_sem, recv_sem, peer):
    copy = pltpu.make_async_remote_copy(
        src_ref=src,
        dst_ref=dst,
        send_sem=send_sem,
        recv_sem=recv_sem,
        device_id={"keys": peer},
        device_id_type=pl.DeviceIdType.MESH,
    )
    copy.start()
    return copy


def gather_ids_kernel(ids_ref, out_ref, held, send_sem, recv_sem):
    y, z, c = place()
    core, depth, row = peer_groups()
    greet(core + depth + row)
    held[y, z, c] = ids_ref[...]
    copies = [send(held.at[y, z, c], held.at[y, z, c], send_sem.at[0], recv_sem.at[0], core[0])]
    for copy in copies:
        copy.wait()
    copies = []
    for i, peer in enumerate(depth):
        copies.append(
            send(held.at[y, z], held.at[y, z], send_sem.at[1 + i], recv_sem.at[1 + i], peer)
        )
    for copy in copies:
        copy.wait()
    copies = []
    for i, peer in enumerate(row):
        copies.append(send(held.at[y], held.at[y], send_sem.at[8 + i], recv_sem.at[8 + i], peer))
    for copy in copies:
        copy.wait()
    out_ref[...] = held[...]


def gather_ids(ids):
    tile = jnp.zeros((8, 128), jnp.int32).at[0, : ids.size].set(ids.reshape(-1))
    shape = (RING_Y, RING_Z, CORES, 8, 128)
    held = pl.pallas_call(
        gather_ids_kernel,
        out_shape=jax.ShapeDtypeStruct(shape, jnp.int32),
        in_specs=[pl.BlockSpec(memory_space=pltpu.VMEM)],
        out_specs=pl.BlockSpec(memory_space=pltpu.VMEM),
        scratch_shapes=[
            pltpu.VMEM(shape, jnp.int32),
            pltpu.SemaphoreType.DMA((11,)),
            pltpu.SemaphoreType.DMA((11,)),
        ],
        compiler_params=pltpu.CompilerParams(collective_id=0, has_side_effects=True),
        name="gather_ids",
    )(tile)
    return held[..., 0, : ids.size].reshape(-1)


def merge(a, b):
    high = jnp.maximum(a[0:1], b[0:1])
    low = jnp.maximum(jnp.minimum(a[0:1], b[0:1]), jnp.maximum(a[1:2], b[1:2]))
    return jnp.concatenate([high, low, jnp.zeros((6, high.shape[1]), high.dtype)], axis=0)


def best_kernel(
    slab_ref, mine_ref, other_ref, out_ref, own, after_core, after_depth, landed, send_sem, recv_sem
):
    core, depth, row = peer_groups()
    greet(core + depth + row)
    c = place()[2]
    for at, queries_ref in ((c, mine_ref), (1 - c, other_ref)):
        count = queries_ref.shape[0]
        scores = lax.dot_general(
            slab_ref[...],
            queries_ref[...],
            (((1,), (1,)), ((), ())),
            preferred_element_type=jnp.float32,
        )
        top = jnp.max(scores, axis=0, keepdims=True)
        at_top = scores == top
        ties = jnp.sum(jnp.where(at_top, 1.0, 0.0), axis=0, keepdims=True)
        rest = jnp.max(jnp.where(at_top, -jnp.inf, scores), axis=0, keepdims=True)
        second = jnp.where(ties > 1.5, top, rest)
        own[:, pl.ds(pl.multiple_of(at * count, count), count)] = jnp.concatenate(
            [top, second, jnp.zeros((6, count), top.dtype)], axis=0
        )
    slot = 0
    holders = [own, after_core, after_depth, out_ref]
    for stage, peers in enumerate((core, depth, row)):
        source = holders[stage]
        copies = []
        for i, peer in enumerate(peers):
            copies.append(
                send(source, landed.at[slot + i], send_sem.at[slot + i], recv_sem.at[slot + i], peer)
            )
        for copy in copies:
            copy.wait()
        total = source[...]
        for i in range(len(peers)):
            total = merge(total, landed[slot + i])
        holders[stage + 1][...] = total
        slot += len(peers)


def best_two(key_slab, mine, other):
    rows = 2 * mine.shape[0]
    return pl.pallas_call(
        best_kernel,
        out_shape=jax.ShapeDtypeStruct((8, rows), jnp.float32),
        in_specs=[pl.BlockSpec(memory_space=pltpu.VMEM)] * 3,
        out_specs=pl.BlockSpec(memory_space=pltpu.VMEM),
        scratch_shapes=[pltpu.VMEM((8, rows), jnp.float32)] * 3
        + [
            pltpu.VMEM((11, 8, rows), jnp.float32),
            pltpu.SemaphoreType.DMA((11,)),
            pltpu.SemaphoreType.DMA((11,)),
        ],
        compiler_params=pltpu.CompilerParams(collective_id=1, has_side_effects=True),
        name="best_two",
    )(key_slab, mine, other)


def take_kernel(counts, reach, row, locs_ref, *refs):
    sources = refs[: len(counts)]
    outs = refs[len(counts) : -1]
    sems = refs[-1]
    starts = np.concatenate([[0], np.cumsum(counts)]).tolist()
    width, rows = outs[0].shape[0], outs[0].shape[1]

    def piece(k, at):
        if sources[k].shape[1] == rows:
            return sources[k].at[at]
        return sources[k].at[at, pl.ds(pl.multiple_of(row(), rows), rows)]

    def begin(s, carry):
        for d, out in enumerate(outs):
            at = locs_ref[d, s]
            for k in reach[d]:

                @pl.when((at >= starts[k]) & (at < starts[k + 1]))
                def _():
                    pltpu.make_async_copy(
                        piece(k, at - starts[k]), out.at[s], sems.at[d, s]
                    ).start()

        return carry

    lax.fori_loop(0, width, begin, 0)

    def finish(s, carry):
        for d, out in enumerate(outs):
            pltpu.make_async_copy(piece(reach[d][0], 0), out.at[s], sems.at[d, s]).wait()
        return carry

    lax.fori_loop(0, width, finish, 0)


def take(sources, reach, locs, rows, row=None):
    counts = tuple(s.shape[0] for s in sources)
    width = locs.shape[1]
    item = (rows, sources[0].shape[2])
    nbytes = 4 * width * item[0] * item[1] * 2
    return pl.pallas_call(
        functools.partial(take_kernel, counts, reach, row),
        out_shape=[jax.ShapeDtypeStruct((width, *item), sources[0].dtype)] * 2,
        in_specs=[pl.BlockSpec(memory_space=pltpu.SMEM)]
        + [pl.BlockSpec(memory_space=pl.ANY)] * len(sources),
        out_specs=[pl.BlockSpec(memory_space=pltpu.VMEM)] * 2,
        scratch_shapes=[pltpu.SemaphoreType.DMA((2, width))],
        cost_estimate=pl.CostEstimate(flops=0, bytes_accessed=nbytes, transcendentals=0),
        compiler_params=pltpu.CompilerParams(vmem_limit_bytes=32 << 20),
        name="take_spans",
    )(locs, *sources)


def attend_kernel(pieces, w_own, w_other, q_ref, o_ref, x, wk, wv):
    c = place()[2]
    parts, requests, part, width = pieces.shape
    spans = requests // 2
    rows = q_ref.shape[0] // spans

    @pl.when(pl.program_id(0) == 0)
    def _():
        for u in range(spans):
            for i in range(parts):
                at = (u * parts + i) * 2 * part
                x[at : at + 2 * part, :] = pieces[i, 2 * u : 2 * u + 2].reshape(2 * part, width)

    for kind, w in enumerate((wk, wv)):
        for j in range(w_own.shape[0]):
            mine = pl.multiple_of(j * 64 + c * 32, 32)
            theirs = pl.multiple_of(j * 64 + (1 - c) * 32, 32)
            w[pl.ds(mine, 32), :] = w_own[j, kind * 32 : kind * 32 + 32, :]
            w[pl.ds(theirs, 32), :] = w_other[j, kind * 32 : kind * 32 + 32, :]
    contract = (((1,), (1,)), ((), ()))
    dot = functools.partial(lax.dot_general, preferred_element_type=jnp.float32)
    for u in range(spans):
        near = x[u * 4 * rows : (u + 1) * 4 * rows, :]
        keys = dot(near, wk[...], contract).astype(jnp.bfloat16)
        values = dot(near, wv[...], contract).astype(jnp.bfloat16)
        for h in range(keys.shape[1] // HEAD_DIM):
            cols = slice(h * HEAD_DIM, (h + 1) * HEAD_DIM)
            q = q_ref[u * rows : (u + 1) * rows, cols]
            logits = dot(q, keys[:, cols], contract) * HEAD_DIM ** (-0.5)
            largest = jnp.max(logits, axis=-1, keepdims=True)
            terms = jnp.exp(logits - largest)
            total = jnp.sum(terms, axis=-1, keepdims=True)
            weights = (terms * (1.0 / total)).astype(jnp.bfloat16)
            out = dot(weights, values[:, cols], (((1,), (0,)), ((), ())))
            o_ref[u * rows : (u + 1) * rows, cols] = out.astype(jnp.bfloat16)


def attend(pieces, w_own, w_other, queries):
    parts, requests, part, width = pieces.shape
    near = requests * parts * part
    tokens, columns = queries.shape
    steps = 8
    pairs = w_own.shape[0] // steps
    cols = columns // steps
    whole = pl.BlockSpec(pieces.shape, lambda g: (0, 0, 0, 0))
    weight = pl.BlockSpec((pairs, w_own.shape[1], width), lambda g: (g, 0, 0))
    block = pl.BlockSpec((tokens, cols), lambda g: (0, g))
    flops = 2 * near * width * 2 * columns
    return pl.pallas_call(
        attend_kernel,
        grid=(steps,),
        out_shape=jax.ShapeDtypeStruct((tokens, columns), jnp.bfloat16),
        in_specs=[whole] + [weight] * 2 + [block],
        out_specs=block,
        scratch_shapes=[
            pltpu.VMEM((near, width), jnp.bfloat16),
            pltpu.VMEM((cols, width), jnp.bfloat16),
            pltpu.VMEM((cols, width), jnp.bfloat16),
        ],
        compiler_params=pltpu.CompilerParams(vmem_limit_bytes=48 << 20),
        cost_estimate=pl.CostEstimate(
            flops=flops, bytes_accessed=20 << 20, transcendentals=tokens * HEADS * 256
        ),
        name="attend",
    )(pieces, w_own, w_other, queries)


def routes(all_ids):
    requests = all_ids.shape[0]
    per_device = requests // (RING_Y * RING_Z * CORES)
    index = np.arange(requests)
    k, n = index // per_device, index % per_device
    to_y, to_z = k // (RING_Z * CORES), (k // CORES) % RING_Z
    tie_y = jnp.asarray((n // 2 + k) % 2 == 1)
    tie_z = jnp.asarray((n + k) % 2 == 1)
    order = jnp.asarray(index, jnp.int32)
    to_y, to_z = jnp.asarray(to_y, jnp.int32), jnp.asarray(to_z, jnp.int32)
    y, z, c = place()
    shard, offset = all_ids // 64, all_ids % 64
    from_y, from_z, from_c = shard // (RING_Z * CORES), (shard // CORES) % RING_Z, shard % CORES
    loc = jnp.where(from_c == c, 0, 64) + offset
    base = 128
    sends = []

    def travel(position, target, ring, tie, node_of, mine, caps, loc, base):
        ahead = (target - position) % ring
        back = (ahead > ring // 2) | ((ahead == ring // 2) & tie)
        left = jnp.where(back, (ring - ahead) % ring, ahead)
        step = jnp.where(back, ring - 1, 1)
        way = back.astype(jnp.int32)
        for width in caps:
            node = node_of(position) * 2 + way
            moving = left > 0
            seat = jnp.where(moving, node, -1)
            priority = (16 - left) * 1024 + order
            before = (seat[:, None] == seat[None, :]) & (priority[:, None] < priority[None, :])
            rank = jnp.sum(before.astype(jnp.int32), axis=0)
            goes = moving & (rank < width)
            seat_rank = jnp.where(goes, node * 64 + rank, -1)
            wanted = (mine * 2 + np.arange(2, dtype=np.int32))[:, None] * 64 + np.arange(
                width, dtype=np.int32
            )
            hit = seat_rank[None, None, :] == wanted[:, :, None]
            sends.append(jnp.sum(jnp.where(hit, loc[None, None, :], 0), axis=-1))
            loc = jnp.where(goes, base + way * width + rank, loc)
            base += 2 * width
            position = jnp.where(goes, (position + step) % ring, position)
            left = left - goes.astype(jnp.int32)
        return jnp.max(left), loc, base

    stuck_y, loc, base = travel(
        from_y, to_y, RING_Y, tie_y, lambda p: p * RING_Z + from_z, y * RING_Z + z, Y_CAPS, loc, base
    )
    stuck_z, loc, base = travel(
        from_z, to_z, RING_Z, tie_z, lambda p: to_y * RING_Z + p, y * RING_Z + z, Z_CAPS, loc, base
    )
    table = loc.reshape(RING_Y * RING_Z, CORES, per_device)
    here = lax.dynamic_index_in_dim(table, y * RING_Z + z, 0, False)
    own = lax.dynamic_index_in_dim(here, c, 0, False)
    other = lax.dynamic_index_in_dim(here, 1 - c, 0, False)
    return sends, jnp.stack([own, other]), jnp.maximum(stuck_y, stuck_z)


def issue_order(moves, widths, chunks):
    done = {(j, -1): 0.0 for j in range(chunks)}
    issued, order, free, clock = set(), [], {True: 0.0, False: 0.0}, 0.0
    while len(order) < chunks * len(moves):
        ready = []
        for j in range(chunks):
            r = sum((j, q) in issued for q in range(len(moves)))
            if r == len(moves) or (j, r - 1) not in done:
                continue
            if r == 0 and j >= 2 and (j - 2, len(Y_CAPS) - 1) not in issued:
                continue
            ready.append((max(clock, done[j, r - 1] + 2.5 * (r > 0)), j, r))
        at, j, r = min(ready)
        along_y = moves[r][0] != 0
        clock = at + 0.5
        free[along_y] = max(free[along_y], clock) + 0.65 * widths[r]
        done[j, r] = free[along_y]
        issued.add((j, r))
        order.append((j, r))
    return order


MOVES = [(1, 0)] * len(Y_CAPS) + [(0, 1)] * len(Z_CAPS)
WIDTHS = Y_CAPS + Z_CAPS
CHUNKS = 4
PART = 16


def carry_kernel(requests, locs_ref, final_ref, store_ref, out_ref, held, *rest):
    rounds = len(MOVES)
    total = CHUNKS * rounds
    out_bufs = rest[:total]
    in_bufs = rest[total : 2 * total]
    last, swap_sems, send_sems, recv_sems = rest[2 * total :]
    y, z, c = place()
    half = held.shape[1]
    spans = store_ref.shape[0]
    steps = [((y + dy) % RING_Y, (z + dz) % RING_Z) for dy, dz in ((1, 0), (-1, 0), (0, 1), (0, -1))]
    near = [key_of(a + 0, b + 0, c) for a, b in steps]
    buddy = key_of(y, z, 1 - c)
    greet(near + [buddy])
    mine = pl.ds(pl.multiple_of(c * half, half), half)
    theirs = pl.ds(pl.multiple_of((1 - c) * half, half), half)
    swap = send(
        store_ref.at[:, theirs], held.at[pl.ds(spans, spans)], swap_sems.at[0], swap_sems.at[1], buddy
    )
    keep = pltpu.make_async_copy(store_ref.at[:, mine], held.at[pl.ds(0, spans)], swap_sems.at[2])
    keep.start()
    swap.wait()
    keep.wait()
    bases = np.concatenate([[2 * spans], 2 * spans + np.cumsum(2 * np.array(WIDTHS))]).tolist()

    def picked(j, r, at):
        step, part = j // 2, j % 2
        rows = slice(part * PART, (part + 1) * PART)
        here = jnp.where(at < 2 * spans, at + step, 0)
        value = held[here, rows, :]
        for q in range(r):
            count = 2 * WIDTHS[q]
            inside = (at >= bases[q]) & (at < bases[q] + count)
            value = jnp.where(inside, in_bufs[j * rounds + q][jnp.where(inside, at - bases[q], 0)], value)
        return value

    flights = {}

    def land(j, r):
        for flight in flights[j, r]:
            flight.wait_recv()

    def issue(j, r):
        if r > 0:
            land(j, r - 1)
        width = WIDTHS[r]
        buf = out_bufs[j * rounds + r]

        def fill(s, carry):
            buf[s] = picked(j, r, locs_ref[r, s])
            return carry

        lax.fori_loop(0, 2 * width, fill, 0)
        flights[j, r] = []
        for d in range(2):
            part = pl.ds(d * width, width)
            k = (j * rounds + r) * 2 + d
            peer = near[d if MOVES[r][0] else 2 + d]
            flights[j, r].append(
                send(buf.at[part], in_bufs[j * rounds + r].at[part], send_sems.at[k], recv_sems.at[k], peer)
            )

    def finish(j):
        land(j, rounds - 1)

        def fill(s, carry):
            out_ref[2 * j, s] = picked(j, rounds, final_ref[0, s])
            last[j, s] = picked(j, rounds, final_ref[1, s])
            return carry

        lax.fori_loop(0, requests, fill, 0)
        k = 2 * total + j
        flights[j, rounds] = [
            send(last.at[j], out_ref.at[2 * j + 1], send_sems.at[k], recv_sems.at[k], buddy)
        ]

    waiting = []
    for j, r in issue_order(MOVES, WIDTHS, CHUNKS):
        issue(j, r)
        if r == rounds - 1:
            waiting.append(j)
        elif waiting:
            finish(waiting.pop(0))
    for j in waiting:
        finish(j)
    for j in range(CHUNKS):
        land(j, rounds)
    for copies in flights.values():
        for copy in copies:
            copy.wait_send()


def carry(store, sends, final):
    spans, rows, enc_width = store.shape
    requests = final.shape[1]
    longest = 2 * max(WIDTHS)
    locs = jnp.stack([jnp.pad(t.reshape(-1), (0, longest - t.size)) for t in sends])
    item = (PART, enc_width)
    bufs = [pltpu.VMEM((2 * w, *item), store.dtype) for _ in range(CHUNKS) for w in WIDTHS]
    copies = 2 * len(bufs) + CHUNKS
    return pl.pallas_call(
        functools.partial(carry_kernel, requests),
        out_shape=jax.ShapeDtypeStruct((2 * CHUNKS, requests, *item), store.dtype),
        in_specs=[pl.BlockSpec(memory_space=pltpu.SMEM)] * 2 + [pl.BlockSpec(memory_space=pl.ANY)],
        out_specs=pl.BlockSpec(memory_space=pltpu.VMEM),
        scratch_shapes=[pltpu.VMEM((2 * spans, rows // 2, enc_width), store.dtype)]
        + bufs * 2
        + [
            pltpu.VMEM((CHUNKS, requests, *item), store.dtype),
            pltpu.SemaphoreType.DMA((3,)),
            pltpu.SemaphoreType.DMA((copies,)),
            pltpu.SemaphoreType.DMA((copies,)),
        ],
        compiler_params=pltpu.CompilerParams(
            collective_id=2, has_side_effects=True, vmem_limit_bytes=60 << 20
        ),
        cost_estimate=pl.CostEstimate(flops=0, bytes_accessed=500 << 20, transcendentals=0),
        name="carry",
    )(locs, final, store)


def direct(neighbour_store, neighbour_ids):
    key_count = lax.axis_size("keys")
    shard_spans = neighbour_store.shape[0]
    flat_ids = neighbour_ids.reshape(-1)
    target, offset = flat_ids // shard_spans, flat_ids % shard_spans
    hit = target[:, None] == jnp.arange(key_count, dtype=jnp.int32)[None, :]
    table = jnp.sum(jnp.where(hit, offset[:, None], 0), axis=0)
    incoming = lax.all_to_all(table, "keys", split_axis=0, concat_axis=0, tiled=True)
    firsts, seconds = take(
        [neighbour_store], [[0]] * 2, jnp.stack([incoming, incoming + 1]), neighbour_store.shape[1]
    )
    arrived = [
        lax.all_to_all(spans, "keys", split_axis=0, concat_axis=0, tiled=True)
        for spans in (firsts, seconds)
    ]
    locs = jnp.stack([target, key_count + target])
    return take(arrived, [[0], [1]], locs, neighbour_store.shape[1])


def body(span_queries, key_slab, neighbour_store, neighbour_ids, attn_queries, kv_weight):
    position = lax.axis_index("keys")
    y, z, c = place()
    own_spans = neighbour_ids.shape[0]
    span_rows = neighbour_store.shape[1]
    enc_width = neighbour_store.shape[2]
    all_ids = gather_ids(neighbour_ids)
    asked = jnp.zeros((16, enc_width), span_queries.dtype)
    asked = lax.dynamic_update_slice(asked, span_queries, (0, 0))
    shard = jnp.concatenate([kv_weight[0], kv_weight[1], asked], axis=0)
    groups = [[key_of(a, b, d) for a in range(RING_Y) for b in range(RING_Z)] for d in range(CORES)]
    weight_own = lax.all_gather(shard, "keys", axis=0, axis_index_groups=groups)
    weight_other = lax.ppermute(weight_own, "keys", shifted(0, 0, 1))
    sends, final, stuck = routes(all_ids)
    flag = jnp.full((8, 128), stuck, jnp.int32)
    seq = lax.axis_size("seq")
    worst = flag
    for d in range(1, seq):
        worst = jnp.maximum(
            worst, lax.ppermute(flag, "seq", [(s, (s + d) % seq) for s in range(seq)])
        )
    pieces = carry(neighbour_store, sends, final)

    def resend(store, ids, fast):
        return jnp.stack(
            [
                spans[:, h * PART : (h + 1) * PART]
                for spans in direct(store, ids)
                for h in range(span_rows // PART)
            ]
        )

    pieces = lax.cond(
        worst[0, 0] > 0, resend, lambda store, ids, fast: fast, neighbour_store, neighbour_ids, pieces
    )
    asked_rows = [
        w[:, -16:, : span_queries.shape[1]].reshape(-1, span_queries.shape[1])
        for w in (weight_own, weight_other)
    ]
    best = best_two(key_slab, *asked_rows)
    column = c * asked_rows[0].shape[0] + (position // CORES) * 16
    best_scores = lax.dynamic_slice_in_dim(best, column, own_spans, axis=1)[:2].T
    attended = attend(pieces, weight_own, weight_other, attn_queries)
    return (best_scores, attended)


def solution(mesh):
    return jax.shard_map(
        body,
        mesh=mesh,
        in_specs=(
            P(("keys", "seq"), None),
            P("keys", None),
            P("keys", None, None),
            P(("keys", "seq"), None),
            P(("keys", "seq"), None),
            P(None, "keys", None),
        ),
        out_specs=(P(("keys", "seq"), None), P(("keys", "seq"), None)),
        check_vma=False,
    )
```

```python
import functools

import jax
import jax.numpy as jnp
import numpy as np
from jax import lax
from jax.experimental import pallas as pl
from jax.experimental.pallas import tpu as pltpu
from jax.sharding import PartitionSpec as P

HEADS = 16
HEAD_DIM = 128
RING_Y, RING_Z, CORES = 4, 8, 2
Y_CAPS = (24, 17)
Z_CAPS = (12, 12, 11, 10)


def key_of(y, z, c):
    return (y * RING_Z + z) * CORES + c


def place():
    k = lax.axis_index("keys")
    return k // (RING_Z * CORES), (k // CORES) % RING_Z, k % CORES


def shifted(dy, dz, dc):
    pairs = []
    for y in range(RING_Y):
        for z in range(RING_Z):
            for c in range(CORES):
                to = key_of((y + dy) % RING_Y, (z + dz) % RING_Z, (c + dc) % CORES)
                pairs.append((key_of(y, z, c), to))
    return pairs


def greet(peers):
    barrier = pltpu.get_barrier_semaphore()
    for peer in peers:
        pl.semaphore_signal(
            barrier, inc=1, device_id={"keys": peer}, device_id_type=pl.DeviceIdType.MESH
        )
    pl.semaphore_wait(barrier, len(peers))


def peer_groups():
    y, z, c = place()
    core = [key_of(y, z, 1 - c)]
    depth = [key_of(y, (z + d) % RING_Z, c) for d in range(1, RING_Z)]
    row = [key_of((y + d) % RING_Y, z, c) for d in range(1, RING_Y)]
    return core, depth, row


def send(src, dst, send_sem, recv_sem, peer):
    copy = pltpu.make_async_remote_copy(
        src_ref=src,
        dst_ref=dst,
        send_sem=send_sem,
        recv_sem=recv_sem,
        device_id={"keys": peer},
        device_id_type=pl.DeviceIdType.MESH,
    )
    copy.start()
    return copy


def gather_ids_kernel(ids_ref, out_ref, held, send_sem, recv_sem):
    y, z, c = place()
    core, depth, row = peer_groups()
    greet(core + depth + row)
    held[y, z, c] = ids_ref[...]
    copies = [send(held.at[y, z, c], held.at[y, z, c], send_sem.at[0], recv_sem.at[0], core[0])]
    for copy in copies:
        copy.wait()
    copies = []
    for i, peer in enumerate(depth):
        copies.append(
            send(held.at[y, z], held.at[y, z], send_sem.at[1 + i], recv_sem.at[1 + i], peer)
        )
    for copy in copies:
        copy.wait()
    copies = []
    for i, peer in enumerate(row):
        copies.append(send(held.at[y], held.at[y], send_sem.at[8 + i], recv_sem.at[8 + i], peer))
    for copy in copies:
        copy.wait()
    out_ref[...] = held[...]


def gather_ids(ids):
    tile = jnp.zeros((8, 128), jnp.int32).at[0, : ids.size].set(ids.reshape(-1))
    shape = (RING_Y, RING_Z, CORES, 8, 128)
    held = pl.pallas_call(
        gather_ids_kernel,
        out_shape=jax.ShapeDtypeStruct(shape, jnp.int32),
        in_specs=[pl.BlockSpec(memory_space=pltpu.VMEM)],
        out_specs=pl.BlockSpec(memory_space=pltpu.VMEM),
        scratch_shapes=[
            pltpu.VMEM(shape, jnp.int32),
            pltpu.SemaphoreType.DMA((11,)),
            pltpu.SemaphoreType.DMA((11,)),
        ],
        compiler_params=pltpu.CompilerParams(collective_id=0, has_side_effects=True),
        name="gather_ids",
    )(tile)
    return held[..., 0, : ids.size].reshape(-1)


def merge(a, b):
    high = jnp.maximum(a[0:1], b[0:1])
    low = jnp.maximum(jnp.minimum(a[0:1], b[0:1]), jnp.maximum(a[1:2], b[1:2]))
    return jnp.concatenate([high, low, jnp.zeros((6, high.shape[1]), high.dtype)], axis=0)


def take_kernel(counts, reach, row, locs_ref, *refs):
    sources = refs[: len(counts)]
    outs = refs[len(counts) : -1]
    sems = refs[-1]
    starts = np.concatenate([[0], np.cumsum(counts)]).tolist()
    width, rows = outs[0].shape[0], outs[0].shape[1]

    def piece(k, at):
        if sources[k].shape[1] == rows:
            return sources[k].at[at]
        return sources[k].at[at, pl.ds(pl.multiple_of(row(), rows), rows)]

    def begin(s, carry):
        for d, out in enumerate(outs):
            at = locs_ref[d, s]
            for k in reach[d]:

                @pl.when((at >= starts[k]) & (at < starts[k + 1]))
                def _():
                    pltpu.make_async_copy(
                        piece(k, at - starts[k]), out.at[s], sems.at[d, s]
                    ).start()

        return carry

    lax.fori_loop(0, width, begin, 0)

    def finish(s, carry):
        for d, out in enumerate(outs):
            pltpu.make_async_copy(piece(reach[d][0], 0), out.at[s], sems.at[d, s]).wait()
        return carry

    lax.fori_loop(0, width, finish, 0)


def take(sources, reach, locs, rows, row=None):
    counts = tuple(s.shape[0] for s in sources)
    width = locs.shape[1]
    item = (rows, sources[0].shape[2])
    nbytes = 4 * width * item[0] * item[1] * 2
    return pl.pallas_call(
        functools.partial(take_kernel, counts, reach, row),
        out_shape=[jax.ShapeDtypeStruct((width, *item), sources[0].dtype)] * 2,
        in_specs=[pl.BlockSpec(memory_space=pltpu.SMEM)]
        + [pl.BlockSpec(memory_space=pl.ANY)] * len(sources),
        out_specs=[pl.BlockSpec(memory_space=pltpu.VMEM)] * 2,
        scratch_shapes=[pltpu.SemaphoreType.DMA((2, width))],
        cost_estimate=pl.CostEstimate(flops=0, bytes_accessed=nbytes, transcendentals=0),
        compiler_params=pltpu.CompilerParams(vmem_limit_bytes=32 << 20),
        name="take_spans",
    )(locs, *sources)


def top_two(scores):
    top = jnp.max(scores, axis=0, keepdims=True)
    at_top = scores == top
    ties = jnp.sum(jnp.where(at_top, 1.0, 0.0), axis=0, keepdims=True)
    rest = jnp.max(jnp.where(at_top, -jnp.inf, scores), axis=0, keepdims=True)
    second = jnp.where(ties > 1.5, top, rest)
    return jnp.concatenate([top, second, jnp.zeros((6, top.shape[1]), top.dtype)], axis=0)


SWAP, SLAB, DEPTH, ROW = 0, 8, 9, 16


def attend_kernel(
    pieces,
    w_own,
    w_all,
    slab,
    q_ref,
    o_ref,
    best_ref,
    x,
    wk,
    wv,
    keys,
    values,
    w_other,
    other_slab,
    asked,
    found,
    after_depth,
    landed,
    asked_sem,
    send_sem,
    recv_sem,
):
    c = place()[2]
    g = pl.program_id(0)
    parts, requests, part, width = pieces.shape
    spans = requests // 2
    near = 2 * part * parts
    rows = q_ref.shape[0] // spans
    pairs = w_own.shape[0]
    steps = w_all.shape[0] // pairs
    core, depth, row = peer_groups()
    contract = (((1,), (1,)), ((), ()))
    dot = functools.partial(lax.dot_general, preferred_element_type=jnp.float32)

    def flight(src, dst, k, peer):
        return pltpu.make_async_remote_copy(
            src_ref=src,
            dst_ref=dst,
            send_sem=send_sem.at[k],
            recv_sem=recv_sem.at[k],
            device_id={"keys": peer},
            device_id_type=pl.DeviceIdType.MESH,
        )

    def weights_flight(b):
        at = pl.ds(b * pairs, pairs)
        return flight(w_all.at[at, pl.ds(0, 64)], w_other.at[at], SWAP + b, core[0])

    slab_flight = lambda: flight(slab, other_slab, SLAB, core[0])
    asked_copy = lambda: pltpu.make_async_copy(w_all.at[:, pl.ds(64, 16)], asked, asked_sem)
    depth_flights = lambda: [
        flight(found, landed.at[i], DEPTH + i, peer) for i, peer in enumerate(depth)
    ]
    row_flights = lambda: [
        flight(after_depth, landed.at[len(depth) + i], ROW + i, peer) for i, peer in enumerate(row)
    ]

    @pl.when(g == 0)
    def _():
        greet(core + depth + row)
        for b in range(steps):
            weights_flight(b).start()
        slab_flight().start()
        asked_copy().start()
        for u in range(spans):
            for i in range(parts):
                at = (u * parts + i) * 2 * part
                x[at : at + 2 * part, :] = pieces[i, 2 * u : 2 * u + 2].reshape(2 * part, width)

    weights_flight(g).wait_recv()
    for kind, w in enumerate((wk, wv)):
        for j in range(pairs):
            mine = pl.multiple_of(j * 64 + c * 32, 32)
            theirs = pl.multiple_of(j * 64 + (1 - c) * 32, 32)
            w[pl.ds(mine, 32), :] = w_own[j, kind * 32 : kind * 32 + 32, :]
            w[pl.ds(theirs, 32), :] = w_other[g * pairs + j, kind * 32 : kind * 32 + 32, :]
    keys[...] = dot(x[...], wk[...], contract).astype(jnp.bfloat16)
    values[...] = dot(x[...], wv[...], contract).astype(jnp.bfloat16)
    zero = jnp.zeros((rows, HEAD_DIM), jnp.bfloat16)

    def both_heads(u):
        q = q_ref[u * rows : (u + 1) * rows, :]
        return jnp.concatenate(
            [
                jnp.concatenate([q[:, :HEAD_DIM], zero], axis=1),
                jnp.concatenate([zero, q[:, HEAD_DIM:]], axis=1),
            ],
            axis=0,
        )

    def softmax(logits):
        scaled = logits * HEAD_DIM ** (-0.5)
        largest = jnp.max(scaled, axis=-1, keepdims=True)
        terms = jnp.exp(scaled - largest)
        total = jnp.sum(terms, axis=-1, keepdims=True)
        return (terms * (1.0 / total)).astype(jnp.bfloat16)

    logits = [dot(both_heads(u), keys[u * near : (u + 1) * near, :], contract) for u in range(spans)]
    weights = [softmax(part_logits) for part_logits in logits]
    outs = [
        dot(weights[u], values[u * near : (u + 1) * near, :], (((1,), (0,)), ((), ())))
        for u in range(spans)
    ]
    for u, out in enumerate(outs):
        tokens = slice(u * rows, (u + 1) * rows)
        o_ref[tokens, :HEAD_DIM] = out[:rows, :HEAD_DIM].astype(jnp.bfloat16)
        o_ref[tokens, HEAD_DIM:] = out[rows:, HEAD_DIM:].astype(jnp.bfloat16)

    @pl.when(g == 1)
    def _():
        slab_flight().wait_recv()
        asked_copy().wait()
        queries = asked[:, :, : slab.shape[1]].reshape(found.shape[1], slab.shape[1])
        found[...] = merge(
            top_two(dot(slab[...], queries, contract)), top_two(dot(other_slab[...], queries, contract))
        )
        for copy in depth_flights():
            copy.start()

    @pl.when(g == 3)
    def _():
        for copy in depth_flights():
            copy.wait_recv()
        total = found[...]
        for i in range(len(depth)):
            total = merge(total, landed[i])
        after_depth[...] = total
        for copy in row_flights():
            copy.start()

    @pl.when(g == 5)
    def _():
        for copy in row_flights():
            copy.wait_recv()
        total = after_depth[...]
        for i in range(len(row)):
            total = merge(total, landed[len(depth) + i])
        best_ref[...] = total

    @pl.when(g == steps - 1)
    def _():
        for b in range(steps):
            weights_flight(b).wait_send()
        for copy in [slab_flight()] + depth_flights() + row_flights():
            copy.wait_send()


def attend(pieces, w_own, slab, queries):
    parts, requests, part, width = pieces.shape
    near = requests * parts * part
    tokens, columns = queries.shape
    steps = 8
    pairs = w_own.shape[0] // steps
    cols = columns // steps
    asked = w_own.shape[0] * 16
    block = pl.BlockSpec((tokens, cols), lambda g: (0, g))
    flops = 2 * near * width * 2 * columns
    bf16 = jnp.bfloat16
    return pl.pallas_call(
        attend_kernel,
        grid=(steps,),
        out_shape=[
            jax.ShapeDtypeStruct((tokens, columns), bf16),
            jax.ShapeDtypeStruct((8, asked), jnp.float32),
        ],
        in_specs=[
            pl.BlockSpec(pieces.shape, lambda g: (0, 0, 0, 0)),
            pl.BlockSpec((pairs, w_own.shape[1], width), lambda g: (g, 0, 0)),
            pl.BlockSpec(memory_space=pl.ANY),
            pl.BlockSpec(slab.shape, lambda g: (0, 0)),
            block,
        ],
        out_specs=[block, pl.BlockSpec((8, asked), lambda g: (0, 0))],
        scratch_shapes=[
            pltpu.VMEM((near, width), bf16),
            pltpu.VMEM((cols, width), bf16),
            pltpu.VMEM((cols, width), bf16),
            pltpu.VMEM((near, cols), bf16),
            pltpu.VMEM((near, cols), bf16),
            pltpu.VMEM((w_own.shape[0], 64, width), bf16),
            pltpu.VMEM(slab.shape, bf16),
            pltpu.VMEM((w_own.shape[0], 16, width), bf16),
            pltpu.VMEM((8, asked), jnp.float32),
            pltpu.VMEM((8, asked), jnp.float32),
            pltpu.VMEM((10, 8, asked), jnp.float32),
            pltpu.SemaphoreType.DMA,
            pltpu.SemaphoreType.DMA((19,)),
            pltpu.SemaphoreType.DMA((19,)),
        ],
        compiler_params=pltpu.CompilerParams(
            collective_id=1, has_side_effects=True, vmem_limit_bytes=48 << 20
        ),
        cost_estimate=pl.CostEstimate(
            flops=flops, bytes_accessed=20 << 20, transcendentals=tokens * HEADS * 256
        ),
        name="attend",
    )(pieces, w_own, w_own, slab, queries)


def routes(all_ids):
    requests = all_ids.shape[0]
    per_device = requests // (RING_Y * RING_Z * CORES)
    index = np.arange(requests)
    k, n = index // per_device, index % per_device
    to_y, to_z = k // (RING_Z * CORES), (k // CORES) % RING_Z
    tie_y = jnp.asarray((n // 2 + k) % 2 == 1)
    tie_z = jnp.asarray((n + k) % 2 == 1)
    order = jnp.asarray(index, jnp.int32)
    to_y, to_z = jnp.asarray(to_y, jnp.int32), jnp.asarray(to_z, jnp.int32)
    y, z, c = place()
    shard, offset = all_ids // 64, all_ids % 64
    from_y, from_z, from_c = shard // (RING_Z * CORES), (shard // CORES) % RING_Z, shard % CORES
    loc = jnp.where(from_c == c, 0, 64) + offset
    base = 128
    sends = []

    def travel(position, target, ring, tie, node_of, mine, caps, loc, base):
        ahead = (target - position) % ring
        back = (ahead > ring // 2) | ((ahead == ring // 2) & tie)
        left = jnp.where(back, (ring - ahead) % ring, ahead)
        step = jnp.where(back, ring - 1, 1)
        way = back.astype(jnp.int32)
        for width in caps:
            node = node_of(position) * 2 + way
            moving = left > 0
            seat = jnp.where(moving, node, -1)
            priority = (16 - left) * 1024 + order
            before = (seat[:, None] == seat[None, :]) & (priority[:, None] < priority[None, :])
            rank = jnp.sum(before.astype(jnp.int32), axis=0)
            goes = moving & (rank < width)
            seat_rank = jnp.where(goes, node * 64 + rank, -1)
            wanted = (mine * 2 + np.arange(2, dtype=np.int32))[:, None] * 64 + np.arange(
                width, dtype=np.int32
            )
            hit = seat_rank[None, None, :] == wanted[:, :, None]
            sends.append(jnp.sum(jnp.where(hit, loc[None, None, :], 0), axis=-1))
            loc = jnp.where(goes, base + way * width + rank, loc)
            base += 2 * width
            position = jnp.where(goes, (position + step) % ring, position)
            left = left - goes.astype(jnp.int32)
        return jnp.max(left), loc, base

    stuck_y, loc, base = travel(
        from_y, to_y, RING_Y, tie_y, lambda p: p * RING_Z + from_z, y * RING_Z + z, Y_CAPS, loc, base
    )
    stuck_z, loc, base = travel(
        from_z, to_z, RING_Z, tie_z, lambda p: to_y * RING_Z + p, y * RING_Z + z, Z_CAPS, loc, base
    )
    table = loc.reshape(RING_Y * RING_Z, CORES, per_device)
    here = lax.dynamic_index_in_dim(table, y * RING_Z + z, 0, False)
    own = lax.dynamic_index_in_dim(here, c, 0, False)
    other = lax.dynamic_index_in_dim(here, 1 - c, 0, False)
    return sends, jnp.stack([own, other]), jnp.maximum(stuck_y, stuck_z)


def issue_order(moves, widths, chunks):
    done = {(j, -1): 0.0 for j in range(chunks)}
    issued, order, free, clock = set(), [], {True: 0.0, False: 0.0}, 0.0
    while len(order) < chunks * len(moves):
        ready = []
        for j in range(chunks):
            r = sum((j, q) in issued for q in range(len(moves)))
            if r == len(moves) or (j, r - 1) not in done:
                continue
            if r == 0 and j >= 2 and (j - 2, len(Y_CAPS) - 1) not in issued:
                continue
            ready.append((max(clock, done[j, r - 1] + 2.5 * (r > 0)), j, r))
        at, j, r = min(ready)
        along_y = moves[r][0] != 0
        clock = at + 0.5
        free[along_y] = max(free[along_y], clock) + 0.65 * widths[r]
        done[j, r] = free[along_y]
        issued.add((j, r))
        order.append((j, r))
    return order


MOVES = [(1, 0)] * len(Y_CAPS) + [(0, 1)] * len(Z_CAPS)
WIDTHS = Y_CAPS + Z_CAPS
CHUNKS = 4
PART = 16


def carry_kernel(requests, locs_ref, final_ref, store_ref, out_ref, held, *rest):
    rounds = len(MOVES)
    total = CHUNKS * rounds
    out_bufs = rest[:total]
    in_bufs = rest[total : 2 * total]
    last, swap_sems, send_sems, recv_sems = rest[2 * total :]
    y, z, c = place()
    half = held.shape[1]
    spans = store_ref.shape[0]
    steps = [((y + dy) % RING_Y, (z + dz) % RING_Z) for dy, dz in ((1, 0), (-1, 0), (0, 1), (0, -1))]
    near = [key_of(a + 0, b + 0, c) for a, b in steps]
    buddy = key_of(y, z, 1 - c)
    greet(near + [buddy])
    mine = pl.ds(pl.multiple_of(c * half, half), half)
    theirs = pl.ds(pl.multiple_of((1 - c) * half, half), half)
    swap = send(
        store_ref.at[:, theirs], held.at[pl.ds(spans, spans)], swap_sems.at[0], swap_sems.at[1], buddy
    )
    keep = pltpu.make_async_copy(store_ref.at[:, mine], held.at[pl.ds(0, spans)], swap_sems.at[2])
    keep.start()
    swap.wait()
    keep.wait()
    bases = np.concatenate([[2 * spans], 2 * spans + np.cumsum(2 * np.array(WIDTHS))]).tolist()

    def picked(j, r, at):
        step, part = j // 2, j % 2
        rows = slice(part * PART, (part + 1) * PART)
        here = jnp.where(at < 2 * spans, at + step, 0)
        value = held[here, rows, :]
        for q in range(r):
            count = 2 * WIDTHS[q]
            inside = (at >= bases[q]) & (at < bases[q] + count)
            value = jnp.where(inside, in_bufs[j * rounds + q][jnp.where(inside, at - bases[q], 0)], value)
        return value

    flights = {}

    def land(j, r):
        for flight in flights[j, r]:
            flight.wait_recv()

    def issue(j, r):
        if r > 0:
            land(j, r - 1)
        width = WIDTHS[r]
        buf = out_bufs[j * rounds + r]

        def fill(s, carry):
            buf[s] = picked(j, r, locs_ref[r, s])
            return carry

        lax.fori_loop(0, 2 * width, fill, 0)
        flights[j, r] = []
        for d in range(2):
            part = pl.ds(d * width, width)
            k = (j * rounds + r) * 2 + d
            peer = near[d if MOVES[r][0] else 2 + d]
            flights[j, r].append(
                send(buf.at[part], in_bufs[j * rounds + r].at[part], send_sems.at[k], recv_sems.at[k], peer)
            )

    def finish(j):
        land(j, rounds - 1)

        def fill(s, carry):
            out_ref[2 * j, s] = picked(j, rounds, final_ref[0, s])
            last[j, s] = picked(j, rounds, final_ref[1, s])
            return carry

        lax.fori_loop(0, requests, fill, 0)
        k = 2 * total + j
        flights[j, rounds] = [
            send(last.at[j], out_ref.at[2 * j + 1], send_sems.at[k], recv_sems.at[k], buddy)
        ]

    waiting = []
    for j, r in issue_order(MOVES, WIDTHS, CHUNKS):
        issue(j, r)
        if r == rounds - 1:
            waiting.append(j)
        elif waiting:
            finish(waiting.pop(0))
    for j in waiting:
        finish(j)
    for j in range(CHUNKS):
        land(j, rounds)
    for copies in flights.values():
        for copy in copies:
            copy.wait_send()


def carry(store, sends, final):
    spans, rows, enc_width = store.shape
    requests = final.shape[1]
    longest = 2 * max(WIDTHS)
    locs = jnp.stack([jnp.pad(t.reshape(-1), (0, longest - t.size)) for t in sends])
    item = (PART, enc_width)
    bufs = [pltpu.VMEM((2 * w, *item), store.dtype) for _ in range(CHUNKS) for w in WIDTHS]
    copies = 2 * len(bufs) + CHUNKS
    return pl.pallas_call(
        functools.partial(carry_kernel, requests),
        out_shape=jax.ShapeDtypeStruct((2 * CHUNKS, requests, *item), store.dtype),
        in_specs=[pl.BlockSpec(memory_space=pltpu.SMEM)] * 2 + [pl.BlockSpec(memory_space=pl.ANY)],
        out_specs=pl.BlockSpec(memory_space=pltpu.VMEM),
        scratch_shapes=[pltpu.VMEM((2 * spans, rows // 2, enc_width), store.dtype)]
        + bufs * 2
        + [
            pltpu.VMEM((CHUNKS, requests, *item), store.dtype),
            pltpu.SemaphoreType.DMA((3,)),
            pltpu.SemaphoreType.DMA((copies,)),
            pltpu.SemaphoreType.DMA((copies,)),
        ],
        compiler_params=pltpu.CompilerParams(
            collective_id=2, has_side_effects=True, vmem_limit_bytes=60 << 20
        ),
        cost_estimate=pl.CostEstimate(flops=0, bytes_accessed=500 << 20, transcendentals=0),
        name="carry",
    )(locs, final, store)


def direct(neighbour_store, neighbour_ids):
    key_count = lax.axis_size("keys")
    shard_spans = neighbour_store.shape[0]
    flat_ids = neighbour_ids.reshape(-1)
    target, offset = flat_ids // shard_spans, flat_ids % shard_spans
    hit = target[:, None] == jnp.arange(key_count, dtype=jnp.int32)[None, :]
    table = jnp.sum(jnp.where(hit, offset[:, None], 0), axis=0)
    incoming = lax.all_to_all(table, "keys", split_axis=0, concat_axis=0, tiled=True)
    firsts, seconds = take(
        [neighbour_store], [[0]] * 2, jnp.stack([incoming, incoming + 1]), neighbour_store.shape[1]
    )
    arrived = [
        lax.all_to_all(spans, "keys", split_axis=0, concat_axis=0, tiled=True)
        for spans in (firsts, seconds)
    ]
    locs = jnp.stack([target, key_count + target])
    return take(arrived, [[0], [1]], locs, neighbour_store.shape[1])


def body(span_queries, key_slab, neighbour_store, neighbour_ids, attn_queries, kv_weight):
    position = lax.axis_index("keys")
    y, z, c = place()
    own_spans = neighbour_ids.shape[0]
    span_rows = neighbour_store.shape[1]
    enc_width = neighbour_store.shape[2]
    all_ids = gather_ids(neighbour_ids)
    asked = jnp.zeros((16, enc_width), span_queries.dtype)
    asked = lax.dynamic_update_slice(asked, span_queries, (0, 0))
    shard = jnp.concatenate([kv_weight[0], kv_weight[1], asked], axis=0)
    groups = [[key_of(a, b, d) for a in range(RING_Y) for b in range(RING_Z)] for d in range(CORES)]
    weight_own = lax.all_gather(shard, "keys", axis=0, axis_index_groups=groups)
    sends, final, stuck = routes(all_ids)
    flag = jnp.full((8, 128), stuck, jnp.int32)
    seq = lax.axis_size("seq")
    worst = flag
    for d in range(1, seq):
        worst = jnp.maximum(
            worst, lax.ppermute(flag, "seq", [(s, (s + d) % seq) for s in range(seq)])
        )
    pieces = carry(neighbour_store, sends, final)

    def resend(store, ids, fast):
        return jnp.stack(
            [
                spans[:, h * PART : (h + 1) * PART]
                for spans in direct(store, ids)
                for h in range(span_rows // PART)
            ]
        )

    pieces = lax.cond(
        worst[0, 0] > 0, resend, lambda store, ids, fast: fast, neighbour_store, neighbour_ids, pieces
    )
    attended, best = attend(pieces, weight_own, key_slab, attn_queries)
    column = (position // CORES) * 16
    best_scores = lax.dynamic_slice_in_dim(best, column, own_spans, axis=1)[:2].T
    return (best_scores, attended)


def solution(mesh):
    return jax.shard_map(
        body,
        mesh=mesh,
        in_specs=(
            P(("keys", "seq"), None),
            P("keys", None),
            P("keys", None, None),
            P(("keys", "seq"), None),
            P(("keys", "seq"), None),
            P(None, "keys", None),
        ),
        out_specs=(P(("keys", "seq"), None), P(("keys", "seq"), None)),
        check_vma=False,
    )
```

```python
import functools

import jax
import jax.numpy as jnp
import numpy as np
from jax import lax
from jax.experimental import pallas as pl
from jax.experimental.pallas import tpu as pltpu
from jax.sharding import PartitionSpec as P

HEADS = 16
HEAD_DIM = 128
RING_Y, RING_Z, CORES = 4, 8, 2
Y_CAPS = (24, 17)
Z_CAPS = (12, 12, 11, 10)


def key_of(y, z, c):
    return (y * RING_Z + z) * CORES + c


def place():
    k = lax.axis_index("keys")
    return k // (RING_Z * CORES), (k // CORES) % RING_Z, k % CORES


def shifted(dy, dz, dc):
    pairs = []
    for y in range(RING_Y):
        for z in range(RING_Z):
            for c in range(CORES):
                to = key_of((y + dy) % RING_Y, (z + dz) % RING_Z, (c + dc) % CORES)
                pairs.append((key_of(y, z, c), to))
    return pairs


def greet(peers, seq_peers=()):
    barrier = pltpu.get_barrier_semaphore()
    for axis, peer in [("keys", p) for p in peers] + [("seq", p) for p in seq_peers]:
        pl.semaphore_signal(
            barrier, inc=1, device_id={axis: peer}, device_id_type=pl.DeviceIdType.MESH
        )
    pl.semaphore_wait(barrier, len(peers) + len(seq_peers))


def peer_groups():
    y, z, c = place()
    core = [key_of(y, z, 1 - c)]
    depth = [key_of(y, (z + d) % RING_Z, c) for d in range(1, RING_Z)]
    row = [key_of((y + d) % RING_Y, z, c) for d in range(1, RING_Y)]
    return core, depth, row


def send(src, dst, send_sem, recv_sem, peer, axis="keys"):
    copy = pltpu.make_async_remote_copy(
        src_ref=src,
        dst_ref=dst,
        send_sem=send_sem,
        recv_sem=recv_sem,
        device_id={axis: peer},
        device_id_type=pl.DeviceIdType.MESH,
    )
    copy.start()
    return copy


def gather_ids_kernel(ids_ref, out_ref, held, send_sem, recv_sem):
    y, z, c = place()
    core, depth, row = peer_groups()
    greet(core + depth + row)
    held[y, z, c] = ids_ref[...]
    copies = [send(held.at[y, z, c], held.at[y, z, c], send_sem.at[0], recv_sem.at[0], core[0])]
    for copy in copies:
        copy.wait()
    copies = []
    for i, peer in enumerate(depth):
        copies.append(
            send(held.at[y, z], held.at[y, z], send_sem.at[1 + i], recv_sem.at[1 + i], peer)
        )
    for copy in copies:
        copy.wait()
    copies = []
    for i, peer in enumerate(row):
        copies.append(send(held.at[y], held.at[y], send_sem.at[8 + i], recv_sem.at[8 + i], peer))
    for copy in copies:
        copy.wait()
    out_ref[...] = held[...]


def gather_ids(ids):
    tile = jnp.pad(ids.reshape(1, -1), ((0, 7), (0, 128 - ids.size)))
    shape = (RING_Y, RING_Z, CORES, 8, 128)
    held = pl.pallas_call(
        gather_ids_kernel,
        out_shape=jax.ShapeDtypeStruct(shape, jnp.int32),
        in_specs=[pl.BlockSpec(memory_space=pltpu.VMEM)],
        out_specs=pl.BlockSpec(memory_space=pltpu.VMEM),
        scratch_shapes=[
            pltpu.VMEM(shape, jnp.int32),
            pltpu.SemaphoreType.DMA((11,)),
            pltpu.SemaphoreType.DMA((11,)),
        ],
        compiler_params=pltpu.CompilerParams(collective_id=0, has_side_effects=True),
        name="gather_ids",
    )(tile)
    return held[..., 0, : ids.size].reshape(1, -1)


def merge(a, b):
    high = jnp.maximum(a[0:1], b[0:1])
    low = jnp.maximum(jnp.minimum(a[0:1], b[0:1]), jnp.maximum(a[1:2], b[1:2]))
    return jnp.concatenate([high, low, jnp.zeros((6, high.shape[1]), high.dtype)], axis=0)


def take_kernel(counts, reach, row, locs_ref, *refs):
    sources = refs[: len(counts)]
    outs = refs[len(counts) : -1]
    sems = refs[-1]
    starts = np.concatenate([[0], np.cumsum(counts)]).tolist()
    width, rows = outs[0].shape[0], outs[0].shape[1]

    def piece(k, at):
        if sources[k].shape[1] == rows:
            return sources[k].at[at]
        return sources[k].at[at, pl.ds(pl.multiple_of(row(), rows), rows)]

    def begin(s, carry):
        for d, out in enumerate(outs):
            at = locs_ref[d, s]
            for k in reach[d]:

                @pl.when((at >= starts[k]) & (at < starts[k + 1]))
                def _():
                    pltpu.make_async_copy(
                        piece(k, at - starts[k]), out.at[s], sems.at[d, s]
                    ).start()

        return carry

    lax.fori_loop(0, width, begin, 0)

    def finish(s, carry):
        for d, out in enumerate(outs):
            pltpu.make_async_copy(piece(reach[d][0], 0), out.at[s], sems.at[d, s]).wait()
        return carry

    lax.fori_loop(0, width, finish, 0)


def take(sources, reach, locs, rows, row=None):
    counts = tuple(s.shape[0] for s in sources)
    width = locs.shape[1]
    item = (rows, sources[0].shape[2])
    nbytes = 4 * width * item[0] * item[1] * 2
    return pl.pallas_call(
        functools.partial(take_kernel, counts, reach, row),
        out_shape=[jax.ShapeDtypeStruct((width, *item), sources[0].dtype)] * 2,
        in_specs=[pl.BlockSpec(memory_space=pltpu.SMEM)]
        + [pl.BlockSpec(memory_space=pl.ANY)] * len(sources),
        out_specs=[pl.BlockSpec(memory_space=pltpu.VMEM)] * 2,
        scratch_shapes=[pltpu.SemaphoreType.DMA((2, width))],
        cost_estimate=pl.CostEstimate(flops=0, bytes_accessed=nbytes, transcendentals=0),
        compiler_params=pltpu.CompilerParams(vmem_limit_bytes=32 << 20),
        name="take_spans",
    )(locs, *sources)


def top_two(scores):
    top = jnp.max(scores, axis=0, keepdims=True)
    at_top = scores == top
    ties = jnp.sum(jnp.where(at_top, 1.0, 0.0), axis=0, keepdims=True)
    rest = jnp.max(jnp.where(at_top, -jnp.inf, scores), axis=0, keepdims=True)
    second = jnp.where(ties > 1.5, top, rest)
    return jnp.concatenate([top, second, jnp.zeros((6, top.shape[1]), top.dtype)], axis=0)


SWAP, SLAB, DEPTH, ROW = 0, 8, 9, 16


def attend_kernel(
    pieces,
    w_own,
    w_all,
    slab,
    asked,
    q_ref,
    o_ref,
    best_ref,
    x,
    wk,
    wv,
    keys,
    values,
    w_other,
    other_slab,
    found,
    after_depth,
    landed,
    send_sem,
    recv_sem,
):
    c = place()[2]
    g = pl.program_id(0)
    parts, requests, part, width = pieces.shape
    spans = requests // 2
    near = 2 * part * parts
    rows = q_ref.shape[0] // spans
    pairs = w_own.shape[1]
    steps = w_all.shape[1] // pairs
    core, depth, row = peer_groups()
    contract = (((1,), (1,)), ((), ()))
    dot = functools.partial(lax.dot_general, preferred_element_type=jnp.float32)

    def flight(src, dst, k, peer):
        return pltpu.make_async_remote_copy(
            src_ref=src,
            dst_ref=dst,
            send_sem=send_sem.at[k],
            recv_sem=recv_sem.at[k],
            device_id={"keys": peer},
            device_id_type=pl.DeviceIdType.MESH,
        )

    def weights_flight(b):
        at = pl.ds(b * pairs, pairs)
        return flight(w_all.at[:, at], w_other.at[:, at], SWAP + b, core[0])

    slab_flight = lambda: flight(slab, other_slab, SLAB, core[0])
    depth_flights = lambda: [
        flight(found, landed.at[i], DEPTH + i, peer) for i, peer in enumerate(depth)
    ]
    row_flights = lambda: [
        flight(after_depth, landed.at[len(depth) + i], ROW + i, peer) for i, peer in enumerate(row)
    ]

    @pl.when(g == 0)
    def _():
        greet(core + depth + row)
        for b in range(steps):
            weights_flight(b).start()
        slab_flight().start()
        for u in range(spans):
            for i in range(parts):
                at = (u * parts + i) * 2 * part
                x[at : at + 2 * part, :] = pieces[i, 2 * u : 2 * u + 2].reshape(2 * part, width)

    weights_flight(g).wait_recv()
    for kind, w in enumerate((wk, wv)):
        for j in range(pairs):
            for h in range(2):
                mine = pl.multiple_of(j * 64 + c * 32 + h * PART, PART)
                theirs = pl.multiple_of(j * 64 + (1 - c) * 32 + h * PART, PART)
                w[pl.ds(mine, PART), :] = w_own[kind * 2 + h, j]
                w[pl.ds(theirs, PART), :] = w_other[kind * 2 + h, g * pairs + j]
    keys[...] = dot(x[...], wk[...], contract).astype(jnp.bfloat16)
    values[...] = dot(x[...], wv[...], contract).astype(jnp.bfloat16)
    zero = jnp.zeros((rows, HEAD_DIM), jnp.bfloat16)

    def both_heads(u):
        q = q_ref[u * rows : (u + 1) * rows, :]
        return jnp.concatenate(
            [
                jnp.concatenate([q[:, :HEAD_DIM], zero], axis=1),
                jnp.concatenate([zero, q[:, HEAD_DIM:]], axis=1),
            ],
            axis=0,
        )

    def softmax(logits):
        scaled = logits * HEAD_DIM ** (-0.5)
        largest = jnp.max(scaled, axis=-1, keepdims=True)
        terms = jnp.exp(scaled - largest)
        total = jnp.sum(terms, axis=-1, keepdims=True)
        return (terms * (1.0 / total)).astype(jnp.bfloat16)

    logits = [dot(both_heads(u), keys[u * near : (u + 1) * near, :], contract) for u in range(spans)]
    weights = [softmax(part_logits) for part_logits in logits]
    outs = [
        dot(weights[u], values[u * near : (u + 1) * near, :], (((1,), (0,)), ((), ())))
        for u in range(spans)
    ]
    for u, out in enumerate(outs):
        tokens = slice(u * rows, (u + 1) * rows)
        o_ref[tokens, :HEAD_DIM] = out[:rows, :HEAD_DIM].astype(jnp.bfloat16)
        o_ref[tokens, HEAD_DIM:] = out[rows:, HEAD_DIM:].astype(jnp.bfloat16)

    @pl.when(g == 1)
    def _():
        slab_flight().wait_recv()
        queries = asked[:, c].reshape(found.shape[1], slab.shape[1])
        found[...] = merge(
            top_two(dot(slab[...], queries, contract)), top_two(dot(other_slab[...], queries, contract))
        )
        for copy in depth_flights():
            copy.start()

    @pl.when(g == 3)
    def _():
        for copy in depth_flights():
            copy.wait_recv()
        total = found[...]
        for i in range(len(depth)):
            total = merge(total, landed[i])
        after_depth[...] = total
        for copy in row_flights():
            copy.start()

    @pl.when(g == 5)
    def _():
        for copy in row_flights():
            copy.wait_recv()
        total = after_depth[...]
        for i in range(len(row)):
            total = merge(total, landed[len(depth) + i])
        best_ref[...] = total

    @pl.when(g == steps - 1)
    def _():
        for b in range(steps):
            weights_flight(b).wait_send()
        for copy in [slab_flight()] + depth_flights() + row_flights():
            copy.wait_send()


def attend(pieces, w_own, slab, asked, queries):
    parts, requests, part, width = pieces.shape
    near = requests * parts * part
    tokens, columns = queries.shape
    steps = 8
    pairs = w_own.shape[1] // steps
    cols = columns // steps
    found = asked.shape[0] * asked.shape[2]
    block = pl.BlockSpec((tokens, cols), lambda g: (0, g))
    flops = 2 * near * width * 2 * columns
    bf16 = jnp.bfloat16
    return pl.pallas_call(
        attend_kernel,
        grid=(steps,),
        out_shape=[
            jax.ShapeDtypeStruct((tokens, columns), bf16),
            jax.ShapeDtypeStruct((8, found), jnp.float32),
        ],
        in_specs=[
            pl.BlockSpec(pieces.shape, lambda g: (0, 0, 0, 0)),
            pl.BlockSpec((w_own.shape[0], pairs, part, width), lambda g: (0, g, 0, 0)),
            pl.BlockSpec(memory_space=pl.ANY),
            pl.BlockSpec(slab.shape, lambda g: (0, 0)),
            pl.BlockSpec(asked.shape, lambda g: (0, 0, 0, 0)),
            block,
        ],
        out_specs=[block, pl.BlockSpec((8, found), lambda g: (0, 0))],
        scratch_shapes=[
            pltpu.VMEM((near, width), bf16),
            pltpu.VMEM((cols, width), bf16),
            pltpu.VMEM((cols, width), bf16),
            pltpu.VMEM((near, cols), bf16),
            pltpu.VMEM((near, cols), bf16),
            pltpu.VMEM(w_own.shape, bf16),
            pltpu.VMEM(slab.shape, bf16),
            pltpu.VMEM((8, found), jnp.float32),
            pltpu.VMEM((8, found), jnp.float32),
            pltpu.VMEM((10, 8, found), jnp.float32),
            pltpu.SemaphoreType.DMA((19,)),
            pltpu.SemaphoreType.DMA((19,)),
        ],
        compiler_params=pltpu.CompilerParams(
            collective_id=1, has_side_effects=True, vmem_limit_bytes=48 << 20
        ),
        cost_estimate=pl.CostEstimate(
            flops=flops, bytes_accessed=20 << 20, transcendentals=tokens * HEADS * 256
        ),
        name="attend",
    )(pieces, w_own, w_own, slab, asked, queries)


def routes_kernel(ids_ref, table_ref, before):
    requests = ids_ref.shape[1]
    per_device = requests // (RING_Y * RING_Z * CORES)
    y, z, c = place()
    before[...] = jnp.where(
        lax.broadcasted_iota(jnp.int32, before.shape, 0)
        < lax.broadcasted_iota(jnp.int32, before.shape, 1),
        1.0,
        0.0,
    ).astype(jnp.bfloat16)
    index = lax.broadcasted_iota(jnp.int32, (1, requests), 1)
    k = sum(jnp.where(index >= t * per_device, 1, 0) for t in range(1, requests // per_device))
    n = index - k * per_device
    to_y, to_z = k >> 4, (k >> 1) & 7
    tie_y, tie_z = ((n >> 1) + k) & 1, (n + k) & 1
    ids = ids_ref[...]
    shard, offset = ids >> 6, ids & 63
    from_y, from_z, from_c = shard >> 4, (shard >> 1) & 7, shard & 1
    loc = jnp.where(from_c == c, 0, 64) + offset
    nodes = RING_Y * RING_Z * 2
    node_rows = lax.broadcasted_iota(jnp.int32, (nodes, requests), 0)
    lanes = lax.broadcasted_iota(jnp.int32, table_ref.shape, 1)
    slots = lax.broadcasted_iota(jnp.int32, (table_ref.shape[0], requests), 0)
    table = jnp.zeros(table_ref.shape, jnp.float32)
    here = y * RING_Z + z

    def column(hits, values):
        return jnp.sum(jnp.where(hits, values.astype(jnp.float32), 0.0), axis=1, keepdims=True)

    base = 128
    r = 0
    stuck = jnp.zeros((1, requests), jnp.int32)
    for along_y, caps in ((True, Y_CAPS), (False, Z_CAPS)):
        ring = RING_Y if along_y else RING_Z
        position, target, tie = (from_y, to_y, tie_y) if along_y else (from_z, to_z, tie_z)
        ahead = (target - position) & (ring - 1)
        back = (ahead > ring // 2) | ((ahead == ring // 2) & (tie == 1))
        left = jnp.where(back, (ring - ahead) & (ring - 1), ahead)
        step = jnp.where(back, ring - 1, 1)
        way = jnp.where(back, 1, 0)
        for width in caps:
            chip = position * RING_Z + from_z if along_y else to_y * RING_Z + position
            node = chip * 2 + way
            seat = node_rows == node
            kinds = [
                jnp.where(seat & (left == d), 1.0, 0.0) for d in range(ring // 2, 0, -1)
            ]
            counts = lax.dot_general(
                jnp.concatenate(kinds, axis=0).astype(jnp.bfloat16),
                before[...],
                (((1,), (0,)), ((), ())),
                preferred_element_type=jnp.float32,
            )
            rank = jnp.zeros((1, requests), jnp.float32)
            ahead_of = jnp.zeros((nodes, 1), jnp.float32)
            for i, kind in enumerate(kinds):
                mine = counts[i * nodes : (i + 1) * nodes] + ahead_of
                rank += jnp.sum(kind * mine, axis=0, keepdims=True)
                ahead_of += jnp.sum(kind, axis=1, keepdims=True)
            rank = rank.astype(jnp.int32)
            goes = (left > 0) & (rank < width)
            slot = jnp.where(goes & (chip == here), way * width + rank, -1)
            table = jnp.where(lanes == r, column(slots == slot, loc), table)
            loc = jnp.where(goes, base + way * width + rank, loc)
            base += 2 * width
            position = jnp.where(goes, (position + step) & (ring - 1), position)
            left = left - jnp.where(goes, 1, 0)
            r += 1
        stuck = jnp.maximum(stuck, left)
    for core in (c, 1 - c):
        first = (here * CORES + core) * per_device
        wanted = (index == first + slots) & (slots < per_device)
        table = jnp.where(lanes == r, column(wanted, loc), table)
        r += 1
    worst = jnp.max(stuck.astype(jnp.float32), axis=1, keepdims=True)
    table = jnp.where(lanes == r, worst, table)
    table_ref[...] = table.astype(jnp.int32)


def routes(all_ids):
    requests = all_ids.shape[1]
    return pl.pallas_call(
        routes_kernel,
        out_shape=jax.ShapeDtypeStruct((2 * max(WIDTHS), 128), jnp.int32),
        in_specs=[pl.BlockSpec(memory_space=pltpu.VMEM)],
        out_specs=pl.BlockSpec(memory_space=pltpu.VMEM),
        scratch_shapes=[pltpu.VMEM((requests, requests), jnp.bfloat16)],
        name="routes",
    )(all_ids)


MOVES = [(1, 0)] * len(Y_CAPS) + [(0, 1)] * len(Z_CAPS)
WIDTHS = Y_CAPS + Z_CAPS
CHUNKS = 4
REQUESTS = 12
PART = 16


def issue_order(moves, widths, chunks):
    done = {(j, -1): 0.0 for j in range(chunks)}
    issued, order, free, clock = set(), [], {True: 0.0, False: 0.0}, 0.0
    while len(order) < chunks * len(moves):
        ready = []
        for j in range(chunks):
            r = sum((j, q) in issued for q in range(len(moves)))
            if r == len(moves) or (j, r - 1) not in done:
                continue
            if r == 0 and j >= 2 and (j - 2, len(Y_CAPS) - 1) not in issued:
                continue
            ready.append((max(clock, done[j, r - 1] + 2.5 * (r > 0)), j, r))
        at, j, r = min(ready)
        along_y = moves[r][0] != 0
        clock = at + 0.5
        free[along_y] = max(free[along_y], clock) + 0.65 * widths[r]
        done[j, r] = free[along_y]
        issued.add((j, r))
        order.append((j, r))
    return order


def carry_kernel(requests, table_ref, store_ref, kv_ref, out_ref, w_ref, held, *rest):
    rounds = len(MOVES)
    total = CHUNKS * rounds
    out_bufs = rest[:total]
    in_bufs = rest[total : 2 * total]
    last, swap_sems, send_sems, recv_sems, w_send_sems, w_recv_sems = rest[2 * total :]
    y, z, c = place()
    half = held.shape[1]
    spans = store_ref.shape[0]
    steps = [((y + dy) % RING_Y, (z + dz) % RING_Z) for dy, dz in ((1, 0), (-1, 0), (0, 1), (0, -1))]
    near = [key_of(a + 0, b + 0, c) for a, b in steps]
    buddy = key_of(y, z, 1 - c)
    _, depth, row = peer_groups()
    x, planes = lax.axis_index("seq"), lax.axis_size("seq")
    seq = [lax.rem(x + d, planes) for d in range(1, planes)]
    greet(depth + row + [buddy], seq)
    quarter = kv_ref.at[x // 2, pl.ds(pl.multiple_of((x % 2) * PART, PART), PART)]
    pair = y * RING_Z + z
    own = pltpu.make_async_copy(quarter, w_ref.at[x, pair], swap_sems.at[3])
    own.start()
    w_flights = [
        [
            send(quarter, w_ref.at[x, pair], w_send_sems.at[i], w_recv_sems.at[i], peer)
            for i, peer in enumerate(depth)
        ]
    ]

    def pass_on(stage):
        if stage == 1:
            own.wait()
        for copy in w_flights[-1]:
            copy.wait_recv()
        if stage == 1:
            part, peers, at, axis = w_ref.at[x, pl.ds(y * RING_Z, RING_Z)], row, 7, "keys"
        else:
            part, peers, at, axis = w_ref.at[x], seq, 10, "seq"
        w_flights.append(
            [
                send(part, part, w_send_sems.at[at + i], w_recv_sems.at[at + i], peer, axis)
                for i, peer in enumerate(peers)
            ]
        )

    mine = pl.ds(pl.multiple_of(c * half, half), half)
    theirs = pl.ds(pl.multiple_of((1 - c) * half, half), half)
    swap = send(
        store_ref.at[:, theirs], held.at[pl.ds(spans, spans)], swap_sems.at[0], swap_sems.at[1], buddy
    )
    keep = pltpu.make_async_copy(store_ref.at[:, mine], held.at[pl.ds(0, spans)], swap_sems.at[2])
    keep.start()
    swap.wait()
    keep.wait()
    bases = np.concatenate([[2 * spans], 2 * spans + np.cumsum(2 * np.array(WIDTHS))]).tolist()

    def picked(j, r, at):
        step, part = j // 2, j % 2
        rows = slice(part * PART, (part + 1) * PART)
        here = jnp.where(at < 2 * spans, at + step, 0)
        value = held[here, rows, :]
        for q in range(r):
            count = 2 * WIDTHS[q]
            inside = (at >= bases[q]) & (at < bases[q] + count)
            value = jnp.where(inside, in_bufs[j * rounds + q][jnp.where(inside, at - bases[q], 0)], value)
        return value

    flights = {}

    def land(j, r):
        for flight in flights[j, r]:
            flight.wait_recv()

    def issue(j, r):
        if r > 0:
            land(j, r - 1)
        width = WIDTHS[r]
        buf = out_bufs[j * rounds + r]

        def fill(s, carry):
            buf[s] = picked(j, r, table_ref[s, r])
            return carry

        lax.fori_loop(0, 2 * width, fill, 0)
        flights[j, r] = []
        for d in range(2):
            part = pl.ds(d * width, width)
            k = (j * rounds + r) * 2 + d
            peer = near[d if MOVES[r][0] else 2 + d]
            flights[j, r].append(
                send(buf.at[part], in_bufs[j * rounds + r].at[part], send_sems.at[k], recv_sems.at[k], peer)
            )

    def finish(j):
        land(j, rounds - 1)

        def fill(s, carry):
            out_ref[2 * j, s] = picked(j, rounds, table_ref[s, rounds])
            last[j, s] = picked(j, rounds, table_ref[s, rounds + 1])
            return carry

        lax.fori_loop(0, requests, fill, 0)
        k = 2 * total + j
        flights[j, rounds] = [
            send(last.at[j], out_ref.at[2 * j + 1], send_sems.at[k], recv_sems.at[k], buddy)
        ]

    waiting = []
    for j, r in issue_order(MOVES, WIDTHS, CHUNKS):
        issue(j, r)
        if r == rounds - 1:
            waiting.append(j)
        elif waiting:
            finish(waiting.pop(0))
        if (j, r) in ((1, 1), (2, 1)):
            pass_on(j)
    for j in waiting:
        finish(j)
    for j in range(CHUNKS):
        land(j, rounds)
    for copy in w_flights[-1]:
        copy.wait_recv()
    for copies in list(flights.values()) + w_flights:
        for copy in copies:
            copy.wait_send()


def carry(store, kv_weight, table):
    spans, rows, enc_width = store.shape
    planes = lax.axis_size("seq")
    item = (PART, enc_width)
    bufs = [pltpu.VMEM((2 * w, *item), store.dtype) for _ in range(CHUNKS) for w in WIDTHS]
    copies = 2 * len(bufs) + CHUNKS
    return pl.pallas_call(
        functools.partial(carry_kernel, REQUESTS),
        out_shape=[
            jax.ShapeDtypeStruct((2 * CHUNKS, REQUESTS, *item), store.dtype),
            jax.ShapeDtypeStruct((planes, RING_Y * RING_Z, *item), store.dtype),
        ],
        in_specs=[pl.BlockSpec(memory_space=pltpu.SMEM)] + [pl.BlockSpec(memory_space=pl.ANY)] * 2,
        out_specs=[pl.BlockSpec(memory_space=pltpu.VMEM)] * 2,
        scratch_shapes=[pltpu.VMEM((2 * spans, rows // 2, enc_width), store.dtype)]
        + bufs * 2
        + [
            pltpu.VMEM((CHUNKS, REQUESTS, *item), store.dtype),
            pltpu.SemaphoreType.DMA((4,)),
            pltpu.SemaphoreType.DMA((copies,)),
            pltpu.SemaphoreType.DMA((copies,)),
            pltpu.SemaphoreType.DMA((13,)),
            pltpu.SemaphoreType.DMA((13,)),
        ],
        compiler_params=pltpu.CompilerParams(
            collective_id=2, has_side_effects=True, vmem_limit_bytes=60 << 20
        ),
        cost_estimate=pl.CostEstimate(flops=0, bytes_accessed=500 << 20, transcendentals=0),
        name="carry",
    )(table, store, kv_weight)


def direct(neighbour_store, neighbour_ids):
    key_count = lax.axis_size("keys")
    shard_spans = neighbour_store.shape[0]
    flat_ids = neighbour_ids.reshape(-1)
    target, offset = flat_ids // shard_spans, flat_ids % shard_spans
    hit = target[:, None] == jnp.arange(key_count, dtype=jnp.int32)[None, :]
    table = jnp.sum(jnp.where(hit, offset[:, None], 0), axis=0)
    incoming = lax.all_to_all(table, "keys", split_axis=0, concat_axis=0, tiled=True)
    firsts, seconds = take(
        [neighbour_store], [[0]] * 2, jnp.stack([incoming, incoming + 1]), neighbour_store.shape[1]
    )
    arrived = [
        lax.all_to_all(spans, "keys", split_axis=0, concat_axis=0, tiled=True)
        for spans in (firsts, seconds)
    ]
    locs = jnp.stack([target, key_count + target])
    return take(arrived, [[0], [1]], locs, neighbour_store.shape[1])


def body(span_queries, key_slab, neighbour_store, neighbour_ids, attn_queries, kv_weight):
    position = lax.axis_index("keys")
    y, z, c = place()
    own_spans = neighbour_ids.shape[0]
    span_rows = neighbour_store.shape[1]
    all_ids = gather_ids(neighbour_ids)
    asked = jnp.pad(span_queries, ((0, 16 - own_spans), (0, 0)))
    all_asked = lax.all_gather(asked, "keys", axis=0, tiled=True)
    all_asked = all_asked.reshape(RING_Y * RING_Z, CORES, *asked.shape)
    table = routes(all_ids)
    flag = table[:8]
    seq = lax.axis_size("seq")
    worst = flag
    for d in range(1, seq):
        worst = jnp.maximum(
            worst, lax.ppermute(flag, "seq", [(s, (s + d) % seq) for s in range(seq)])
        )
    pieces, weight_own = carry(neighbour_store, kv_weight, table)

    def resend(store, ids, fast):
        return jnp.stack(
            [
                spans[:, h * PART : (h + 1) * PART]
                for spans in direct(store, ids)
                for h in range(span_rows // PART)
            ]
        )

    pieces = lax.cond(
        worst[0, len(WIDTHS) + 2] > 0, resend, lambda store, ids, fast: fast, neighbour_store, neighbour_ids, pieces
    )
    attended, best = attend(pieces, weight_own, key_slab, all_asked, attn_queries)
    column = (position // CORES) * 16
    best_scores = lax.dynamic_slice_in_dim(best, column, own_spans, axis=1)[:2].T
    return (best_scores, attended)


def solution(mesh):
    return jax.shard_map(
        body,
        mesh=mesh,
        in_specs=(
            P(("keys", "seq"), None),
            P("keys", None),
            P("keys", None, None),
            P(("keys", "seq"), None),
            P(("keys", "seq"), None),
            P(None, "keys", None),
        ),
        out_specs=(P(("keys", "seq"), None), P(("keys", "seq"), None)),
        check_vma=False,
    )
```

```python
import functools

import jax
import jax.numpy as jnp
import numpy as np
from jax import lax
from jax.experimental import pallas as pl
from jax.experimental.pallas import tpu as pltpu
from jax.sharding import PartitionSpec as P

HEADS = 16
HEAD_DIM = 128
RING_Y, RING_Z, CORES = 4, 8, 2
Y_CAPS, Z_CAPS = (24, 17), (12, 12, 11, 10)
Z_FIRST_CAPS, Y_LAST_CAPS = (19, 16, 16, 15), (14, 11)
TRIPS = (((True, Y_CAPS), (False, Z_CAPS)), ((False, Z_FIRST_CAPS), (True, Y_LAST_CAPS)))
MOVES = tuple([along for along, caps in trip for _ in caps] for trip in TRIPS)
WIDTHS = tuple([w for _, caps in trip for w in caps] for trip in TRIPS)
CHUNK_TRIPS = (0, 0, 0, 1)
COLUMNS = 8
PART = 16
REQUESTS = 12


def key_of(y, z, c):
    return (y * RING_Z + z) * CORES + c


def place():
    k = lax.axis_index("keys")
    return k // (RING_Z * CORES), (k // CORES) % RING_Z, k % CORES


def shifted(dy, dz, dc):
    pairs = []
    for y in range(RING_Y):
        for z in range(RING_Z):
            for c in range(CORES):
                to = key_of((y + dy) % RING_Y, (z + dz) % RING_Z, (c + dc) % CORES)
                pairs.append((key_of(y, z, c), to))
    return pairs


def greet(peers, seq_peers=()):
    barrier = pltpu.get_barrier_semaphore()
    for axis, peer in [("keys", p) for p in peers] + [("seq", p) for p in seq_peers]:
        pl.semaphore_signal(
            barrier, inc=1, device_id={axis: peer}, device_id_type=pl.DeviceIdType.MESH
        )
    pl.semaphore_wait(barrier, len(peers) + len(seq_peers))


def peer_groups():
    y, z, c = place()
    core = [key_of(y, z, 1 - c)]
    depth = [key_of(y, (z + d) % RING_Z, c) for d in range(1, RING_Z)]
    row = [key_of((y + d) % RING_Y, z, c) for d in range(1, RING_Y)]
    return core, depth, row


def send(src, dst, send_sem, recv_sem, peer, axis="keys"):
    copy = pltpu.make_async_remote_copy(
        src_ref=src,
        dst_ref=dst,
        send_sem=send_sem,
        recv_sem=recv_sem,
        device_id={axis: peer},
        device_id_type=pl.DeviceIdType.MESH,
    )
    copy.start()
    return copy


def gather_ids_kernel(ids_ref, out_ref, held, send_sem, recv_sem):
    y, z, c = place()
    core, depth, row = peer_groups()
    greet(core + depth + row)
    held[y, z, c] = ids_ref[...]
    copies = [send(held.at[y, z, c], held.at[y, z, c], send_sem.at[0], recv_sem.at[0], core[0])]
    for copy in copies:
        copy.wait()
    copies = []
    for i, peer in enumerate(depth):
        copies.append(
            send(held.at[y, z], held.at[y, z], send_sem.at[1 + i], recv_sem.at[1 + i], peer)
        )
    for copy in copies:
        copy.wait()
    copies = []
    for i, peer in enumerate(row):
        copies.append(send(held.at[y], held.at[y], send_sem.at[8 + i], recv_sem.at[8 + i], peer))
    for copy in copies:
        copy.wait()
    out_ref[...] = held[...]


def gather_ids(ids):
    tile = jnp.pad(ids.reshape(1, -1), ((0, 7), (0, 128 - ids.size)))
    shape = (RING_Y, RING_Z, CORES, 8, 128)
    held = pl.pallas_call(
        gather_ids_kernel,
        out_shape=jax.ShapeDtypeStruct(shape, jnp.int32),
        in_specs=[pl.BlockSpec(memory_space=pltpu.VMEM)],
        out_specs=pl.BlockSpec(memory_space=pltpu.VMEM),
        scratch_shapes=[
            pltpu.VMEM(shape, jnp.int32),
            pltpu.SemaphoreType.DMA((11,)),
            pltpu.SemaphoreType.DMA((11,)),
        ],
        compiler_params=pltpu.CompilerParams(collective_id=0, has_side_effects=True),
        name="gather_ids",
    )(tile)
    return held[..., 0, : ids.size].reshape(1, -1)


def merge(a, b):
    high = jnp.maximum(a[0:1], b[0:1])
    low = jnp.maximum(jnp.minimum(a[0:1], b[0:1]), jnp.maximum(a[1:2], b[1:2]))
    return jnp.concatenate([high, low, jnp.zeros((6, high.shape[1]), high.dtype)], axis=0)


def take_kernel(counts, reach, row, locs_ref, *refs):
    sources = refs[: len(counts)]
    outs = refs[len(counts) : -1]
    sems = refs[-1]
    starts = np.concatenate([[0], np.cumsum(counts)]).tolist()
    width, rows = outs[0].shape[0], outs[0].shape[1]

    def piece(k, at):
        if sources[k].shape[1] == rows:
            return sources[k].at[at]
        return sources[k].at[at, pl.ds(pl.multiple_of(row(), rows), rows)]

    def begin(s, carry):
        for d, out in enumerate(outs):
            at = locs_ref[d, s]
            for k in reach[d]:

                @pl.when((at >= starts[k]) & (at < starts[k + 1]))
                def _():
                    pltpu.make_async_copy(
                        piece(k, at - starts[k]), out.at[s], sems.at[d, s]
                    ).start()

        return carry

    lax.fori_loop(0, width, begin, 0)

    def finish(s, carry):
        for d, out in enumerate(outs):
            pltpu.make_async_copy(piece(reach[d][0], 0), out.at[s], sems.at[d, s]).wait()
        return carry

    lax.fori_loop(0, width, finish, 0)


def take(sources, reach, locs, rows, row=None):
    counts = tuple(s.shape[0] for s in sources)
    width = locs.shape[1]
    item = (rows, sources[0].shape[2])
    nbytes = 4 * width * item[0] * item[1] * 2
    return pl.pallas_call(
        functools.partial(take_kernel, counts, reach, row),
        out_shape=[jax.ShapeDtypeStruct((width, *item), sources[0].dtype)] * 2,
        in_specs=[pl.BlockSpec(memory_space=pltpu.SMEM)]
        + [pl.BlockSpec(memory_space=pl.ANY)] * len(sources),
        out_specs=[pl.BlockSpec(memory_space=pltpu.VMEM)] * 2,
        scratch_shapes=[pltpu.SemaphoreType.DMA((2, width))],
        cost_estimate=pl.CostEstimate(flops=0, bytes_accessed=nbytes, transcendentals=0),
        compiler_params=pltpu.CompilerParams(vmem_limit_bytes=32 << 20),
        name="take_spans",
    )(locs, *sources)


def top_two(scores):
    top = jnp.max(scores, axis=0, keepdims=True)
    at_top = scores == top
    ties = jnp.sum(jnp.where(at_top, 1.0, 0.0), axis=0, keepdims=True)
    rest = jnp.max(jnp.where(at_top, -jnp.inf, scores), axis=0, keepdims=True)
    second = jnp.where(ties > 1.5, top, rest)
    return jnp.concatenate([top, second, jnp.zeros((6, top.shape[1]), top.dtype)], axis=0)


SWAP, SLAB, DEPTH, ROW = 0, 8, 9, 16


def attend_kernel(
    pieces,
    w_own,
    w_all,
    slab,
    asked,
    q_ref,
    o_ref,
    best_ref,
    x,
    wk,
    wv,
    keys,
    values,
    w_other,
    other_slab,
    found,
    after_depth,
    landed,
    send_sem,
    recv_sem,
):
    c = place()[2]
    g = pl.program_id(0)
    parts, requests, part, width = pieces.shape
    spans = requests // 2
    near = 2 * part * parts
    rows = q_ref.shape[0] // spans
    pairs = w_own.shape[1]
    steps = w_all.shape[1] // pairs
    core, depth, row = peer_groups()
    contract = (((1,), (1,)), ((), ()))
    dot = functools.partial(lax.dot_general, preferred_element_type=jnp.float32)

    def flight(src, dst, k, peer):
        return pltpu.make_async_remote_copy(
            src_ref=src,
            dst_ref=dst,
            send_sem=send_sem.at[k],
            recv_sem=recv_sem.at[k],
            device_id={"keys": peer},
            device_id_type=pl.DeviceIdType.MESH,
        )

    def weights_flight(b):
        at = pl.ds(b * pairs, pairs)
        return flight(w_all.at[:, at], w_other.at[:, at], SWAP + b, core[0])

    slab_flight = lambda: flight(slab, other_slab, SLAB, core[0])
    depth_flights = lambda: [
        flight(found, landed.at[i], DEPTH + i, peer) for i, peer in enumerate(depth)
    ]
    row_flights = lambda: [
        flight(after_depth, landed.at[len(depth) + i], ROW + i, peer) for i, peer in enumerate(row)
    ]

    @pl.when(g == 0)
    def _():
        greet(core + depth + row)
        for b in range(steps):
            weights_flight(b).start()
        slab_flight().start()
        for u in range(spans):
            for i in range(parts):
                at = (u * parts + i) * 2 * part
                x[at : at + 2 * part, :] = pieces[i, 2 * u : 2 * u + 2].reshape(2 * part, width)

    weights_flight(g).wait_recv()
    for kind, w in enumerate((wk, wv)):
        for j in range(pairs):
            for h in range(2):
                mine = pl.multiple_of(j * 64 + c * 32 + h * PART, PART)
                theirs = pl.multiple_of(j * 64 + (1 - c) * 32 + h * PART, PART)
                w[pl.ds(mine, PART), :] = w_own[kind * 2 + h, j]
                w[pl.ds(theirs, PART), :] = w_other[kind * 2 + h, g * pairs + j]
    keys[...] = dot(x[...], wk[...], contract).astype(jnp.bfloat16)
    values[...] = dot(x[...], wv[...], contract).astype(jnp.bfloat16)
    zero = jnp.zeros((rows, HEAD_DIM), jnp.bfloat16)

    def both_heads(u):
        q = q_ref[u * rows : (u + 1) * rows, :]
        return jnp.concatenate(
            [
                jnp.concatenate([q[:, :HEAD_DIM], zero], axis=1),
                jnp.concatenate([zero, q[:, HEAD_DIM:]], axis=1),
            ],
            axis=0,
        )

    def softmax(logits):
        scaled = logits * HEAD_DIM ** (-0.5)
        largest = jnp.max(scaled, axis=-1, keepdims=True)
        terms = jnp.exp(scaled - largest)
        total = jnp.sum(terms, axis=-1, keepdims=True)
        return (terms * (1.0 / total)).astype(jnp.bfloat16)

    logits = [dot(both_heads(u), keys[u * near : (u + 1) * near, :], contract) for u in range(spans)]
    weights = [softmax(part_logits) for part_logits in logits]
    outs = [
        dot(weights[u], values[u * near : (u + 1) * near, :], (((1,), (0,)), ((), ())))
        for u in range(spans)
    ]
    for u, out in enumerate(outs):
        tokens = slice(u * rows, (u + 1) * rows)
        o_ref[tokens, :HEAD_DIM] = out[:rows, :HEAD_DIM].astype(jnp.bfloat16)
        o_ref[tokens, HEAD_DIM:] = out[rows:, HEAD_DIM:].astype(jnp.bfloat16)

    @pl.when(g == 1)
    def _():
        slab_flight().wait_recv()
        queries = asked[:, c].reshape(found.shape[1], slab.shape[1])
        found[...] = merge(
            top_two(dot(slab[...], queries, contract)), top_two(dot(other_slab[...], queries, contract))
        )
        for copy in depth_flights():
            copy.start()

    @pl.when(g == 3)
    def _():
        for copy in depth_flights():
            copy.wait_recv()
        total = found[...]
        for i in range(len(depth)):
            total = merge(total, landed[i])
        after_depth[...] = total
        for copy in row_flights():
            copy.start()

    @pl.when(g == 5)
    def _():
        for copy in row_flights():
            copy.wait_recv()
        total = after_depth[...]
        for i in range(len(row)):
            total = merge(total, landed[len(depth) + i])
        best_ref[...] = total

    @pl.when(g == steps - 1)
    def _():
        for b in range(steps):
            weights_flight(b).wait_send()
        for copy in [slab_flight()] + depth_flights() + row_flights():
            copy.wait_send()


def attend(pieces, w_own, slab, asked, queries):
    parts, requests, part, width = pieces.shape
    near = requests * parts * part
    tokens, columns = queries.shape
    steps = 8
    pairs = w_own.shape[1] // steps
    cols = columns // steps
    found = asked.shape[0] * asked.shape[2]
    block = pl.BlockSpec((tokens, cols), lambda g: (0, g))
    flops = 2 * near * width * 2 * columns
    bf16 = jnp.bfloat16
    return pl.pallas_call(
        attend_kernel,
        grid=(steps,),
        out_shape=[
            jax.ShapeDtypeStruct((tokens, columns), bf16),
            jax.ShapeDtypeStruct((8, found), jnp.float32),
        ],
        in_specs=[
            pl.BlockSpec(pieces.shape, lambda g: (0, 0, 0, 0)),
            pl.BlockSpec((w_own.shape[0], pairs, part, width), lambda g: (0, g, 0, 0)),
            pl.BlockSpec(memory_space=pl.ANY),
            pl.BlockSpec(slab.shape, lambda g: (0, 0)),
            pl.BlockSpec(asked.shape, lambda g: (0, 0, 0, 0)),
            block,
        ],
        out_specs=[block, pl.BlockSpec((8, found), lambda g: (0, 0))],
        scratch_shapes=[
            pltpu.VMEM((near, width), bf16),
            pltpu.VMEM((cols, width), bf16),
            pltpu.VMEM((cols, width), bf16),
            pltpu.VMEM((near, cols), bf16),
            pltpu.VMEM((near, cols), bf16),
            pltpu.VMEM(w_own.shape, bf16),
            pltpu.VMEM(slab.shape, bf16),
            pltpu.VMEM((8, found), jnp.float32),
            pltpu.VMEM((8, found), jnp.float32),
            pltpu.VMEM((10, 8, found), jnp.float32),
            pltpu.SemaphoreType.DMA((19,)),
            pltpu.SemaphoreType.DMA((19,)),
        ],
        compiler_params=pltpu.CompilerParams(
            collective_id=1, has_side_effects=True, vmem_limit_bytes=48 << 20
        ),
        cost_estimate=pl.CostEstimate(
            flops=flops, bytes_accessed=20 << 20, transcendentals=tokens * HEADS * 256
        ),
        name="attend",
    )(pieces, w_own, w_own, slab, asked, queries)


def routes_kernel(ids_ref, table_ref, before):
    requests = ids_ref.shape[1]
    per_device = requests // (RING_Y * RING_Z * CORES)
    y, z, c = place()
    before[...] = jnp.where(
        lax.broadcasted_iota(jnp.int32, before.shape, 0)
        < lax.broadcasted_iota(jnp.int32, before.shape, 1),
        1.0,
        0.0,
    ).astype(jnp.bfloat16)
    index = lax.broadcasted_iota(jnp.int32, (1, requests), 1)
    k = sum(jnp.where(index >= t * per_device, 1, 0) for t in range(1, requests // per_device))
    n = index - k * per_device
    to_y, to_z = k >> 4, (k >> 1) & 7
    tie_y, tie_z = ((n >> 1) + k) & 1, (n + k) & 1
    ids = ids_ref[...]
    shard, offset = ids >> 6, ids & 63
    from_y, from_z, from_c = shard >> 4, (shard >> 1) & 7, shard & 1
    loc = jnp.where(from_c == c, 0, 64) + offset
    nodes = RING_Y * RING_Z * 2
    node_rows = lax.broadcasted_iota(jnp.int32, (nodes, requests), 0)
    lanes = lax.broadcasted_iota(jnp.int32, table_ref.shape, 1)
    slots = lax.broadcasted_iota(jnp.int32, (table_ref.shape[0], requests), 0)
    table = jnp.zeros(table_ref.shape, jnp.float32)
    here = y * RING_Z + z

    def column(hits, values):
        return jnp.sum(jnp.where(hits, values.astype(jnp.float32), 0.0), axis=1, keepdims=True)

    stuck = jnp.zeros((1, requests), jnp.int32)
    first_loc = loc
    for t, trip in enumerate(TRIPS):
        base, r, loc = 128, t * COLUMNS, first_loc
        for leg, (along_y, caps) in enumerate(trip):
            ring = RING_Y if along_y else RING_Z
            position, target, tie = (from_y, to_y, tie_y) if along_y else (from_z, to_z, tie_z)
            if along_y:
                other = to_z if leg else from_z
            else:
                other = to_y if leg else from_y
            ahead = (target - position) & (ring - 1)
            back = (ahead > ring // 2) | ((ahead == ring // 2) & (tie == 1))
            left = jnp.where(back, (ring - ahead) & (ring - 1), ahead)
            step = jnp.where(back, ring - 1, 1)
            way = jnp.where(back, 1, 0)
            for width in caps:
                chip = position * RING_Z + other if along_y else other * RING_Z + position
                node = chip * 2 + way
                seat = node_rows == node
                kinds = [
                    jnp.where(seat & (left == d), 1.0, 0.0) for d in range(ring // 2, 0, -1)
                ]
                counts = lax.dot_general(
                    jnp.concatenate(kinds, axis=0).astype(jnp.bfloat16),
                    before[...],
                    (((1,), (0,)), ((), ())),
                    preferred_element_type=jnp.float32,
                )
                rank = jnp.zeros((1, requests), jnp.float32)
                ahead_of = jnp.zeros((nodes, 1), jnp.float32)
                for i, kind in enumerate(kinds):
                    mine = counts[i * nodes : (i + 1) * nodes] + ahead_of
                    rank += jnp.sum(kind * mine, axis=0, keepdims=True)
                    ahead_of += jnp.sum(kind, axis=1, keepdims=True)
                rank = rank.astype(jnp.int32)
                goes = (left > 0) & (rank < width)
                slot = jnp.where(goes & (chip == here), way * width + rank, -1)
                table = jnp.where(lanes == r, column(slots == slot, loc), table)
                loc = jnp.where(goes, base + way * width + rank, loc)
                base += 2 * width
                position = jnp.where(goes, (position + step) & (ring - 1), position)
                left = left - jnp.where(goes, 1, 0)
                r += 1
            stuck = jnp.maximum(stuck, left)
        for core in (c, 1 - c):
            first = (here * CORES + core) * per_device
            wanted = (index == first + slots) & (slots < per_device)
            table = jnp.where(lanes == r, column(wanted, loc), table)
            r += 1
    worst = jnp.max(stuck.astype(jnp.float32), axis=1, keepdims=True)
    table = jnp.where(lanes == len(TRIPS) * COLUMNS, worst, table)
    table_ref[...] = table.astype(jnp.int32)


def routes(all_ids):
    requests = all_ids.shape[1]
    return pl.pallas_call(
        routes_kernel,
        out_shape=jax.ShapeDtypeStruct((2 * max(WIDTHS[0] + WIDTHS[1]), 128), jnp.int32),
        in_specs=[pl.BlockSpec(memory_space=pltpu.VMEM)],
        out_specs=pl.BlockSpec(memory_space=pltpu.VMEM),
        scratch_shapes=[pltpu.VMEM((requests, requests), jnp.bfloat16)],
        name="routes",
    )(all_ids)


ISSUES = (
    ((3, 0), (1, 0), (0, 0), (3, 1), (1, 1), (3, 2), (0, 1), (3, 3), (2, 0), (1, 2), (0, 2), (1, 3))
    + ((2, 1), (0, 3), (1, 4), (-1, 1), (2, 2), (3, 4), (-1, 2), (0, 4), (2, 3), (3, 5), (0, 5))
    + ((2, 4), (1, 5), (2, 5))
)


def carry_kernel(table_ref, store_ref, kv_ref, out_ref, w_ref, *rest):
    rounds = len(MOVES[0])
    total = len(CHUNK_TRIPS) * rounds
    held, rest = rest[:2], rest[2:]
    out_bufs = rest[:total]
    in_bufs = rest[total : 2 * total]
    last, swap_sems, send_sems, recv_sems, w_send_sems, w_recv_sems = rest[2 * total :]
    y, z, c = place()
    spans = store_ref.shape[0]
    steps = [((y + dy) % RING_Y, (z + dz) % RING_Z) for dy, dz in ((1, 0), (-1, 0), (0, 1), (0, -1))]
    near = [key_of(a, b, c) for a, b in steps]
    buddy = key_of(y, z, 1 - c)
    _, depth, row = peer_groups()
    x, planes = lax.axis_index("seq"), lax.axis_size("seq")
    seq = [lax.rem(x + d, planes) for d in range(1, planes)]
    greet(depth + row + [buddy], seq)
    quarter = kv_ref.at[x // 2, pl.ds(pl.multiple_of((x % 2) * PART, PART), PART)]
    pair = y * RING_Z + z
    own = pltpu.make_async_copy(quarter, w_ref.at[x, pair], swap_sems.at[6])
    own.start()
    w_flights = [
        [
            send(quarter, w_ref.at[x, pair], w_send_sems.at[i], w_recv_sems.at[i], peer)
            for i, peer in enumerate(depth)
        ]
    ]

    def pass_on(stage):
        if stage == 1:
            own.wait()
        for copy in w_flights[-1]:
            copy.wait_recv()
        if stage == 1:
            part, peers, at, axis = w_ref.at[x, pl.ds(y * RING_Z, RING_Z)], row, 7, "keys"
        else:
            part, peers, at, axis = w_ref.at[x], seq, 10, "seq"
        w_flights.append(
            [
                send(part, part, w_send_sems.at[at + i], w_recv_sems.at[at + i], peer, axis)
                for i, peer in enumerate(peers)
            ]
        )

    halves = {}
    for part in (1, 0):
        mine = pl.ds(pl.multiple_of((2 * c + part) * PART, PART), PART)
        theirs = pl.ds(pl.multiple_of((2 * (1 - c) + part) * PART, PART), PART)
        keep = pltpu.make_async_copy(
            store_ref.at[:, mine], held[part].at[pl.ds(0, spans)], swap_sems.at[3 * part + 2]
        )
        keep.start()
        swap = send(
            store_ref.at[:, theirs],
            held[part].at[pl.ds(spans, spans)],
            swap_sems.at[3 * part],
            swap_sems.at[3 * part + 1],
            buddy,
        )
        halves[part] = (swap, keep)
    ready = set()
    bases = [
        np.concatenate([[2 * spans], 2 * spans + np.cumsum(2 * np.array(w))]).tolist() for w in WIDTHS
    ]

    def picked(j, r, at):
        step, part = j // 2, j % 2
        value = held[part][jnp.where(at < 2 * spans, at + step, 0)]
        for q in range(r):
            base, count = bases[CHUNK_TRIPS[j]][q], 2 * WIDTHS[CHUNK_TRIPS[j]][q]
            inside = (at >= base) & (at < base + count)
            block = in_bufs[j * rounds + q][jnp.where(inside, at - base, 0)]
            value = jnp.where(inside, block, value)
        return value

    flights = {}

    def land(j, r):
        for flight in flights[j, r]:
            flight.wait_recv()

    def issue(j, r):
        trip = CHUNK_TRIPS[j]
        if r > 0:
            land(j, r - 1)
        elif j % 2 not in ready:
            ready.add(j % 2)
            for copy in halves[j % 2]:
                copy.wait()
        width = WIDTHS[trip][r]
        buf = out_bufs[j * rounds + r]

        def fill(s, carry):
            buf[s] = picked(j, r, table_ref[s, trip * COLUMNS + r])
            return carry

        lax.fori_loop(0, 2 * width, fill, 0)
        flights[j, r] = []
        for d in range(2):
            part = pl.ds(d * width, width)
            k = (j * rounds + r) * 2 + d
            peer = near[d if MOVES[trip][r] else 2 + d]
            flights[j, r].append(
                send(buf.at[part], in_bufs[j * rounds + r].at[part], send_sems.at[k], recv_sems.at[k], peer)
            )

    def finish(j):
        land(j, rounds - 1)
        column = CHUNK_TRIPS[j] * COLUMNS + rounds

        def fill(s, carry):
            out_ref[2 * j, s] = picked(j, rounds, table_ref[s, column])
            last[j, s] = picked(j, rounds, table_ref[s, column + 1])
            return carry

        lax.fori_loop(0, REQUESTS, fill, 0)
        k = 2 * total + j
        flights[j, rounds] = [
            send(last.at[j], out_ref.at[2 * j + 1], send_sems.at[k], recv_sems.at[k], buddy)
        ]

    waiting = []
    for j, r in ISSUES:
        if j < 0:
            pass_on(r)
            continue
        issue(j, r)
        if r == rounds - 1:
            waiting.append(j)
        elif waiting:
            finish(waiting.pop(0))
    for j in waiting:
        finish(j)
    for j in range(len(CHUNK_TRIPS)):
        land(j, rounds)
    for copy in w_flights[-1]:
        copy.wait_recv()
    for copies in list(flights.values()) + w_flights:
        for copy in copies:
            copy.wait_send()


def carry(store, kv_weight, table):
    spans, _, enc_width = store.shape
    planes = lax.axis_size("seq")
    item = (PART, enc_width)
    chunks = len(CHUNK_TRIPS)
    bufs = [pltpu.VMEM((2 * w, *item), store.dtype) for t in CHUNK_TRIPS for w in WIDTHS[t]]
    copies = 2 * len(bufs) + chunks
    return pl.pallas_call(
        carry_kernel,
        out_shape=[
            jax.ShapeDtypeStruct((2 * chunks, REQUESTS, *item), store.dtype),
            jax.ShapeDtypeStruct((planes, RING_Y * RING_Z, *item), store.dtype),
        ],
        in_specs=[pl.BlockSpec(memory_space=pltpu.SMEM)] + [pl.BlockSpec(memory_space=pl.ANY)] * 2,
        out_specs=[pl.BlockSpec(memory_space=pltpu.VMEM)] * 2,
        scratch_shapes=[pltpu.VMEM((2 * spans, *item), store.dtype)] * 2
        + bufs * 2
        + [
            pltpu.VMEM((chunks, REQUESTS, *item), store.dtype),
            pltpu.SemaphoreType.DMA((7,)),
            pltpu.SemaphoreType.DMA((copies,)),
            pltpu.SemaphoreType.DMA((copies,)),
            pltpu.SemaphoreType.DMA((13,)),
            pltpu.SemaphoreType.DMA((13,)),
        ],
        compiler_params=pltpu.CompilerParams(
            collective_id=2, has_side_effects=True, vmem_limit_bytes=60 << 20
        ),
        cost_estimate=pl.CostEstimate(flops=0, bytes_accessed=500 << 20, transcendentals=0),
        name="carry",
    )(table, store, kv_weight)


def direct(neighbour_store, neighbour_ids):
    key_count = lax.axis_size("keys")
    shard_spans = neighbour_store.shape[0]
    flat_ids = neighbour_ids.reshape(-1)
    target, offset = flat_ids // shard_spans, flat_ids % shard_spans
    hit = target[:, None] == jnp.arange(key_count, dtype=jnp.int32)[None, :]
    table = jnp.sum(jnp.where(hit, offset[:, None], 0), axis=0)
    incoming = lax.all_to_all(table, "keys", split_axis=0, concat_axis=0, tiled=True)
    firsts, seconds = take(
        [neighbour_store], [[0]] * 2, jnp.stack([incoming, incoming + 1]), neighbour_store.shape[1]
    )
    arrived = [
        lax.all_to_all(spans, "keys", split_axis=0, concat_axis=0, tiled=True)
        for spans in (firsts, seconds)
    ]
    locs = jnp.stack([target, key_count + target])
    return take(arrived, [[0], [1]], locs, neighbour_store.shape[1])


def body(span_queries, key_slab, neighbour_store, neighbour_ids, attn_queries, kv_weight):
    position = lax.axis_index("keys")
    y, z, c = place()
    own_spans = neighbour_ids.shape[0]
    span_rows = neighbour_store.shape[1]
    all_ids = gather_ids(neighbour_ids)
    asked = jnp.pad(span_queries, ((0, 16 - own_spans), (0, 0)))
    all_asked = lax.all_gather(asked, "keys", axis=0, tiled=True)
    all_asked = all_asked.reshape(RING_Y * RING_Z, CORES, *asked.shape)
    table = routes(all_ids)
    flag = table[:8]
    seq = lax.axis_size("seq")
    worst = flag
    for d in range(1, seq):
        worst = jnp.maximum(
            worst, lax.ppermute(flag, "seq", [(s, (s + d) % seq) for s in range(seq)])
        )
    pieces, weight_own = carry(neighbour_store, kv_weight, table)

    def resend(store, ids, fast):
        return jnp.stack(
            [
                spans[:, h * PART : (h + 1) * PART]
                for spans in direct(store, ids)
                for h in range(span_rows // PART)
            ]
        )

    pieces = lax.cond(
        worst[0, len(TRIPS) * COLUMNS] > 0, resend, lambda store, ids, fast: fast, neighbour_store, neighbour_ids, pieces
    )
    attended, best = attend(pieces, weight_own, key_slab, all_asked, attn_queries)
    column = (position // CORES) * 16
    best_scores = lax.dynamic_slice_in_dim(best, column, own_spans, axis=1)[:2].T
    return (best_scores, attended)


def solution(mesh):
    return jax.shard_map(
        body,
        mesh=mesh,
        in_specs=(
            P(("keys", "seq"), None),
            P("keys", None),
            P("keys", None, None),
            P(("keys", "seq"), None),
            P(("keys", "seq"), None),
            P(None, "keys", None),
        ),
        out_specs=(P(("keys", "seq"), None), P(("keys", "seq"), None)),
        check_vma=False,
    )
```

```python
import functools

import jax
import jax.numpy as jnp
import numpy as np
from jax import lax
from jax.experimental import pallas as pl
from jax.experimental.pallas import tpu as pltpu
from jax.sharding import PartitionSpec as P

HEADS = 16
HEAD_DIM = 128
RING_Y, RING_Z, CORES = 4, 8, 2
Y_CAPS, Z_CAPS = (24, 17), (12, 12, 11, 10)
Z_FIRST_CAPS, Y_LAST_CAPS = (19, 16, 16, 15), (14, 11)
TRIPS = (((True, Y_CAPS), (False, Z_CAPS)), ((False, Z_FIRST_CAPS), (True, Y_LAST_CAPS)))
MOVES = tuple([along for along, caps in trip for _ in caps] for trip in TRIPS)
WIDTHS = tuple([w for _, caps in trip for w in caps] for trip in TRIPS)
CHUNK_TRIPS = (0, 0, 0, 1)
COLUMNS = 8
PART = 16
REQUESTS = 12


def key_of(y, z, c):
    return (y * RING_Z + z) * CORES + c


def place():
    k = lax.axis_index("keys")
    return k // (RING_Z * CORES), (k // CORES) % RING_Z, k % CORES


def shifted(dy, dz, dc):
    pairs = []
    for y in range(RING_Y):
        for z in range(RING_Z):
            for c in range(CORES):
                to = key_of((y + dy) % RING_Y, (z + dz) % RING_Z, (c + dc) % CORES)
                pairs.append((key_of(y, z, c), to))
    return pairs


def greet(peers, seq_peers=()):
    barrier = pltpu.get_barrier_semaphore()
    for axis, peer in [("keys", p) for p in peers] + [("seq", p) for p in seq_peers]:
        pl.semaphore_signal(
            barrier, inc=1, device_id={axis: peer}, device_id_type=pl.DeviceIdType.MESH
        )
    pl.semaphore_wait(barrier, len(peers) + len(seq_peers))


def peer_groups():
    y, z, c = place()
    core = [key_of(y, z, 1 - c)]
    depth = [key_of(y, (z + d) % RING_Z, c) for d in range(1, RING_Z)]
    row = [key_of((y + d) % RING_Y, z, c) for d in range(1, RING_Y)]
    return core, depth, row


def send(src, dst, send_sem, recv_sem, peer, axis="keys"):
    copy = pltpu.make_async_remote_copy(
        src_ref=src,
        dst_ref=dst,
        send_sem=send_sem,
        recv_sem=recv_sem,
        device_id={axis: peer},
        device_id_type=pl.DeviceIdType.MESH,
    )
    copy.start()
    return copy


def gather_ids_kernel(ids_ref, store_ref, out_ref, swapped_ref, held, rows, send_sem, recv_sem):
    y, z, c = place()
    core, depth, row = peer_groups()
    greet(core + depth + row)
    held[z, c] = ids_ref[...]
    own = held.at[z, c]
    first = send(own, own, send_sem.at[0], recv_sem.at[0], core[0])
    half = swapped_ref.shape[1]
    theirs = pl.ds(pl.multiple_of((1 - c) * half, half), half)
    swap = send(store_ref.at[:, theirs], swapped_ref, send_sem.at[11], recv_sem.at[11], core[0])
    first.wait()
    copies = []
    for i, peer in enumerate(depth):
        copies.append(send(held.at[z], held.at[z], send_sem.at[1 + i], recv_sem.at[1 + i], peer))
    for copy in copies:
        copy.wait()
    rows[y] = held[:, :, 0, :].reshape(rows.shape[1:])
    copies = []
    for i, peer in enumerate(row):
        copies.append(send(rows.at[y], rows.at[y], send_sem.at[8 + i], recv_sem.at[8 + i], peer))
    for copy in copies:
        copy.wait()
    out_ref[...] = rows[...]
    swap.wait()


def gather_ids(ids, store):
    tile = jnp.pad(ids.reshape(1, -1), ((0, 7), (0, 128 - ids.size)))
    shape = (RING_Y, RING_Z * CORES, 128)
    spans, span_rows, width = store.shape
    all_ids, swapped = pl.pallas_call(
        gather_ids_kernel,
        out_shape=[
            jax.ShapeDtypeStruct(shape, jnp.int32),
            jax.ShapeDtypeStruct((spans, span_rows // 2, width), store.dtype),
        ],
        in_specs=[pl.BlockSpec(memory_space=pltpu.VMEM), pl.BlockSpec(memory_space=pl.ANY)],
        out_specs=[pl.BlockSpec(memory_space=pltpu.VMEM)] * 2,
        scratch_shapes=[
            pltpu.VMEM((RING_Z, CORES, 8, 128), jnp.int32),
            pltpu.VMEM(shape, jnp.int32),
            pltpu.SemaphoreType.DMA((12,)),
            pltpu.SemaphoreType.DMA((12,)),
        ],
        compiler_params=pltpu.CompilerParams(
            collective_id=0, has_side_effects=True, vmem_limit_bytes=60 << 20
        ),
        name="gather_ids",
    )(tile, store)
    return all_ids.reshape(-1, 128)[:, : ids.size].reshape(1, -1), swapped


def merge(a, b):
    high = jnp.maximum(a[0:1], b[0:1])
    low = jnp.maximum(jnp.minimum(a[0:1], b[0:1]), jnp.maximum(a[1:2], b[1:2]))
    return jnp.concatenate([high, low, jnp.zeros((6, high.shape[1]), high.dtype)], axis=0)


def take_kernel(counts, reach, row, locs_ref, *refs):
    sources = refs[: len(counts)]
    outs = refs[len(counts) : -1]
    sems = refs[-1]
    starts = np.concatenate([[0], np.cumsum(counts)]).tolist()
    width, rows = outs[0].shape[0], outs[0].shape[1]

    def piece(k, at):
        if sources[k].shape[1] == rows:
            return sources[k].at[at]
        return sources[k].at[at, pl.ds(pl.multiple_of(row(), rows), rows)]

    def begin(s, carry):
        for d, out in enumerate(outs):
            at = locs_ref[d, s]
            for k in reach[d]:

                @pl.when((at >= starts[k]) & (at < starts[k + 1]))
                def _():
                    pltpu.make_async_copy(
                        piece(k, at - starts[k]), out.at[s], sems.at[d, s]
                    ).start()

        return carry

    lax.fori_loop(0, width, begin, 0)

    def finish(s, carry):
        for d, out in enumerate(outs):
            pltpu.make_async_copy(piece(reach[d][0], 0), out.at[s], sems.at[d, s]).wait()
        return carry

    lax.fori_loop(0, width, finish, 0)


def take(sources, reach, locs, rows, row=None):
    counts = tuple(s.shape[0] for s in sources)
    width = locs.shape[1]
    item = (rows, sources[0].shape[2])
    nbytes = 4 * width * item[0] * item[1] * 2
    return pl.pallas_call(
        functools.partial(take_kernel, counts, reach, row),
        out_shape=[jax.ShapeDtypeStruct((width, *item), sources[0].dtype)] * 2,
        in_specs=[pl.BlockSpec(memory_space=pltpu.SMEM)]
        + [pl.BlockSpec(memory_space=pl.ANY)] * len(sources),
        out_specs=[pl.BlockSpec(memory_space=pltpu.VMEM)] * 2,
        scratch_shapes=[pltpu.SemaphoreType.DMA((2, width))],
        cost_estimate=pl.CostEstimate(flops=0, bytes_accessed=nbytes, transcendentals=0),
        compiler_params=pltpu.CompilerParams(vmem_limit_bytes=32 << 20),
        name="take_spans",
    )(locs, *sources)


def top_two(scores):
    top = jnp.max(scores, axis=0, keepdims=True)
    at_top = scores == top
    ties = jnp.sum(jnp.where(at_top, 1.0, 0.0), axis=0, keepdims=True)
    rest = jnp.max(jnp.where(at_top, -jnp.inf, scores), axis=0, keepdims=True)
    second = jnp.where(ties > 1.5, top, rest)
    return jnp.concatenate([top, second, jnp.zeros((6, top.shape[1]), top.dtype)], axis=0)


SWAP, SLAB, DEPTH, ROW = 0, 8, 9, 16


def attend_kernel(
    pieces,
    w_own,
    w_all,
    slab,
    asked,
    q_ref,
    o_ref,
    best_ref,
    x,
    wk,
    wv,
    keys,
    values,
    w_other,
    other_slab,
    found,
    after_depth,
    landed,
    send_sem,
    recv_sem,
):
    c = place()[2]
    g = pl.program_id(0)
    parts, requests, part, width = pieces.shape
    spans = requests // 2
    near = 2 * part * parts
    rows = q_ref.shape[0] // spans
    pairs = w_own.shape[1]
    steps = w_all.shape[1] // pairs
    core, depth, row = peer_groups()
    contract = (((1,), (1,)), ((), ()))
    dot = functools.partial(lax.dot_general, preferred_element_type=jnp.float32)

    def flight(src, dst, k, peer):
        return pltpu.make_async_remote_copy(
            src_ref=src,
            dst_ref=dst,
            send_sem=send_sem.at[k],
            recv_sem=recv_sem.at[k],
            device_id={"keys": peer},
            device_id_type=pl.DeviceIdType.MESH,
        )

    def weights_flight(b):
        at = pl.ds(b * pairs, pairs)
        return flight(w_all.at[:, at], w_other.at[:, at], SWAP + b, core[0])

    slab_flight = lambda: flight(slab, other_slab, SLAB, core[0])
    depth_flights = lambda: [
        flight(found, landed.at[i], DEPTH + i, peer) for i, peer in enumerate(depth)
    ]
    row_flights = lambda: [
        flight(after_depth, landed.at[len(depth) + i], ROW + i, peer) for i, peer in enumerate(row)
    ]

    @pl.when(g == 0)
    def _():
        greet(core + depth + row)
        for b in range(steps):
            weights_flight(b).start()
        slab_flight().start()
        for u in range(spans):
            for i in range(parts):
                at = (u * parts + i) * 2 * part
                x[at : at + 2 * part, :] = pieces[i, 2 * u : 2 * u + 2].reshape(2 * part, width)

    weights_flight(g).wait_recv()
    for kind, w in enumerate((wk, wv)):
        for j in range(pairs):
            for h in range(2):
                mine = pl.multiple_of(j * 64 + c * 32 + h * PART, PART)
                theirs = pl.multiple_of(j * 64 + (1 - c) * 32 + h * PART, PART)
                w[pl.ds(mine, PART), :] = w_own[kind * 2 + h, j]
                w[pl.ds(theirs, PART), :] = w_other[kind * 2 + h, g * pairs + j]
    keys[...] = dot(x[...], wk[...], contract).astype(jnp.bfloat16)
    values[...] = dot(x[...], wv[...], contract).astype(jnp.bfloat16)
    zero = jnp.zeros((rows, HEAD_DIM), jnp.bfloat16)

    def both_heads(u):
        q = q_ref[u * rows : (u + 1) * rows, :]
        return jnp.concatenate(
            [
                jnp.concatenate([q[:, :HEAD_DIM], zero], axis=1),
                jnp.concatenate([zero, q[:, HEAD_DIM:]], axis=1),
            ],
            axis=0,
        )

    def softmax(logits):
        scaled = logits * HEAD_DIM ** (-0.5)
        largest = jnp.max(scaled, axis=-1, keepdims=True)
        terms = jnp.exp(scaled - largest)
        total = jnp.sum(terms, axis=-1, keepdims=True)
        return (terms * (1.0 / total)).astype(jnp.bfloat16)

    logits = [dot(both_heads(u), keys[u * near : (u + 1) * near, :], contract) for u in range(spans)]
    weights = [softmax(part_logits) for part_logits in logits]
    outs = [
        dot(weights[u], values[u * near : (u + 1) * near, :], (((1,), (0,)), ((), ())))
        for u in range(spans)
    ]
    for u, out in enumerate(outs):
        tokens = slice(u * rows, (u + 1) * rows)
        o_ref[tokens, :HEAD_DIM] = out[:rows, :HEAD_DIM].astype(jnp.bfloat16)
        o_ref[tokens, HEAD_DIM:] = out[rows:, HEAD_DIM:].astype(jnp.bfloat16)

    @pl.when(g == 1)
    def _():
        slab_flight().wait_recv()
        queries = asked[:, c].reshape(found.shape[1], slab.shape[1])
        found[...] = merge(
            top_two(dot(slab[...], queries, contract)), top_two(dot(other_slab[...], queries, contract))
        )
        for copy in depth_flights():
            copy.start()

    @pl.when(g == 3)
    def _():
        for copy in depth_flights():
            copy.wait_recv()
        total = found[...]
        for i in range(len(depth)):
            total = merge(total, landed[i])
        after_depth[...] = total
        for copy in row_flights():
            copy.start()

    @pl.when(g == 5)
    def _():
        for copy in row_flights():
            copy.wait_recv()
        total = after_depth[...]
        for i in range(len(row)):
            total = merge(total, landed[len(depth) + i])
        best_ref[...] = total

    @pl.when(g == steps - 1)
    def _():
        for b in range(steps):
            weights_flight(b).wait_send()
        for copy in [slab_flight()] + depth_flights() + row_flights():
            copy.wait_send()


def attend(pieces, w_own, slab, asked, queries):
    parts, requests, part, width = pieces.shape
    near = requests * parts * part
    tokens, columns = queries.shape
    steps = 8
    pairs = w_own.shape[1] // steps
    cols = columns // steps
    found = asked.shape[0] * asked.shape[2]
    block = pl.BlockSpec((tokens, cols), lambda g: (0, g))
    flops = 2 * near * width * 2 * columns
    bf16 = jnp.bfloat16
    return pl.pallas_call(
        attend_kernel,
        grid=(steps,),
        out_shape=[
            jax.ShapeDtypeStruct((tokens, columns), bf16),
            jax.ShapeDtypeStruct((8, found), jnp.float32),
        ],
        in_specs=[
            pl.BlockSpec(pieces.shape, lambda g: (0, 0, 0, 0)),
            pl.BlockSpec((w_own.shape[0], pairs, part, width), lambda g: (0, g, 0, 0)),
            pl.BlockSpec(memory_space=pl.ANY),
            pl.BlockSpec(slab.shape, lambda g: (0, 0)),
            pl.BlockSpec(asked.shape, lambda g: (0, 0, 0, 0)),
            block,
        ],
        out_specs=[block, pl.BlockSpec((8, found), lambda g: (0, 0))],
        scratch_shapes=[
            pltpu.VMEM((near, width), bf16),
            pltpu.VMEM((cols, width), bf16),
            pltpu.VMEM((cols, width), bf16),
            pltpu.VMEM((near, cols), bf16),
            pltpu.VMEM((near, cols), bf16),
            pltpu.VMEM(w_own.shape, bf16),
            pltpu.VMEM(slab.shape, bf16),
            pltpu.VMEM((8, found), jnp.float32),
            pltpu.VMEM((8, found), jnp.float32),
            pltpu.VMEM((10, 8, found), jnp.float32),
            pltpu.SemaphoreType.DMA((19,)),
            pltpu.SemaphoreType.DMA((19,)),
        ],
        compiler_params=pltpu.CompilerParams(
            collective_id=1, has_side_effects=True, vmem_limit_bytes=60 << 20
        ),
        cost_estimate=pl.CostEstimate(
            flops=flops, bytes_accessed=20 << 20, transcendentals=tokens * HEADS * 256
        ),
        name="attend",
    )(pieces, w_own, w_own, slab, asked, queries)


def routes_kernel(ids_ref, table_ref, before):
    requests = ids_ref.shape[1]
    per_device = requests // (RING_Y * RING_Z * CORES)
    y, z, c = place()
    before[...] = jnp.where(
        lax.broadcasted_iota(jnp.int32, before.shape, 0)
        < lax.broadcasted_iota(jnp.int32, before.shape, 1),
        1.0,
        0.0,
    ).astype(jnp.bfloat16)
    index = lax.broadcasted_iota(jnp.int32, (1, requests), 1)
    k = sum(jnp.where(index >= t * per_device, 1, 0) for t in range(1, requests // per_device))
    n = index - k * per_device
    to_y, to_z = k >> 4, (k >> 1) & 7
    tie_y, tie_z = ((n >> 1) + k) & 1, (n + k) & 1
    ids = ids_ref[...]
    shard, offset = ids >> 6, ids & 63
    from_y, from_z, from_c = shard >> 4, (shard >> 1) & 7, shard & 1
    loc = jnp.where(from_c == c, 0, 64) + offset
    nodes = RING_Y * RING_Z * 2
    node_rows = lax.broadcasted_iota(jnp.int32, (nodes, requests), 0)
    lanes = lax.broadcasted_iota(jnp.int32, table_ref.shape, 1)
    slots = lax.broadcasted_iota(jnp.int32, (table_ref.shape[0], requests), 0)
    table = jnp.zeros(table_ref.shape, jnp.float32)
    here = y * RING_Z + z

    def column(hits, values):
        return jnp.sum(jnp.where(hits, values.astype(jnp.float32), 0.0), axis=1, keepdims=True)

    stuck = jnp.zeros((1, requests), jnp.int32)
    first_loc = loc
    for t, trip in enumerate(TRIPS):
        base, r, loc = 128, t * COLUMNS, first_loc
        for leg, (along_y, caps) in enumerate(trip):
            ring = RING_Y if along_y else RING_Z
            position, target, tie = (from_y, to_y, tie_y) if along_y else (from_z, to_z, tie_z)
            if along_y:
                other = to_z if leg else from_z
            else:
                other = to_y if leg else from_y
            ahead = (target - position) & (ring - 1)
            back = (ahead > ring // 2) | ((ahead == ring // 2) & (tie == 1))
            left = jnp.where(back, (ring - ahead) & (ring - 1), ahead)
            step = jnp.where(back, ring - 1, 1)
            way = jnp.where(back, 1, 0)
            for width in caps:
                chip = position * RING_Z + other if along_y else other * RING_Z + position
                node = chip * 2 + way
                seat = node_rows == node
                kinds = [
                    jnp.where(seat & (left == d), 1.0, 0.0) for d in range(ring // 2, 0, -1)
                ]
                counts = lax.dot_general(
                    jnp.concatenate(kinds, axis=0).astype(jnp.bfloat16),
                    before[...],
                    (((1,), (0,)), ((), ())),
                    preferred_element_type=jnp.float32,
                )
                rank = jnp.zeros((1, requests), jnp.float32)
                ahead_of = jnp.zeros((nodes, 1), jnp.float32)
                for i, kind in enumerate(kinds):
                    mine = counts[i * nodes : (i + 1) * nodes] + ahead_of
                    rank += jnp.sum(kind * mine, axis=0, keepdims=True)
                    ahead_of += jnp.sum(kind, axis=1, keepdims=True)
                rank = rank.astype(jnp.int32)
                goes = (left > 0) & (rank < width)
                slot = jnp.where(goes & (chip == here), way * width + rank, -1)
                table = jnp.where(lanes == r, column(slots == slot, loc), table)
                loc = jnp.where(goes, base + way * width + rank, loc)
                base += 2 * width
                position = jnp.where(goes, (position + step) & (ring - 1), position)
                left = left - jnp.where(goes, 1, 0)
                r += 1
            stuck = jnp.maximum(stuck, left)
        for core in (c, 1 - c):
            first = (here * CORES + core) * per_device
            wanted = (index == first + slots) & (slots < per_device)
            table = jnp.where(lanes == r, column(wanted, loc), table)
            r += 1
    worst = jnp.max(stuck.astype(jnp.float32), axis=1, keepdims=True)
    table = jnp.where(lanes == len(TRIPS) * COLUMNS, worst, table)
    table_ref[...] = table.astype(jnp.int32)


def routes(all_ids):
    requests = all_ids.shape[1]
    return pl.pallas_call(
        routes_kernel,
        out_shape=jax.ShapeDtypeStruct((2 * max(WIDTHS[0] + WIDTHS[1]), 128), jnp.int32),
        in_specs=[pl.BlockSpec(memory_space=pltpu.VMEM)],
        out_specs=pl.BlockSpec(memory_space=pltpu.VMEM),
        scratch_shapes=[pltpu.VMEM((requests, requests), jnp.bfloat16)],
        name="routes",
    )(all_ids)


ISSUES = (
    ((3, 0), (1, 0), (0, 0), (3, 1), (1, 1), (3, 2), (0, 1), (3, 3), (2, 0), (1, 2), (0, 2), (1, 3))
    + ((2, 1), (0, 3), (1, 4), (-1, 1), (2, 2), (3, 4), (-1, 2), (0, 4), (2, 3), (3, 5), (0, 5))
    + ((2, 4), (1, 5), (2, 5))
)


def carry_kernel(table_ref, flag_ref, store_ref, swapped_ref, kv_ref, out_ref, w_ref, worst_ref, *rest):
    rounds = len(MOVES[0])
    total = len(CHUNK_TRIPS) * rounds
    held, rest = rest[:2], rest[2:]
    out_bufs = rest[:total]
    in_bufs = rest[total : 2 * total]
    last, flags, held_sems, send_sems, recv_sems, w_send_sems, w_recv_sems = rest[2 * total :]
    y, z, c = place()
    spans = store_ref.shape[0]
    steps = [((y + dy) % RING_Y, (z + dz) % RING_Z) for dy, dz in ((1, 0), (-1, 0), (0, 1), (0, -1))]
    near = [key_of(a, b, c) for a, b in steps]
    buddy = key_of(y, z, 1 - c)
    halves = {}
    for part in (1, 0):
        mine = pl.ds(pl.multiple_of((2 * c + part) * PART, PART), PART)
        halves[part] = [
            pltpu.make_async_copy(
                store_ref.at[:, mine], held[part].at[pl.ds(0, spans)], held_sems.at[2 * part]
            ),
            pltpu.make_async_copy(
                swapped_ref.at[:, pl.ds(part * PART, PART)],
                held[part].at[pl.ds(spans, spans)],
                held_sems.at[2 * part + 1],
            ),
        ]
        for copy in halves[part]:
            copy.start()
    _, depth, row = peer_groups()
    x, planes = lax.axis_index("seq"), lax.axis_size("seq")
    seq = [lax.rem(x + d, planes) for d in range(1, planes)]
    greet(depth + row + [buddy], seq)
    quarter = kv_ref.at[x // 2, pl.ds(pl.multiple_of((x % 2) * PART, PART), PART)]
    pair = y * RING_Z + z
    own = pltpu.make_async_copy(quarter, w_ref.at[x, pair], held_sems.at[4])
    own.start()
    w_flights = [
        [
            send(quarter, w_ref.at[x, pair], w_send_sems.at[i], w_recv_sems.at[i], peer)
            for i, peer in enumerate(depth)
        ]
    ]

    flag_flights = [
        send(flag_ref.at[pl.ds(0, 8)], flags.at[i], w_send_sems.at[13 + i], w_recv_sems.at[13 + i], peer, "seq")
        for i, peer in enumerate(seq)
    ]

    def pass_on(stage):
        if stage == 1:
            own.wait()
        for copy in w_flights[-1]:
            copy.wait_recv()
        if stage == 1:
            part, peers, at, axis = w_ref.at[x, pl.ds(y * RING_Z, RING_Z)], row, 7, "keys"
        else:
            part, peers, at, axis = w_ref.at[x], seq, 10, "seq"
        w_flights.append(
            [
                send(part, part, w_send_sems.at[at + i], w_recv_sems.at[at + i], peer, axis)
                for i, peer in enumerate(peers)
            ]
        )

    ready = set()
    bases = [
        np.concatenate([[2 * spans], 2 * spans + np.cumsum(2 * np.array(w))]).tolist() for w in WIDTHS
    ]

    def picked(j, r, at):
        step, part = j // 2, j % 2
        value = held[part][jnp.where(at < 2 * spans, at + step, 0)]
        for q in range(r):
            base, count = bases[CHUNK_TRIPS[j]][q], 2 * WIDTHS[CHUNK_TRIPS[j]][q]
            inside = (at >= base) & (at < base + count)
            block = in_bufs[j * rounds + q][jnp.where(inside, at - base, 0)]
            value = jnp.where(inside, block, value)
        return value

    flights = {}

    def land(j, r):
        for flight in flights[j, r]:
            flight.wait_recv()

    def issue(j, r):
        trip = CHUNK_TRIPS[j]
        if r > 0:
            land(j, r - 1)
        elif j % 2 not in ready:
            ready.add(j % 2)
            for copy in halves[j % 2]:
                copy.wait()
        width = WIDTHS[trip][r]
        buf = out_bufs[j * rounds + r]

        def fill(s, carry):
            buf[s] = picked(j, r, table_ref[s, trip * COLUMNS + r])
            return carry

        lax.fori_loop(0, 2 * width, fill, 0)
        flights[j, r] = []
        for d in range(2):
            part = pl.ds(d * width, width)
            k = (j * rounds + r) * 2 + d
            peer = near[d if MOVES[trip][r] else 2 + d]
            flights[j, r].append(
                send(buf.at[part], in_bufs[j * rounds + r].at[part], send_sems.at[k], recv_sems.at[k], peer)
            )

    def finish(j):
        land(j, rounds - 1)
        column = CHUNK_TRIPS[j] * COLUMNS + rounds

        def fill(s, carry):
            out_ref[2 * j, s] = picked(j, rounds, table_ref[s, column])
            last[j, s] = picked(j, rounds, table_ref[s, column + 1])
            return carry

        lax.fori_loop(0, REQUESTS, fill, 0)
        k = 2 * total + j
        flights[j, rounds] = [
            send(last.at[j], out_ref.at[2 * j + 1], send_sems.at[k], recv_sems.at[k], buddy)
        ]

    waiting = []
    for j, r in ISSUES:
        if j < 0:
            pass_on(r)
            continue
        issue(j, r)
        if r == rounds - 1:
            waiting.append(j)
        elif waiting:
            finish(waiting.pop(0))
    for j in waiting:
        finish(j)
    for j in range(len(CHUNK_TRIPS)):
        land(j, rounds)
    for copy in w_flights[-1]:
        copy.wait_recv()
    worst = flag_ref[0:8, :]
    for i, copy in enumerate(flag_flights):
        copy.wait_recv()
        worst = jnp.maximum(worst, flags[i])
    worst_ref[...] = worst
    for copies in list(flights.values()) + w_flights + [flag_flights]:
        for copy in copies:
            copy.wait_send()


def carry(store, swapped, kv_weight, table):
    spans, _, enc_width = store.shape
    planes = lax.axis_size("seq")
    item = (PART, enc_width)
    chunks = len(CHUNK_TRIPS)
    bufs = [pltpu.VMEM((2 * w, *item), store.dtype) for t in CHUNK_TRIPS for w in WIDTHS[t]]
    copies = 2 * len(bufs) + chunks
    return pl.pallas_call(
        carry_kernel,
        out_shape=[
            jax.ShapeDtypeStruct((2 * chunks, REQUESTS, *item), store.dtype),
            jax.ShapeDtypeStruct((planes, RING_Y * RING_Z, *item), store.dtype),
            jax.ShapeDtypeStruct((8, 128), table.dtype),
        ],
        in_specs=[pl.BlockSpec(memory_space=pltpu.SMEM), pl.BlockSpec(memory_space=pltpu.VMEM)]
        + [pl.BlockSpec(memory_space=pl.ANY)] * 3,
        out_specs=[pl.BlockSpec(memory_space=pltpu.VMEM)] * 3,
        scratch_shapes=[pltpu.VMEM((2 * spans, *item), store.dtype)] * 2
        + bufs * 2
        + [
            pltpu.VMEM((chunks, REQUESTS, *item), store.dtype),
            pltpu.VMEM((planes - 1, 8, 128), table.dtype),
            pltpu.SemaphoreType.DMA((5,)),
            pltpu.SemaphoreType.DMA((copies,)),
            pltpu.SemaphoreType.DMA((copies,)),
            pltpu.SemaphoreType.DMA((16,)),
            pltpu.SemaphoreType.DMA((16,)),
        ],
        compiler_params=pltpu.CompilerParams(
            collective_id=2, has_side_effects=True, vmem_limit_bytes=60 << 20
        ),
        cost_estimate=pl.CostEstimate(flops=0, bytes_accessed=500 << 20, transcendentals=0),
        name="carry",
    )(table, table, store, swapped, kv_weight)


def direct(neighbour_store, neighbour_ids):
    key_count = lax.axis_size("keys")
    shard_spans = neighbour_store.shape[0]
    flat_ids = neighbour_ids.reshape(-1)
    target, offset = flat_ids // shard_spans, flat_ids % shard_spans
    hit = target[:, None] == jnp.arange(key_count, dtype=jnp.int32)[None, :]
    table = jnp.sum(jnp.where(hit, offset[:, None], 0), axis=0)
    incoming = lax.all_to_all(table, "keys", split_axis=0, concat_axis=0, tiled=True)
    firsts, seconds = take(
        [neighbour_store], [[0]] * 2, jnp.stack([incoming, incoming + 1]), neighbour_store.shape[1]
    )
    arrived = [
        lax.all_to_all(spans, "keys", split_axis=0, concat_axis=0, tiled=True)
        for spans in (firsts, seconds)
    ]
    locs = jnp.stack([target, key_count + target])
    return take(arrived, [[0], [1]], locs, neighbour_store.shape[1])


def body(span_queries, key_slab, neighbour_store, neighbour_ids, attn_queries, kv_weight):
    position = lax.axis_index("keys")
    y, z, c = place()
    own_spans = neighbour_ids.shape[0]
    span_rows = neighbour_store.shape[1]
    all_ids, swapped = gather_ids(neighbour_ids, neighbour_store)
    asked = jnp.pad(span_queries, ((0, 16 - own_spans), (0, 0)))
    all_asked = lax.all_gather(asked, "keys", axis=0, tiled=True)
    all_asked = all_asked.reshape(RING_Y * RING_Z, CORES, *asked.shape)
    table = routes(all_ids)
    pieces, weight_own, worst = carry(neighbour_store, swapped, kv_weight, table)

    def resend(store, ids, fast):
        return jnp.stack(
            [
                spans[:, h * PART : (h + 1) * PART]
                for spans in direct(store, ids)
                for h in range(span_rows // PART)
            ]
        )

    pieces = lax.cond(
        worst[0, len(TRIPS) * COLUMNS] > 0, resend, lambda store, ids, fast: fast, neighbour_store, neighbour_ids, pieces
    )
    attended, best = attend(pieces, weight_own, key_slab, all_asked, attn_queries)
    column = (position // CORES) * 16
    best_scores = lax.dynamic_slice_in_dim(best, column, own_spans, axis=1)[:2].T
    return (best_scores, attended)


def solution(mesh):
    return jax.shard_map(
        body,
        mesh=mesh,
        in_specs=(
            P(("keys", "seq"), None),
            P("keys", None),
            P("keys", None, None),
            P(("keys", "seq"), None),
            P(("keys", "seq"), None),
            P(None, "keys", None),
        ),
        out_specs=(P(("keys", "seq"), None), P(("keys", "seq"), None)),
        check_vma=False,
    )
```

```python
import functools

import jax
import jax.numpy as jnp
import numpy as np
from jax import lax
from jax.experimental import pallas as pl
from jax.experimental.pallas import tpu as pltpu
from jax.sharding import PartitionSpec as P

HEADS = 16
HEAD_DIM = 128
RING_Y, RING_Z, CORES = 4, 8, 2
Y_CAPS, Z_CAPS = (24, 17), (12, 11, 10, 10)
Z_FIRST_CAPS, Y_LAST_CAPS = (19, 16, 16, 15), (14, 11)
TRIPS = (((True, Y_CAPS), (False, Z_CAPS)), ((False, Z_FIRST_CAPS), (True, Y_LAST_CAPS)))
MOVES = tuple([along for along, caps in trip for _ in caps] for trip in TRIPS)
WIDTHS = tuple([w for _, caps in trip for w in caps] for trip in TRIPS)
CHUNK_TRIPS = (0, 0, 0, 1)
COLUMNS = 8
PART = 16
REQUESTS = 12


def key_of(y, z, c):
    return (y * RING_Z + z) * CORES + c


def place():
    k = lax.axis_index("keys")
    return k // (RING_Z * CORES), (k // CORES) % RING_Z, k % CORES


def shifted(dy, dz, dc):
    pairs = []
    for y in range(RING_Y):
        for z in range(RING_Z):
            for c in range(CORES):
                to = key_of((y + dy) % RING_Y, (z + dz) % RING_Z, (c + dc) % CORES)
                pairs.append((key_of(y, z, c), to))
    return pairs


def greet(peers, seq_peers=()):
    barrier = pltpu.get_barrier_semaphore()
    for axis, peer in [("keys", p) for p in peers] + [("seq", p) for p in seq_peers]:
        pl.semaphore_signal(
            barrier, inc=1, device_id={axis: peer}, device_id_type=pl.DeviceIdType.MESH
        )
    pl.semaphore_wait(barrier, len(peers) + len(seq_peers))


def peer_groups():
    y, z, c = place()
    core = [key_of(y, z, 1 - c)]
    depth = [key_of(y, (z + d) % RING_Z, c) for d in range(1, RING_Z)]
    row = [key_of((y + d) % RING_Y, z, c) for d in range(1, RING_Y)]
    return core, depth, row


def send(src, dst, send_sem, recv_sem, peer, axis="keys"):
    copy = pltpu.make_async_remote_copy(
        src_ref=src,
        dst_ref=dst,
        send_sem=send_sem,
        recv_sem=recv_sem,
        device_id={axis: peer},
        device_id_type=pl.DeviceIdType.MESH,
    )
    copy.start()
    return copy


def gather_ids_kernel(ids_ref, store_ref, out_ref, swapped_ref, held, rows, send_sem, recv_sem):
    y, z, c = place()
    core, depth, row = peer_groups()
    greet(core + depth + row)
    held[z, c] = ids_ref[...]
    own = held.at[z, c]
    first = send(own, own, send_sem.at[0], recv_sem.at[0], core[0])
    half = swapped_ref.shape[1]
    theirs = pl.ds(pl.multiple_of((1 - c) * half, half), half)
    swap = send(store_ref.at[:, theirs], swapped_ref, send_sem.at[11], recv_sem.at[11], core[0])
    first.wait()
    copies = []
    for i, peer in enumerate(depth):
        copies.append(send(held.at[z], held.at[z], send_sem.at[1 + i], recv_sem.at[1 + i], peer))
    for copy in copies:
        copy.wait()
    rows[y] = held[:, :, 0, :].reshape(rows.shape[1:])
    copies = []
    for i, peer in enumerate(row):
        copies.append(send(rows.at[y], rows.at[y], send_sem.at[8 + i], recv_sem.at[8 + i], peer))
    for copy in copies:
        copy.wait()
    out_ref[...] = rows[...]
    swap.wait()


def gather_ids(ids, store):
    tile = jnp.pad(ids.reshape(1, -1), ((0, 7), (0, 128 - ids.size)))
    shape = (RING_Y, RING_Z * CORES, 128)
    spans, span_rows, width = store.shape
    all_ids, swapped = pl.pallas_call(
        gather_ids_kernel,
        out_shape=[
            jax.ShapeDtypeStruct(shape, jnp.int32),
            jax.ShapeDtypeStruct((spans, span_rows // 2, width), store.dtype),
        ],
        in_specs=[pl.BlockSpec(memory_space=pltpu.VMEM), pl.BlockSpec(memory_space=pl.ANY)],
        out_specs=[pl.BlockSpec(memory_space=pltpu.VMEM)] * 2,
        scratch_shapes=[
            pltpu.VMEM((RING_Z, CORES, 8, 128), jnp.int32),
            pltpu.VMEM(shape, jnp.int32),
            pltpu.SemaphoreType.DMA((12,)),
            pltpu.SemaphoreType.DMA((12,)),
        ],
        compiler_params=pltpu.CompilerParams(
            collective_id=0, has_side_effects=True, vmem_limit_bytes=60 << 20
        ),
        name="gather_ids",
    )(tile, store)
    return all_ids.reshape(-1, 128)[:, : ids.size].reshape(1, -1), swapped


def merge(a, b):
    high = jnp.maximum(a[0:1], b[0:1])
    low = jnp.maximum(jnp.minimum(a[0:1], b[0:1]), jnp.maximum(a[1:2], b[1:2]))
    return jnp.concatenate([high, low, jnp.zeros((6, high.shape[1]), high.dtype)], axis=0)


def take_kernel(counts, reach, row, locs_ref, *refs):
    sources = refs[: len(counts)]
    outs = refs[len(counts) : -1]
    sems = refs[-1]
    starts = np.concatenate([[0], np.cumsum(counts)]).tolist()
    width, rows = outs[0].shape[0], outs[0].shape[1]

    def piece(k, at):
        if sources[k].shape[1] == rows:
            return sources[k].at[at]
        return sources[k].at[at, pl.ds(pl.multiple_of(row(), rows), rows)]

    def begin(s, carry):
        for d, out in enumerate(outs):
            at = locs_ref[d, s]
            for k in reach[d]:

                @pl.when((at >= starts[k]) & (at < starts[k + 1]))
                def _():
                    pltpu.make_async_copy(
                        piece(k, at - starts[k]), out.at[s], sems.at[d, s]
                    ).start()

        return carry

    lax.fori_loop(0, width, begin, 0)

    def finish(s, carry):
        for d, out in enumerate(outs):
            pltpu.make_async_copy(piece(reach[d][0], 0), out.at[s], sems.at[d, s]).wait()
        return carry

    lax.fori_loop(0, width, finish, 0)


def take(sources, reach, locs, rows, row=None):
    counts = tuple(s.shape[0] for s in sources)
    width = locs.shape[1]
    item = (rows, sources[0].shape[2])
    nbytes = 4 * width * item[0] * item[1] * 2
    return pl.pallas_call(
        functools.partial(take_kernel, counts, reach, row),
        out_shape=[jax.ShapeDtypeStruct((width, *item), sources[0].dtype)] * 2,
        in_specs=[pl.BlockSpec(memory_space=pltpu.SMEM)]
        + [pl.BlockSpec(memory_space=pl.ANY)] * len(sources),
        out_specs=[pl.BlockSpec(memory_space=pltpu.VMEM)] * 2,
        scratch_shapes=[pltpu.SemaphoreType.DMA((2, width))],
        cost_estimate=pl.CostEstimate(flops=0, bytes_accessed=nbytes, transcendentals=0),
        compiler_params=pltpu.CompilerParams(vmem_limit_bytes=32 << 20),
        name="take_spans",
    )(locs, *sources)


def top_two(scores):
    top = jnp.max(scores, axis=0, keepdims=True)
    at_top = scores == top
    ties = jnp.sum(jnp.where(at_top, 1.0, 0.0), axis=0, keepdims=True)
    rest = jnp.max(jnp.where(at_top, -jnp.inf, scores), axis=0, keepdims=True)
    second = jnp.where(ties > 1.5, top, rest)
    return jnp.concatenate([top, second, jnp.zeros((6, top.shape[1]), top.dtype)], axis=0)


SWAP, SLAB, DEPTH, ROW = 0, 8, 9, 16


def attend_kernel(
    pieces,
    w_own,
    w_all,
    slab,
    asked,
    q_ref,
    o_ref,
    best_ref,
    x,
    wk,
    wv,
    keys,
    values,
    w_other,
    other_slab,
    found,
    after_depth,
    landed,
    send_sem,
    recv_sem,
):
    c = place()[2]
    g = pl.program_id(0)
    parts, requests, part, width = pieces.shape
    spans = requests // 2
    near = 2 * part * parts
    rows = q_ref.shape[0] // spans
    pairs = w_own.shape[1]
    steps = w_all.shape[1] // pairs
    core, depth, row = peer_groups()
    contract = (((1,), (1,)), ((), ()))
    dot = functools.partial(lax.dot_general, preferred_element_type=jnp.float32)

    def flight(src, dst, k, peer):
        return pltpu.make_async_remote_copy(
            src_ref=src,
            dst_ref=dst,
            send_sem=send_sem.at[k],
            recv_sem=recv_sem.at[k],
            device_id={"keys": peer},
            device_id_type=pl.DeviceIdType.MESH,
        )

    def weights_flight(b):
        at = pl.ds(b * pairs, pairs)
        return flight(w_all.at[:, at], w_other.at[:, at], SWAP + b, core[0])

    slab_flight = lambda: flight(slab, other_slab, SLAB, core[0])
    depth_flights = lambda: [
        flight(found, landed.at[i], DEPTH + i, peer) for i, peer in enumerate(depth)
    ]
    row_flights = lambda: [
        flight(after_depth, landed.at[len(depth) + i], ROW + i, peer) for i, peer in enumerate(row)
    ]

    @pl.when(g == 0)
    def _():
        greet(core + depth + row)
        for b in range(steps):
            weights_flight(b).start()
        slab_flight().start()
        for u in range(spans):
            for i in range(parts):
                at = (u * parts + i) * 2 * part
                x[at : at + 2 * part, :] = pieces[i, 2 * u : 2 * u + 2].reshape(2 * part, width)

    weights_flight(g).wait_recv()
    for kind, w in enumerate((wk, wv)):
        for j in range(pairs):
            for h in range(2):
                mine = pl.multiple_of(j * 64 + c * 32 + h * PART, PART)
                theirs = pl.multiple_of(j * 64 + (1 - c) * 32 + h * PART, PART)
                w[pl.ds(mine, PART), :] = w_own[kind * 2 + h, j]
                w[pl.ds(theirs, PART), :] = w_other[kind * 2 + h, g * pairs + j]
    keys[...] = dot(x[...], wk[...], contract).astype(jnp.bfloat16)
    values[...] = dot(x[...], wv[...], contract).astype(jnp.bfloat16)
    zero = jnp.zeros((rows, HEAD_DIM), jnp.bfloat16)

    def both_heads(u):
        q = q_ref[u * rows : (u + 1) * rows, :]
        return jnp.concatenate(
            [
                jnp.concatenate([q[:, :HEAD_DIM], zero], axis=1),
                jnp.concatenate([zero, q[:, HEAD_DIM:]], axis=1),
            ],
            axis=0,
        )

    def softmax(logits):
        scaled = logits * HEAD_DIM ** (-0.5)
        largest = jnp.max(scaled, axis=-1, keepdims=True)
        terms = jnp.exp(scaled - largest)
        total = jnp.sum(terms, axis=-1, keepdims=True)
        return (terms * (1.0 / total)).astype(jnp.bfloat16)

    logits = [dot(both_heads(u), keys[u * near : (u + 1) * near, :], contract) for u in range(spans)]
    weights = [softmax(part_logits) for part_logits in logits]
    outs = [
        dot(weights[u], values[u * near : (u + 1) * near, :], (((1,), (0,)), ((), ())))
        for u in range(spans)
    ]
    for u, out in enumerate(outs):
        tokens = slice(u * rows, (u + 1) * rows)
        o_ref[tokens, :HEAD_DIM] = out[:rows, :HEAD_DIM].astype(jnp.bfloat16)
        o_ref[tokens, HEAD_DIM:] = out[rows:, HEAD_DIM:].astype(jnp.bfloat16)

    @pl.when(g == 1)
    def _():
        slab_flight().wait_recv()
        queries = asked[:, c].reshape(found.shape[1], slab.shape[1])
        found[...] = merge(
            top_two(dot(slab[...], queries, contract)), top_two(dot(other_slab[...], queries, contract))
        )
        for copy in depth_flights():
            copy.start()

    @pl.when(g == 3)
    def _():
        for copy in depth_flights():
            copy.wait_recv()
        total = found[...]
        for i in range(len(depth)):
            total = merge(total, landed[i])
        after_depth[...] = total
        for copy in row_flights():
            copy.start()

    @pl.when(g == 5)
    def _():
        for copy in row_flights():
            copy.wait_recv()
        total = after_depth[...]
        for i in range(len(row)):
            total = merge(total, landed[len(depth) + i])
        best_ref[...] = total

    @pl.when(g == steps - 1)
    def _():
        for b in range(steps):
            weights_flight(b).wait_send()
        for copy in [slab_flight()] + depth_flights() + row_flights():
            copy.wait_send()


def attend(pieces, w_own, slab, asked, queries):
    parts, requests, part, width = pieces.shape
    near = requests * parts * part
    tokens, columns = queries.shape
    steps = 8
    pairs = w_own.shape[1] // steps
    cols = columns // steps
    found = asked.shape[0] * asked.shape[2]
    block = pl.BlockSpec((tokens, cols), lambda g: (0, g))
    flops = 2 * near * width * 2 * columns
    bf16 = jnp.bfloat16
    return pl.pallas_call(
        attend_kernel,
        grid=(steps,),
        out_shape=[
            jax.ShapeDtypeStruct((tokens, columns), bf16),
            jax.ShapeDtypeStruct((8, found), jnp.float32),
        ],
        in_specs=[
            pl.BlockSpec(pieces.shape, lambda g: (0, 0, 0, 0)),
            pl.BlockSpec((w_own.shape[0], pairs, part, width), lambda g: (0, g, 0, 0)),
            pl.BlockSpec(memory_space=pl.ANY),
            pl.BlockSpec(slab.shape, lambda g: (0, 0)),
            pl.BlockSpec(asked.shape, lambda g: (0, 0, 0, 0)),
            block,
        ],
        out_specs=[block, pl.BlockSpec((8, found), lambda g: (0, 0))],
        scratch_shapes=[
            pltpu.VMEM((near, width), bf16),
            pltpu.VMEM((cols, width), bf16),
            pltpu.VMEM((cols, width), bf16),
            pltpu.VMEM((near, cols), bf16),
            pltpu.VMEM((near, cols), bf16),
            pltpu.VMEM(w_own.shape, bf16),
            pltpu.VMEM(slab.shape, bf16),
            pltpu.VMEM((8, found), jnp.float32),
            pltpu.VMEM((8, found), jnp.float32),
            pltpu.VMEM((10, 8, found), jnp.float32),
            pltpu.SemaphoreType.DMA((19,)),
            pltpu.SemaphoreType.DMA((19,)),
        ],
        compiler_params=pltpu.CompilerParams(
            collective_id=1, has_side_effects=True, vmem_limit_bytes=48 << 20
        ),
        cost_estimate=pl.CostEstimate(
            flops=flops, bytes_accessed=20 << 20, transcendentals=tokens * HEADS * 256
        ),
        name="attend",
    )(pieces, w_own, w_own, slab, asked, queries)


def routes_kernel(ids_ref, table_ref, before):
    requests = ids_ref.shape[1]
    per_device = requests // (RING_Y * RING_Z * CORES)
    y, z, c = place()
    before[...] = jnp.where(
        lax.broadcasted_iota(jnp.int32, before.shape, 0)
        < lax.broadcasted_iota(jnp.int32, before.shape, 1),
        1.0,
        0.0,
    ).astype(jnp.bfloat16)
    index = lax.broadcasted_iota(jnp.int32, (1, requests), 1)
    k = sum(jnp.where(index >= t * per_device, 1, 0) for t in range(1, requests // per_device))
    n = index - k * per_device
    to_y, to_z = k >> 4, (k >> 1) & 7
    tie_y, tie_z = ((n >> 1) + k) & 1, (n + k) & 1
    ids = ids_ref[...]
    shard, offset = ids >> 6, ids & 63
    from_y, from_z, from_c = shard >> 4, (shard >> 1) & 7, shard & 1
    loc = jnp.where(from_c == c, 0, 64) + offset
    nodes = RING_Y * RING_Z * 2
    node_rows = lax.broadcasted_iota(jnp.int32, (nodes, requests), 0)
    lanes = lax.broadcasted_iota(jnp.int32, table_ref.shape, 1)
    slots = lax.broadcasted_iota(jnp.int32, (table_ref.shape[0], requests), 0)
    table = jnp.zeros(table_ref.shape, jnp.float32)
    here = y * RING_Z + z

    def column(hits, values):
        return jnp.sum(jnp.where(hits, values.astype(jnp.float32), 0.0), axis=1, keepdims=True)

    stuck = jnp.zeros((1, requests), jnp.int32)
    first_loc = loc
    for t, trip in enumerate(TRIPS):
        base, r, loc = 128, t * COLUMNS, first_loc
        for leg, (along_y, caps) in enumerate(trip):
            ring = RING_Y if along_y else RING_Z
            position, target, tie = (from_y, to_y, tie_y) if along_y else (from_z, to_z, tie_z)
            if along_y:
                other = to_z if leg else from_z
            else:
                other = to_y if leg else from_y
            ahead = (target - position) & (ring - 1)
            back = (ahead > ring // 2) | ((ahead == ring // 2) & (tie == 1))
            left = jnp.where(back, (ring - ahead) & (ring - 1), ahead)
            step = jnp.where(back, ring - 1, 1)
            way = jnp.where(back, 1, 0)
            for width in caps:
                chip = position * RING_Z + other if along_y else other * RING_Z + position
                node = chip * 2 + way
                seat = node_rows == node
                kinds = [
                    jnp.where(seat & (left == d), 1.0, 0.0) for d in range(ring // 2, 0, -1)
                ]
                counts = lax.dot_general(
                    jnp.concatenate(kinds, axis=0).astype(jnp.bfloat16),
                    before[...],
                    (((1,), (0,)), ((), ())),
                    preferred_element_type=jnp.float32,
                )
                rank = jnp.zeros((1, requests), jnp.float32)
                ahead_of = jnp.zeros((nodes, 1), jnp.float32)
                for i, kind in enumerate(kinds):
                    mine = counts[i * nodes : (i + 1) * nodes] + ahead_of
                    rank += jnp.sum(kind * mine, axis=0, keepdims=True)
                    ahead_of += jnp.sum(kind, axis=1, keepdims=True)
                rank = rank.astype(jnp.int32)
                goes = (left > 0) & (rank < width)
                slot = jnp.where(goes & (chip == here), way * width + rank, -1)
                table = jnp.where(lanes == r, column(slots == slot, loc), table)
                loc = jnp.where(goes, base + way * width + rank, loc)
                base += 2 * width
                position = jnp.where(goes, (position + step) & (ring - 1), position)
                left = left - jnp.where(goes, 1, 0)
                r += 1
            stuck = jnp.maximum(stuck, left)
        for core in (c, 1 - c):
            first = (here * CORES + core) * per_device
            wanted = (index == first + slots) & (slots < per_device)
            table = jnp.where(lanes == r, column(wanted, loc), table)
            r += 1
    worst = jnp.max(stuck.astype(jnp.float32), axis=1, keepdims=True)
    table = jnp.where(lanes == len(TRIPS) * COLUMNS, worst, table)
    table_ref[...] = table.astype(jnp.int32)


def routes(all_ids):
    requests = all_ids.shape[1]
    return pl.pallas_call(
        routes_kernel,
        out_shape=jax.ShapeDtypeStruct((2 * max(WIDTHS[0] + WIDTHS[1]), 128), jnp.int32),
        in_specs=[pl.BlockSpec(memory_space=pltpu.VMEM)],
        out_specs=pl.BlockSpec(memory_space=pltpu.VMEM),
        scratch_shapes=[pltpu.VMEM((requests, requests), jnp.bfloat16)],
        name="routes",
    )(all_ids)


ISSUES = (
    ((3, 0), (1, 0), (0, 0), (3, 1), (1, 1), (3, 2), (0, 1), (3, 3), (2, 0), (1, 2), (0, 2), (1, 3))
    + ((2, 1), (0, 3), (1, 4), (-1, 1), (2, 2), (3, 4), (-1, 2), (0, 4), (2, 3), (3, 5), (0, 5))
    + ((2, 4), (1, 5), (2, 5))
)


def carry_kernel(table_ref, flag_ref, store_ref, swapped_ref, kv_ref, out_ref, w_ref, worst_ref, *rest):
    rounds = len(MOVES[0])
    total = len(CHUNK_TRIPS) * rounds
    held, rest = rest[:2], rest[2:]
    out_bufs = rest[:total]
    in_bufs = rest[total : 2 * total]
    last, flags, held_sems, send_sems, recv_sems, w_send_sems, w_recv_sems = rest[2 * total :]
    y, z, c = place()
    spans = store_ref.shape[0]
    steps = [((y + dy) % RING_Y, (z + dz) % RING_Z) for dy, dz in ((1, 0), (-1, 0), (0, 1), (0, -1))]
    near = [key_of(a, b, c) for a, b in steps]
    buddy = key_of(y, z, 1 - c)
    halves = {}
    for part in (1, 0):
        mine = pl.ds(pl.multiple_of((2 * c + part) * PART, PART), PART)
        halves[part] = [
            pltpu.make_async_copy(
                store_ref.at[:, mine], held[part].at[pl.ds(0, spans)], held_sems.at[2 * part]
            ),
            pltpu.make_async_copy(
                swapped_ref.at[:, pl.ds(part * PART, PART)],
                held[part].at[pl.ds(spans, spans)],
                held_sems.at[2 * part + 1],
            ),
        ]
        for copy in halves[part]:
            copy.start()
    _, depth, row = peer_groups()
    x, planes = lax.axis_index("seq"), lax.axis_size("seq")
    seq = [lax.rem(x + d, planes) for d in range(1, planes)]
    greet(depth + row + [buddy], seq)
    quarter = kv_ref.at[x // 2, pl.ds(pl.multiple_of((x % 2) * PART, PART), PART)]
    pair = y * RING_Z + z
    own = pltpu.make_async_copy(quarter, w_ref.at[x, pair], held_sems.at[4])
    own.start()
    w_flights = [
        [
            send(quarter, w_ref.at[x, pair], w_send_sems.at[i], w_recv_sems.at[i], peer)
            for i, peer in enumerate(depth)
        ]
    ]

    flag_flights = [
        send(flag_ref.at[pl.ds(0, 8)], flags.at[i], w_send_sems.at[13 + i], w_recv_sems.at[13 + i], peer, "seq")
        for i, peer in enumerate(seq)
    ]

    def pass_on(stage):
        if stage == 1:
            own.wait()
        for copy in w_flights[-1]:
            copy.wait_recv()
        if stage == 1:
            part, peers, at, axis = w_ref.at[x, pl.ds(y * RING_Z, RING_Z)], row, 7, "keys"
        else:
            part, peers, at, axis = w_ref.at[x], seq, 10, "seq"
        w_flights.append(
            [
                send(part, part, w_send_sems.at[at + i], w_recv_sems.at[at + i], peer, axis)
                for i, peer in enumerate(peers)
            ]
        )

    ready = set()
    bases = [
        np.concatenate([[2 * spans], 2 * spans + np.cumsum(2 * np.array(w))]).tolist() for w in WIDTHS
    ]

    def picked(j, r, at):
        step, part = j // 2, j % 2
        value = held[part][jnp.where(at < 2 * spans, at + step, 0)]
        for q in range(r):
            base, count = bases[CHUNK_TRIPS[j]][q], 2 * WIDTHS[CHUNK_TRIPS[j]][q]
            inside = (at >= base) & (at < base + count)
            block = in_bufs[j * rounds + q][jnp.where(inside, at - base, 0)]
            value = jnp.where(inside, block, value)
        return value

    flights = {}

    def land(j, r):
        for flight in flights[j, r]:
            flight.wait_recv()

    def issue(j, r):
        trip = CHUNK_TRIPS[j]
        if r > 0:
            land(j, r - 1)
        elif j % 2 not in ready:
            ready.add(j % 2)
            for copy in halves[j % 2]:
                copy.wait()
        width = WIDTHS[trip][r]
        buf = out_bufs[j * rounds + r]

        def fill(s, carry):
            buf[s] = picked(j, r, table_ref[s, trip * COLUMNS + r])
            return carry

        lax.fori_loop(0, 2 * width, fill, 0)
        flights[j, r] = []
        for d in range(2):
            part = pl.ds(d * width, width)
            k = (j * rounds + r) * 2 + d
            peer = near[d if MOVES[trip][r] else 2 + d]
            flights[j, r].append(
                send(buf.at[part], in_bufs[j * rounds + r].at[part], send_sems.at[k], recv_sems.at[k], peer)
            )

    def finish(j):
        land(j, rounds - 1)
        column = CHUNK_TRIPS[j] * COLUMNS + rounds

        def fill(s, carry):
            out_ref[2 * j, s] = picked(j, rounds, table_ref[s, column])
            last[j, s] = picked(j, rounds, table_ref[s, column + 1])
            return carry

        lax.fori_loop(0, REQUESTS, fill, 0)
        k = 2 * total + j
        flights[j, rounds] = [
            send(last.at[j], out_ref.at[2 * j + 1], send_sems.at[k], recv_sems.at[k], buddy)
        ]

    waiting = []
    for j, r in ISSUES:
        if j < 0:
            pass_on(r)
            continue
        issue(j, r)
        if r == rounds - 1:
            waiting.append(j)
        elif waiting:
            finish(waiting.pop(0))
    for j in waiting:
        finish(j)
    for j in range(len(CHUNK_TRIPS)):
        land(j, rounds)
    for copy in w_flights[-1]:
        copy.wait_recv()
    worst = flag_ref[0:8, :]
    for i, copy in enumerate(flag_flights):
        copy.wait_recv()
        worst = jnp.maximum(worst, flags[i])
    worst_ref[...] = worst
    for copies in list(flights.values()) + w_flights + [flag_flights]:
        for copy in copies:
            copy.wait_send()


def carry(store, swapped, kv_weight, table):
    spans, _, enc_width = store.shape
    planes = lax.axis_size("seq")
    item = (PART, enc_width)
    chunks = len(CHUNK_TRIPS)
    bufs = [pltpu.VMEM((2 * w, *item), store.dtype) for t in CHUNK_TRIPS for w in WIDTHS[t]]
    copies = 2 * len(bufs) + chunks
    return pl.pallas_call(
        carry_kernel,
        out_shape=[
            jax.ShapeDtypeStruct((2 * chunks, REQUESTS, *item), store.dtype),
            jax.ShapeDtypeStruct((planes, RING_Y * RING_Z, *item), store.dtype),
            jax.ShapeDtypeStruct((8, 128), table.dtype),
        ],
        in_specs=[pl.BlockSpec(memory_space=pltpu.SMEM), pl.BlockSpec(memory_space=pltpu.VMEM)]
        + [pl.BlockSpec(memory_space=pl.ANY)] * 3,
        out_specs=[pl.BlockSpec(memory_space=pltpu.VMEM)] * 3,
        scratch_shapes=[pltpu.VMEM((2 * spans, *item), store.dtype)] * 2
        + bufs * 2
        + [
            pltpu.VMEM((chunks, REQUESTS, *item), store.dtype),
            pltpu.VMEM((planes - 1, 8, 128), table.dtype),
            pltpu.SemaphoreType.DMA((5,)),
            pltpu.SemaphoreType.DMA((copies,)),
            pltpu.SemaphoreType.DMA((copies,)),
            pltpu.SemaphoreType.DMA((16,)),
            pltpu.SemaphoreType.DMA((16,)),
        ],
        compiler_params=pltpu.CompilerParams(
            collective_id=2, has_side_effects=True, vmem_limit_bytes=60 << 20
        ),
        cost_estimate=pl.CostEstimate(flops=0, bytes_accessed=500 << 20, transcendentals=0),
        name="carry",
    )(table, table, store, swapped, kv_weight)


def direct(neighbour_store, neighbour_ids):
    key_count = lax.axis_size("keys")
    shard_spans = neighbour_store.shape[0]
    flat_ids = neighbour_ids.reshape(-1)
    target, offset = flat_ids // shard_spans, flat_ids % shard_spans
    hit = target[:, None] == jnp.arange(key_count, dtype=jnp.int32)[None, :]
    table = jnp.sum(jnp.where(hit, offset[:, None], 0), axis=0)
    incoming = lax.all_to_all(table, "keys", split_axis=0, concat_axis=0, tiled=True)
    firsts, seconds = take(
        [neighbour_store], [[0]] * 2, jnp.stack([incoming, incoming + 1]), neighbour_store.shape[1]
    )
    arrived = [
        lax.all_to_all(spans, "keys", split_axis=0, concat_axis=0, tiled=True)
        for spans in (firsts, seconds)
    ]
    locs = jnp.stack([target, key_count + target])
    return take(arrived, [[0], [1]], locs, neighbour_store.shape[1])


def body(span_queries, key_slab, neighbour_store, neighbour_ids, attn_queries, kv_weight):
    position = lax.axis_index("keys")
    y, z, c = place()
    own_spans = neighbour_ids.shape[0]
    span_rows = neighbour_store.shape[1]
    all_ids, swapped = gather_ids(neighbour_ids, neighbour_store)
    asked = jnp.pad(span_queries, ((0, 16 - own_spans), (0, 0)))
    all_asked = lax.all_gather(asked, "keys", axis=0, tiled=True)
    all_asked = all_asked.reshape(RING_Y * RING_Z, CORES, *asked.shape)
    table = routes(all_ids)
    pieces, weight_own, worst = carry(neighbour_store, swapped, kv_weight, table)

    def resend(store, ids, fast):
        return jnp.stack(
            [
                spans[:, h * PART : (h + 1) * PART]
                for spans in direct(store, ids)
                for h in range(span_rows // PART)
            ]
        )

    pieces = lax.cond(
        worst[0, len(TRIPS) * COLUMNS] > 0, resend, lambda store, ids, fast: fast, neighbour_store, neighbour_ids, pieces
    )
    attended, best = attend(pieces, weight_own, key_slab, all_asked, attn_queries)
    column = (position // CORES) * 16
    best_scores = lax.dynamic_slice_in_dim(best, column, own_spans, axis=1)[:2].T
    return (best_scores, attended)


def solution(mesh):
    return jax.shard_map(
        body,
        mesh=mesh,
        in_specs=(
            P(("keys", "seq"), None),
            P("keys", None),
            P("keys", None, None),
            P(("keys", "seq"), None),
            P(("keys", "seq"), None),
            P(None, "keys", None),
        ),
        out_specs=(P(("keys", "seq"), None), P(("keys", "seq"), None)),
        check_vma=False,
    )
```
